512 devices in a mesh: dp: 64 (over y, z_lo, core), proto: 8 (over z_hi, x).
Axes of the slice: x: 4, y: 8, z: 8 (z_hi: 2, z_lo: 4; z = z_hi * 4 + z_lo), core: 2. Of those that a mesh axis runs over, the one named last changes fastest.
Arguments:
- tokens: bfloat16 [4096, 32, 128], P('dp'), may hold values from -7 to 7
- offsets: int32 [2, 4096], P(None, 'dp'), may hold values from 0 to 8
- species: int32 [4096], P('dp'), may hold values from 0 to 15
- prototypes: bfloat16 [65536, 128], P('proto'), may hold values from -2 to 2
Outputs:
- view_grads: float32 [2, 4096, 128], P(None, 'dp')
- proto_grads: float32 [65536, 128], P(('proto', 'dp'))
- loss: float32 [], replicated
The draws below stay inside these ranges and needn't reach their ends.
Inputs may be any that keep to these rules, and one draw needn't show every extreme that they name: `offsets`: the start of a view's pooled positions within its window.
All inputs are finite; a program needn't handle non-finite values.
Results may differ from the reference program's by a relative error of at most 0.011.
The reference program's roundings to bfloat16 on the way count: a program that leaves them out, or rounds other values in their place, can miss the bound.
Values sent between devices are 32-bit elements; how exact they have to be, the bound alone decides.
A program may use at most 64 MiB of HBM per device.

```python
import math
import jax
import jax.numpy as jnp
import numpy as np
from jax import lax

PROTOS = 65536
FEAT = 128
NGROUP = 16
SEQ = 32
CROP = 24
ITERS = 3
W_DEV = 64
WINDOWS = 4096
N_DP = 64


cluster_total = 32


def cluster_centers(key, width):
    return jax.random.truncated_normal(key, -4.0, 4.0, (cluster_total, width), jnp.float32)


def draw_tokens(key, part):
    centers = cluster_centers(key, FEAT)
    key = jax.random.fold_in(key, 11)
    first_key, second_key, noise_key = jax.random.split(key, 3)
    pick_one = jax.random.randint(first_key, (WINDOWS,), 0, cluster_total)
    pick_two = jax.random.randint(second_key, (WINDOWS,), 0, cluster_total)
    chosen = jnp.minimum(pick_one, pick_two)
    noise_part = jax.random.truncated_normal(noise_key, -4.0, 4.0, (WINDOWS, SEQ, FEAT), jnp.float32)
    strength = 1.15 / math.sqrt(CROP)
    center_rows = jnp.take(centers, chosen, axis=0)
    return (strength * center_rows[:, None, :] + noise_part).astype(jnp.bfloat16)


def draw_prototypes(key, part):
    centers = cluster_centers(key, FEAT)
    key = jax.random.fold_in(key, 23)
    label_key, noise_key = jax.random.split(key)
    labels = jax.random.randint(label_key, (PROTOS,), 0, cluster_total)
    noise_part = jax.random.truncated_normal(noise_key, -4.0, 4.0, (PROTOS, FEAT), jnp.float32)
    spread = 0.88
    center_rows = jnp.take(centers, labels, axis=0)
    return ((center_rows + spread * noise_part) / math.sqrt(FEAT)).astype(jnp.bfloat16)


def with_ends(array, stream_key, low, largest):
    dims = array.shape
    place = [jax.random.randint(jax.random.fold_in(stream_key, axis), (), 0, dims[axis]) for axis in range(len(dims))]
    array = array.at[tuple(place)].set(low)
    longest = dims.index(max(dims))
    place[longest] = (place[longest] + 1) % dims[longest]
    return array.at[tuple(place)].set(largest)


def rank_table(amount, lean):
    loads = [(1 << 20) // math.isqrt(standing ** lean) + 1 for standing in range(1, amount + 1)]
    deviation = 1 + sum(loads) // (1 << 30)
    return np.cumsum(np.array([max(1, weight // deviation) for weight in loads]))


def skewed_ids(own_key, extent, count, skew):
    grid = rank_table(count, skew)
    lot = jax.random.randint(jax.random.fold_in(own_key, 1), extent, 0, int(grid[count - 1]))
    grade = jnp.searchsorted(jnp.asarray(grid, jnp.int32), lot, side="right")
    return jax.random.permutation(jax.random.fold_in(own_key, 2), count)[grade].astype(jnp.int32)


def setup_inputs(seed: int = 0) -> dict:
    keys = jax.random.split(jax.random.key(seed), 5)
    tokens = draw_tokens(jax.random.fold_in(keys[4], 71), 0)
    offsets = with_ends(jax.random.randint(keys[1], (2, WINDOWS), 0, SEQ - CROP + 1), jax.random.fold_in(keys[1], 1), 0, SEQ - CROP).astype(jnp.int32)
    species = with_ends(skewed_ids(keys[2], (WINDOWS,), NGROUP, 2), jax.random.fold_in(keys[2], 3), 0, NGROUP - 1).astype(jnp.int32)
    prototypes = draw_prototypes(jax.random.fold_in(keys[4], 71), 0)
    return {"tokens": tokens, "offsets": offsets, "species": species, "prototypes": prototypes}


peaking_denominator = 0.1
entropic = 0.05

def unit_rows(matrix):
    return matrix * lax.rsqrt(lax.optimization_barrier(jnp.mean(matrix * matrix, axis=-1, keepdims=True)) + 1e-06) / math.sqrt(matrix.shape[-1])

def reference(tokens, offsets, species, prototypes):
    windows = tokens.shape[0]
    position = jnp.arange(SEQ, dtype=jnp.int32)
    starts = offsets[:, :, None]
    window_mask = ((position >= starts) & (position < starts + CROP)).astype(jnp.float32)
    pooled = jnp.einsum('vwt,wtf->vwf', window_mask, tokens.astype(jnp.float32)) / CROP
    unit_views, back_views = jax.vjp(unit_rows, pooled)
    queries = unit_views.astype(jnp.bfloat16)
    unit_protos, back_protos = jax.vjp(unit_rows, prototypes.astype(jnp.float32))
    unit_keys = unit_protos.astype(jnp.bfloat16)
    keys_wide = lax.optimization_barrier(unit_keys).astype(jnp.float32)
    onehot = (species[:, None] == jnp.arange(NGROUP, dtype=jnp.int32)).astype(jnp.float32)
    counts = lax.optimization_barrier(jnp.sum(onehot, axis=0))
    prototype_weight = windows / (NGROUP * lax.optimization_barrier(jnp.sum(onehot * counts[None, :], axis=1)))
    row_blocks = queries.reshape(2, N_DP, W_DEV, FEAT).transpose(1, 0, 2, 3)
    weight_blocks = prototype_weight.reshape(N_DP, W_DEV)

    def kernel(row_block):
        cosine_match_matrix = jnp.einsum('vwf,kf->vwk', row_block.astype(jnp.float32), keys_wide)
        rounded = lax.optimization_barrier(jnp.exp(cosine_match_matrix / entropic).astype(jnp.bfloat16))
        return (cosine_match_matrix, rounded.astype(jnp.float32))
    empty = jnp.zeros((2, PROTOS), jnp.float32)
    proto_scale = jnp.full((2, PROTOS), 1.0 / PROTOS, jnp.float32)
    for sweep_index in range(ITERS):

        def later_sweep(running, row_block, proto_scale=proto_scale):
            cosine_match_matrix, kernel_vals = kernel(row_block)
            window_scale = 1.0 / lax.optimization_barrier(jnp.sum(kernel_vals * proto_scale[:, None, :], axis=2))
            return (running + lax.optimization_barrier(jnp.sum(kernel_vals * window_scale[:, :, None], axis=1)), None)
        columns, _ = lax.scan(later_sweep, empty, row_blocks)
        proto_scale = 1.0 / (PROTOS * columns)

    def last_sweep(running, inputs_pair):
        row_block, anchor_table_portion = inputs_pair
        cosine_match_matrix, kernel_vals = kernel(row_block)
        window_scale = 1.0 / lax.optimization_barrier(jnp.sum(kernel_vals * proto_scale[:, None, :], axis=2))
        assigned = kernel_vals * proto_scale[:, None, :] * window_scale[:, :, None]
        unscaled_anchor_closeness = cosine_match_matrix / peaking_denominator
        logarithmic_normalizer = jnp.log(lax.optimization_barrier(jnp.sum(jnp.exp(unscaled_anchor_closeness), axis=2)))
        guessed_label_share = jnp.exp(unscaled_anchor_closeness - logarithmic_normalizer[:, :, None])
        crossed_label_aim = assigned[::-1]
        crossed = lax.optimization_barrier(jnp.sum(crossed_label_aim * unscaled_anchor_closeness, axis=2))
        partial_loss = jnp.sum(anchor_table_portion * lax.optimization_barrier(jnp.sum(logarithmic_normalizer - crossed, axis=0))) / 2.0
        kinship_slope = (anchor_table_portion[None, :, None] / (2.0 * peaking_denominator) * (guessed_label_share - crossed_label_aim)).astype(jnp.bfloat16)
        kinship_slope = lax.optimization_barrier(kinship_slope).astype(jnp.float32)
        query_grad = jnp.einsum('vwk,kf->vwf', kinship_slope, keys_wide)
        key_grad = running[1] + jnp.einsum('vwk,vwf->kf', kinship_slope, row_block.astype(jnp.float32))
        return ((running[0] + partial_loss, key_grad), query_grad)
    start = (jnp.zeros((), jnp.float32), jnp.zeros((PROTOS, FEAT), jnp.float32))
    (summed, key_grad), query_blocks = lax.scan(last_sweep, start, (row_blocks, weight_blocks))
    query_grad = query_blocks.transpose(1, 0, 2, 3).reshape(2, windows, FEAT)
    view_grads = back_views(query_grad)[0]
    proto_grads = back_protos(key_grad)[0]
    return (view_grads, proto_grads, summed / windows)
```

```python
import math

import jax
import jax.numpy as jnp
from jax import lax
from jax.experimental import pallas as pl
from jax.experimental.pallas import tpu as pltpu
from jax.sharding import PartitionSpec as P

MESH = pl.DeviceIdType.MESH
F32 = jnp.float32
BF16 = jnp.bfloat16
NGROUP = 16
CROP = 24
SEQ = 32
FEAT = 128
WINDOWS = 4096
PROTOS = 65536
EPS = 1e-6
NY, NZL, NC, NZH, NX = 8, 4, 2, 2, 4
NZ = NZH * NZL
RING8 = (4, 3, 5, 2, 6, 1, 7)
XC = ((2, 0), (2, 1), (1, 0), (3, 0), (1, 1), (3, 1), (0, 1))
RING4 = (2, 1, 3)
NT = (((1,), (1,)), ((), ()))
NN = (((1,), (0,)), ((), ()))


def mm(a, b, dims=NN):
    return lax.dot_general(a, b, dims, preferred_element_type=F32)


def split3(row, count=16):
    hi = row.astype(BF16).astype(F32)
    rest = row - hi
    mid = rest.astype(BF16).astype(F32)
    lo = rest - mid
    width = row.shape[1]
    at = lax.broadcasted_iota(jnp.int32, (count, width), 0)
    full = lambda r: jnp.broadcast_to(r, (count, width))
    out = jnp.where(at == 0, full(hi), jnp.where(at == 1, full(mid), jnp.where(at == 2, full(lo), 0.0)))
    return out.astype(BF16)


def unit_scale(rows):
    return lax.rsqrt(jnp.mean(rows * rows, axis=-1, keepdims=True) + EPS)


def unit_back(rows, grad):
    scale = unit_scale(rows)
    along = jnp.mean(rows * grad, axis=-1, keepdims=True)
    return (grad - rows * (along * scale * scale)) * (scale / math.sqrt(FEAT))


def kernel(
    tok_ref, off_ref, spec_ref, proto_ref,
    view_ref, pgrad_ref, loss_ref,
    tok, kraw, keys, keys_t, pooled, qg, q16, s_buf, e_buf, k_buf, t_buf, g_buf,
    a_src, a_xc, a_z, b_src, b_y, z_src, z_xc, z_z, cnt_src, cnt_y,
    kg_src, kg_y, c_src, c_rcv, x_src, x_rcv, w_src, w_rcv, fin, l_xc, l_z, l_y,
    x_rows, qt,
    load_sem, g_ssem, g_rsem, gs_ssem, gs_rsem,
    a_ssem, a_rsem, b_ssem, b_rsem, z_ssem, z_rsem, cnt_ssem, cnt_rsem,
    kg_ssem, kg_rsem, f_ssem, f_rsem, l_ssem, l_rsem,
):
    dp = lax.axis_index("dp")
    pr = lax.axis_index("proto")
    y, zl, c = lax.div(dp, 8), lax.rem(lax.div(dp, 2), 4), lax.rem(dp, 2)
    zh, x = lax.div(pr, 4), lax.rem(pr, 4)
    z = zh * NZL + zl

    def dev(y=y, z=z, c=c, x=x):
        return ((y * NZL + lax.rem(z, NZL)) * NC + c, lax.div(z, NZL) * NX + x)

    xc_ids = [dev(x=lax.rem(x + dx, NX), c=lax.rem(c + dc, NC)) for dx, dc in XC]
    z_of = [lax.rem(z + j, NZ) for j in RING8]
    z_ids = [dev(z=k) for k in z_of]
    y_of = [lax.rem(y + j, NY) for j in RING8]
    y_ids = [dev(y=k) for k in y_of]
    x_of = [lax.rem(x + j, NX) for j in RING4]
    x_ids = [dev(x=k) for k in x_of]
    sib = dev(c=1 - c)

    def remote(src, dst, ssem, rsem, to):
        return pltpu.make_async_remote_copy(
            src_ref=src, dst_ref=dst, send_sem=ssem, recv_sem=rsem, device_id=to, device_id_type=MESH
        )

    def got(ref, sem):
        remote(ref, ref, sem, sem, sib).wait_recv()

    def sent(ref, sem):
        remote(ref, ref, sem, sem, sib).wait_send()

    barrier = pltpu.get_barrier_semaphore()
    load_tok = pltpu.make_async_copy(tok_ref, tok, load_sem.at[0])
    load_key = pltpu.make_async_copy(proto_ref.at[:, zl * NC + c], kraw, load_sem.at[1])
    load_tok.start()
    load_key.start()
    for to in xc_ids + z_ids + y_ids:
        pl.semaphore_signal(barrier, inc=1, device_id=to, device_id_type=MESH)

    off = off_ref[...].astype(F32)
    off_row = jnp.concatenate([off[0:1], off[1:2]], axis=1)
    lane = lax.broadcasted_iota(jnp.int32, (128, 128), 1)
    first = jnp.broadcast_to(off_row, (128, 128)).T.astype(jnp.int32)
    row = lax.broadcasted_iota(jnp.int32, (128, 128), 0)
    first = first + (row & 63) * SEQ
    load_tok.wait()
    total = jnp.zeros((128, FEAT), F32)
    for part in range(4):
        mask = jnp.concatenate(
            [
                jnp.where((lane + col >= first) & (lane + col < first + CROP), 1.0, 0.0).astype(BF16)
                for col in range(part * 512, part * 512 + 512, 128)
            ],
            axis=1,
        )
        total = total + mm(mask, tok[pl.ds(part * 512, 512)])
    rows = total / CROP
    pooled[...] = rows
    query = (rows * unit_scale(rows) / math.sqrt(FEAT)).astype(BF16).astype(F32)
    qg[c, zl, pl.ds(0, 128)] = query
    spec = spec_ref[...].astype(F32)
    both = jnp.concatenate([spec, spec], axis=1)
    half = lax.broadcasted_iota(jnp.int32, (8, 128), 1) // 64
    qg[c, zl, pl.ds(128, 8)] = jnp.where(half == c, jnp.broadcast_to(both, (8, 128)), 0.0)

    pl.semaphore_wait(barrier, 21)
    step2 = 2 + 4 * c
    mine = qg.at[c, zl]
    for i, to in enumerate((dev(z=lax.rem(z + step2, NZ)), dev(z=lax.rem(z + 1, NZ)), dev(z=lax.rem(z + 7, NZ)))):
        remote(mine, mine, g_ssem, g_rsem.at[i], to).start()
    remote(mine, mine, gs_ssem, gs_rsem.at[0], sib).start()

    load_key.wait()
    for i in range(8):
        raw = kraw[i].astype(F32)
        unit = raw * unit_scale(raw) / math.sqrt(FEAT)
        keys[pl.ds(i * 128, 128)] = unit.astype(BF16)
        keys_t[:, pl.ds(i * 128, 128)] = unit.astype(BF16).astype(F32).T.astype(BF16)

    def scores(zp):
        zp128 = pl.multiple_of(zp * 128, 128)
        pair = []
        for v in range(2):
            q = jnp.concatenate([qg[0, zp, pl.ds(v * 64, 64)], qg[1, zp, pl.ds(v * 64, 64)]], axis=0).astype(BF16)
            q16[v, pl.ds(zp128, 128)] = q
            pair.append(q)
        rhs = jnp.concatenate(pair, axis=0)

        def block(kb, sums):
            k0 = pl.multiple_of(kb * 128, 128)
            s = mm(keys[pl.ds(k0, 128)], rhs, NT)
            e = jnp.exp(s * 10.0)
            k = (e * e).astype(BF16)
            for v in range(2):
                at = (v, pl.ds(k0, 128), pl.ds(zp128, 128))
                s_buf[at] = s[:, v * 128 : v * 128 + 128]
                e_buf[at] = e[:, v * 128 : v * 128 + 128]
                k_buf[at] = k[:, v * 128 : v * 128 + 128]
            fold = lambda a: jnp.sum(a.reshape(16, 8, 256), axis=0)
            return sums[0] + fold(e), sums[1] + fold(k.astype(F32))

        zero = jnp.zeros((8, 256), F32)
        es, ks = lax.fori_loop(0, 8, block, (zero, zero))
        es = jnp.sum(es, axis=0, keepdims=True)
        ks = jnp.sum(ks, axis=0, keepdims=True)
        for v in range(2):
            z_src[0, :, pl.ds(v * 512 + zp128, 128)] = es[:, v * 128 : v * 128 + 128]
            a_src[0, 0, :, pl.ds(v * 512 + zp128, 128)] = ks[:, v * 128 : v * 128 + 128] * (1.0 / PROTOS)

    got(qg.at[1 - c, zl], gs_rsem.at[0])
    scores(zl)
    for i, step in ((1, 3), (2, 1), (0, 2)):
        zp = lax.rem(zl + step, NZL)
        piece = qg.at[c, zp]
        got(piece, g_rsem.at[i])
        remote(piece, piece, gs_ssem, gs_rsem.at[i + 1], sib).start()
        got(qg.at[1 - c, zp], gs_rsem.at[i + 1])
        scores(zp)

    spec_row = jnp.concatenate([qg[0, i, pl.ds(128, 1)] + qg[1, i, pl.ds(128, 1)] for i in range(4)], axis=1)
    group = lax.broadcasted_iota(jnp.int32, (NGROUP, 512), 0)
    onehot = jnp.where(group == jnp.broadcast_to(spec_row, (NGROUP, 512)).astype(jnp.int32), 1.0, 0.0)

    def a_sum(it, between_1=None, between_2=None):
        for i, to in enumerate(xc_ids):
            remote(a_src.at[it, 0], a_xc.at[it, i], a_ssem.at[it, 0], a_rsem.at[it, 0], to).start()
        if between_1 is not None:
            between_1()
        got(a_xc.at[it], a_rsem.at[it, 0])
        part = a_src[it, 0]
        for i in range(7):
            part = part + a_xc[it, i]
        a_src[it, 1] = part
        for i, to in enumerate(z_ids):
            remote(a_src.at[it, 1], a_z.at[it, i], a_ssem.at[it, 1], a_rsem.at[it, 1], to).start()
        if between_2 is not None:
            between_2()
        got(a_z.at[it], a_rsem.at[it, 1])
        for i in range(7):
            part = part + a_z[it, i]
        return part

    def b_sum(it, between=None):
        for i, to in enumerate(y_ids):
            remote(b_src.at[it], b_y.at[it, i], b_ssem.at[it], b_rsem.at[it], to).start()
        if between is not None:
            between()
        got(b_y.at[it], b_rsem.at[it])
        part = b_src[it]
        for i in range(7):
            part = part + b_y[it, i]
        return part

    def send_counts():
        cnt_src[...] = jnp.broadcast_to(jnp.sum(onehot, axis=1, keepdims=True), (NGROUP, 128))
        for i, to in enumerate(y_ids):
            remote(cnt_src, cnt_y.at[i], cnt_ssem, cnt_rsem, to).start()

    def z_first():
        for i, to in enumerate(xc_ids):
            remote(z_src.at[0], z_xc.at[i], z_ssem.at[0], z_rsem.at[0], to).start()

    def z_second():
        got(z_xc, z_rsem.at[0])
        part = z_src[0]
        for i in range(7):
            part = part + z_xc[i]
        z_src[1] = part
        for i, to in enumerate(z_ids):
            remote(z_src.at[1], z_z.at[i], z_ssem.at[1], z_rsem.at[1], to).start()

    def columns(it, scale):
        for v in range(2):
            out = mm(split3(scale[:, v * 512 : v * 512 + 512]), k_buf[v], NT)
            b_src[it, :, pl.ds(v * 1024, 1024)] = jnp.sum(out, axis=0, keepdims=True)

    def row_sums(it, scale):
        for v in range(2):
            out = mm(split3(scale[:, v * 1024 : v * 1024 + 1024]), k_buf[v])
            a_src[it, 0, :, pl.ds(v * 512, 512)] = jnp.sum(out, axis=0, keepdims=True)

    window_scale = 1.0 / a_sum(0, send_counts)
    columns(0, window_scale)
    proto_scale = 1.0 / (PROTOS * b_sum(0, z_first))
    row_sums(1, proto_scale)
    window_scale = 1.0 / a_sum(1)
    columns(1, window_scale)
    proto_scale = 1.0 / (PROTOS * b_sum(1, z_second))
    row_sums(2, proto_scale)
    window_scale = 1.0 / a_sum(2)
    columns(2, window_scale)
    proto_scale = 1.0 / (PROTOS * b_sum(2))
    row_sums(3, proto_scale)

    def assign():
        for v in range(2):
            for i in range(8):
                p = proto_scale[:, v * 1024 + i * 128 : v * 1024 + i * 128 + 128]
                col = jnp.broadcast_to(p, (128, 128)).T
                for j in range(4):
                    at = (v, pl.ds(i * 128, 128), pl.ds(j * 128, 128))
                    t_buf[at] = k_buf[at].astype(F32) * col

    def cross():
        for v in range(2):

            def block(kb, acc):
                k0 = pl.multiple_of(kb * 32, 32)
                prod = t_buf[1 - v, pl.ds(k0, 32)] * s_buf[v, pl.ds(k0, 32)]
                return acc + jnp.sum(prod.reshape(4, 8, 512), axis=0)

            acc = lax.fori_loop(0, 32, block, jnp.zeros((8, 512), F32))
            x_rows[v] = jnp.sum(acc, axis=0, keepdims=True)

    last = 1.0 / a_sum(3, assign, cross)

    got(z_z, z_rsem.at[1])
    totals = z_src[1]
    for i in range(7):
        totals = totals + z_z[i]
    got(cnt_y, cnt_rsem)
    counts = cnt_src[...]
    for i in range(7):
        counts = counts + cnt_y[i]
    seen = jnp.sum(onehot * jnp.concatenate([counts] * 4, axis=1), axis=0, keepdims=True)
    weight = WINDOWS / (NGROUP * seen)
    last_v = [last[:, 0:512], last[:, 512:1024]]
    tot_v = [totals[:, 0:512], totals[:, 512:1024]]
    a_v = [5.0 * weight / tot_v[v] for v in range(2)]
    b_v = [5.0 * weight * last_v[1 - v] for v in range(2)]
    terms = jnp.zeros((1, 512), F32)
    for v in range(2):
        terms = terms + 0.5 * weight * (jnp.log(tot_v[v]) / 64.0 - 10.0 * last_v[1 - v] * x_rows[v])
    terms = terms[:, 0:128] + terms[:, 128:256] + terms[:, 256:384] + terms[:, 384:512]
    me_xc = x * NC + c
    l_xc[me_xc] = terms
    for to in xc_ids:
        remote(l_xc.at[me_xc], l_xc.at[me_xc], l_ssem.at[0], l_rsem.at[0], to).start()

    def add_slots(ref):
        out = ref[0]
        for i in range(1, 8):
            out = out + ref[i]
        return out

    for i, yy in enumerate(y_of + [y]):
        k0 = pl.multiple_of(yy * 128, 128)
        part = jnp.zeros((128, FEAT), F32)
        for v in range(2):
            at = (pl.ds(k0, 128), slice(None))
            g = (e_buf[(v,) + at] * a_v[v] - t_buf[(1 - v,) + at] * b_v[v]).astype(BF16)
            g_buf[(v,) + at] = g
            part = part + mm(g, q16[v])
        kg_src[i] = part
        if i < 7:
            remote(kg_src.at[i], kg_y.at[i], kg_ssem, kg_rsem, y_ids[i]).start()

    c_src[...] = mm(keys_t[...], g_buf[1 - c])
    remote(c_src, c_rcv, f_ssem.at[0], f_rsem.at[0], sib).start()
    own = mm(keys_t[...], g_buf[c])
    got(c_rcv, f_rsem.at[0])
    x_src[...] = own + c_rcv[...]
    for i, xx in enumerate(x_of):
        remote(x_src.at[pl.ds(pl.multiple_of(xx * 32, 32), 32)], x_rcv.at[i], f_ssem.at[1], f_rsem.at[1], x_ids[i]).start()
    got(x_rcv, f_rsem.at[1])
    part = x_src[pl.ds(pl.multiple_of(x * 32, 32), 32)] + x_rcv[0] + x_rcv[1] + x_rcv[2]
    for i in range(4):
        w_src[i] = part[:, i * 128 : i * 128 + 128]
    others = [l for l in range(8)]
    got(l_xc.at[pl.ds(0, 7)], l_rsem.at[0])
    l_z[z] = add_slots(l_xc)
    for i, to in enumerate(z_ids):
        remote(l_z.at[z], l_z.at[z], l_ssem.at[1], l_rsem.at[1], to).start()
        remote(w_src.at[lax.rem(z_of[i], NZL)], w_rcv.at[i], f_ssem.at[2], f_rsem.at[2], to).start()
    got(w_rcv, f_rsem.at[2])
    part = w_src[zl]
    for i in range(7):
        part = part + w_rcv[i]
    mine = fin.at[c, pl.ds(pl.multiple_of(x * 32, 32), 32)]
    fin[c, pl.ds(pl.multiple_of(x * 32, 32), 32)] = part
    for to in xc_ids:
        remote(mine, mine, f_ssem.at[3], f_rsem.at[3], to).start()
    got(l_z.at[pl.ds(0, 7)], l_rsem.at[1])
    l_y[y] = add_slots(l_z)
    for to in y_ids:
        remote(l_y.at[y], l_y.at[y], l_ssem.at[2], l_rsem.at[2], to).start()

    got(kg_y, kg_rsem)
    part = kg_src[7]
    for i in range(7):
        part = part + kg_y[i]
    pgrad_ref[...] = unit_back(kraw[y].astype(F32), part)

    got(w_rcv, f_rsem.at[3])
    for v in range(2):
        qt[v] = fin[v].T
    for v in range(2):
        grad = qt[v, pl.ds(pl.multiple_of(c * 64, 64), 64)]
        view_ref[v] = unit_back(pooled[pl.ds(v * 64, 64)], grad)

    got(l_y.at[pl.ds(0, 7)], l_rsem.at[2])
    loss_ref[...] = jnp.sum(add_slots(l_y), axis=1, keepdims=True) * (1.0 / WINDOWS)

    sent(qg.at[0, pl.ds(0, 3)], g_ssem)
    sent(qg.at[0], gs_ssem)
    for it in range(4):
        sent(a_xc.at[it], a_ssem.at[it, 0])
        sent(a_z.at[it], a_ssem.at[it, 1])
    for it in range(3):
        sent(b_y.at[it], b_ssem.at[it])
    sent(z_xc, z_ssem.at[0])
    sent(z_z, z_ssem.at[1])
    sent(cnt_y, cnt_ssem)
    sent(kg_y, kg_ssem)
    sent(c_rcv, f_ssem.at[0])
    sent(x_rcv, f_ssem.at[1])
    sent(w_rcv, f_ssem.at[2])
    sent(w_rcv, f_ssem.at[3])
    for i in range(3):
        sent(l_xc.at[pl.ds(0, 7)], l_ssem.at[i])


def on_device(tokens, offsets, species, prototypes):
    vmem = pltpu.VMEM
    dma = pltpu.SemaphoreType.DMA
    anywhere = pl.BlockSpec(memory_space=pl.ANY)
    inside = pl.BlockSpec(memory_space=pltpu.VMEM)
    scratch = [
        vmem((64 * SEQ, FEAT), BF16),
        vmem((8, 128, FEAT), BF16),
        vmem((1024, FEAT), BF16),
        vmem((FEAT, 1024), BF16),
        vmem((128, FEAT), F32),
        vmem((2, 4, 136, FEAT), F32),
        vmem((2, 512, FEAT), BF16),
        vmem((2, 1024, 512), F32),
        vmem((2, 1024, 512), F32),
        vmem((2, 1024, 512), BF16),
        vmem((2, 1024, 512), F32),
        vmem((2, 1024, 512), BF16),
        vmem((4, 2, 1, 1024), F32),
        vmem((4, 7, 1, 1024), F32),
        vmem((4, 7, 1, 1024), F32),
        vmem((3, 1, 2048), F32),
        vmem((3, 7, 1, 2048), F32),
        vmem((2, 1, 1024), F32),
        vmem((7, 1, 1024), F32),
        vmem((7, 1, 1024), F32),
        vmem((NGROUP, 128), F32),
        vmem((7, NGROUP, 128), F32),
        vmem((8, 128, FEAT), F32),
        vmem((7, 128, FEAT), F32),
        vmem((FEAT, 512), F32),
        vmem((FEAT, 512), F32),
        vmem((FEAT, 512), F32),
        vmem((3, 32, 512), F32),
        vmem((4, 32, 128), F32),
        vmem((7, 32, 128), F32),
        vmem((2, FEAT, 128), F32),
        vmem((8, 1, 128), F32),
        vmem((8, 1, 128), F32),
        vmem((8, 1, 128), F32),
        vmem((2, 1, 512), F32),
        vmem((2, 128, FEAT), F32),
        dma((2,)),
        dma, dma((3,)), dma, dma((4,)),
        dma((4, 2)), dma((4, 2)), dma((3,)), dma((3,)), dma((2,)), dma((2,)), dma, dma,
        dma, dma, dma((4,)), dma((4,)), dma((3,)), dma((3,)),
    ]
    view_grads, proto_grads, loss = pl.pallas_call(
        kernel,
        out_shape=(
            jax.ShapeDtypeStruct((2, 64, FEAT), F32),
            jax.ShapeDtypeStruct((128, FEAT), F32),
            jax.ShapeDtypeStruct((1, 1), F32),
        ),
        in_specs=[anywhere, inside, inside, anywhere],
        out_specs=(inside, inside, inside),
        scratch_shapes=scratch,
        compiler_params=pltpu.CompilerParams(
            collective_id=0, has_side_effects=True, vmem_limit_bytes=56 * 2**20
        ),
        name="swav_step",
    )(
        tokens.reshape(64 * SEQ, FEAT),
        offsets,
        species.reshape(1, 64),
        prototypes.reshape(8, 8, 128, FEAT),
    )
    return view_grads, proto_grads, loss.reshape(())


def solution(mesh):
    return jax.shard_map(
        on_device,
        mesh=mesh,
        in_specs=(P("dp", None, None), P(None, "dp"), P("dp"), P("proto", None)),
        out_specs=(P(None, "dp", None), P(("proto", "dp"), None), P()),
        check_vma=False,
    )
```

```python
import math

import jax
import jax.numpy as jnp
from jax import lax
from jax.experimental import pallas as pl
from jax.experimental.pallas import tpu as pltpu
from jax.sharding import PartitionSpec as P

MESH = pl.DeviceIdType.MESH
F32 = jnp.float32
BF16 = jnp.bfloat16
NGROUP = 16
CROP = 24
SEQ = 32
FEAT = 128
WINDOWS = 4096
PROTOS = 65536
EPS = 1e-6
NY, NZL, NC, NZH, NX = 8, 4, 2, 2, 4
NZ = NZH * NZL
RING8 = (4, 3, 5, 2, 6, 1, 7)
XC = ((2, 0), (2, 1), (1, 0), (3, 0), (1, 1), (3, 1), (0, 1))
RING4 = (2, 1, 3)
PLANE = tuple(
    sorted(
        ((dx, dz) for dx in range(NX) for dz in range(NZ) if dx or dz),
        key=lambda o: -(min(o[0], NX - o[0]) + min(o[1], NZ - o[1])),
    )
)
NP = len(PLANE)
NT = (((1,), (1,)), ((), ()))
NN = (((1,), (0,)), ((), ()))


def mm(a, b, dims=NN):
    return lax.dot_general(a, b, dims, preferred_element_type=F32)


def split3(row, count=16):
    hi = row.astype(BF16).astype(F32)
    rest = row - hi
    mid = rest.astype(BF16).astype(F32)
    lo = rest - mid
    width = row.shape[1]
    at = lax.broadcasted_iota(jnp.int32, (count, width), 0)
    full = lambda r: jnp.broadcast_to(r, (count, width))
    out = jnp.where(at == 0, full(hi), jnp.where(at == 1, full(mid), jnp.where(at == 2, full(lo), 0.0)))
    return out.astype(BF16)


def unit_scale(rows):
    return lax.rsqrt(jnp.mean(rows * rows, axis=-1, keepdims=True) + EPS)


def unit_back(rows, grad):
    scale = unit_scale(rows)
    along = jnp.mean(rows * grad, axis=-1, keepdims=True)
    return (grad - rows * (along * scale * scale)) * (scale / math.sqrt(FEAT))


def kernel(
    tok_ref, off_ref, spec_ref, proto_ref,
    view_ref, pgrad_ref, loss_ref,
    tok, kraw, keys, keys_t, pooled, qg, q16, s_buf, e_buf, k_buf, t_buf, two,
    a_src, a_c, a_pl, b_src, b_y, z_src, z_c, z_pl, cnt_src, cnt_y,
    kg_src, kg_half, kg_fwd, kg_y, c_src, c_rcv, x_src, x_rcv, w_src, w_rcv, fin, l_xc, l_z, l_y,
    x_rows, p_row, ab_rows, qt,
    load_sem, g_ssem, g_rsem, gs_ssem, gs_rsem,
    a_ssem, a_rsem, b_ssem, b_rsem, z_ssem, z_rsem, cnt_ssem, cnt_rsem,
    kg_ssem, kg_rsem, f_ssem, f_rsem, fin_ssem, fin_rsem, l_ssem, l_rsem,
):
    dp = lax.axis_index("dp")
    pr = lax.axis_index("proto")
    y, zl, c = lax.div(dp, 8), lax.rem(lax.div(dp, 2), 4), lax.rem(dp, 2)
    zh, x = lax.div(pr, 4), lax.rem(pr, 4)
    z = zh * NZL + zl

    def dev(y=y, z=z, c=c, x=x):
        return ((y * NZL + lax.rem(z, NZL)) * NC + c, lax.div(z, NZL) * NX + x)

    xc_ids = [dev(x=lax.rem(x + dx, NX), c=lax.rem(c + dc, NC)) for dx, dc in XC]
    z_of = [lax.rem(z + j, NZ) for j in RING8]
    z_ids = [dev(z=k) for k in z_of]
    y_of = [lax.rem(y + j, NY) for j in RING8]
    y_ids = [dev(y=k) for k in y_of]
    x_of = [lax.rem(x + j, NX) for j in RING4]
    x_ids = [dev(x=k) for k in x_of]
    sib = dev(c=1 - c)
    plane_ids = [dev(x=lax.rem(x + dx, NX), z=lax.rem(z + dz, NZ)) for dx, dz in PLANE]
    cross_ids = [xc_ids[i] for i in range(7) if XC[i][0] and XC[i][1]]

    def remote(src, dst, ssem, rsem, to):
        return pltpu.make_async_remote_copy(
            src_ref=src, dst_ref=dst, send_sem=ssem, recv_sem=rsem, device_id=to, device_id_type=MESH
        )

    def got(ref, sem):
        remote(ref, ref, sem, sem, sib).wait_recv()

    def sent(ref, sem):
        remote(ref, ref, sem, sem, sib).wait_send()

    barrier = pltpu.get_barrier_semaphore()
    load_tok = pltpu.make_async_copy(tok_ref, tok, load_sem.at[0])
    load_key = pltpu.make_async_copy(proto_ref.at[:, zl * NC + c], kraw, load_sem.at[1])
    load_tok.start()
    load_key.start()
    for to in [sib] + plane_ids + cross_ids + y_ids:
        pl.semaphore_signal(barrier, inc=1, device_id=to, device_id_type=MESH)

    off = off_ref[...].astype(F32)
    off_row = jnp.concatenate([off[0:1], off[1:2]], axis=1)
    lane = lax.broadcasted_iota(jnp.int32, (128, 128), 1)
    first = jnp.broadcast_to(off_row, (128, 128)).T.astype(jnp.int32)
    row = lax.broadcasted_iota(jnp.int32, (128, 128), 0)
    first = first + (row & 63) * SEQ
    load_tok.wait()
    total = jnp.zeros((128, FEAT), F32)
    for part in range(4):
        mask = jnp.concatenate(
            [
                jnp.where((lane + col >= first) & (lane + col < first + CROP), 1.0, 0.0).astype(BF16)
                for col in range(part * 512, part * 512 + 512, 128)
            ],
            axis=1,
        )
        total = total + mm(mask, tok[pl.ds(part * 512, 512)])
    rows = total / CROP
    pooled[...] = rows
    query = (rows * unit_scale(rows) / math.sqrt(FEAT)).astype(BF16).astype(F32)
    qg[c, zl, pl.ds(0, 128)] = query
    spec = spec_ref[...].astype(F32)
    both = jnp.concatenate([spec, spec], axis=1)
    half = lax.broadcasted_iota(jnp.int32, (8, 128), 1) // 64
    qg[c, zl, pl.ds(128, 8)] = jnp.where(half == c, jnp.broadcast_to(both, (8, 128)), 0.0)

    pl.semaphore_wait(barrier, 11 + NP)
    step2 = 2 + 4 * c
    mine = qg.at[c, zl]
    for i, to in enumerate((dev(z=lax.rem(z + step2, NZ)), dev(z=lax.rem(z + 1, NZ)), dev(z=lax.rem(z + 7, NZ)))):
        remote(mine, mine, g_ssem, g_rsem.at[i], to).start()
    remote(mine, mine, gs_ssem, gs_rsem.at[0], sib).start()

    load_key.wait()
    for i in range(8):
        raw = kraw[i].astype(F32)
        unit = raw * unit_scale(raw) / math.sqrt(FEAT)
        keys[pl.ds(i * 128, 128)] = unit.astype(BF16)
        turned = unit.astype(BF16).astype(F32).T.astype(BF16)
        keys_t[:, pl.ds(i * 128, 128)] = turned
        keys_t[:, pl.ds(1024 + i * 128, 128)] = turned

    def scores(zp):
        zp128 = pl.multiple_of(zp * 128, 128)
        pair = []
        for v in range(2):
            q = jnp.concatenate([qg[0, zp, pl.ds(v * 64, 64)], qg[1, zp, pl.ds(v * 64, 64)]], axis=0).astype(BF16)
            q16[v, pl.ds(zp128, 128)] = q
            pair.append(q)
        rhs = jnp.concatenate(pair, axis=0)

        def block(kb, sums):
            k0 = pl.multiple_of(kb * 128, 128)
            s = mm(keys[pl.ds(k0, 128)], rhs, NT)
            e = jnp.exp(s * 10.0)
            k = (e * e).astype(BF16)
            for v in range(2):
                at = (v, pl.ds(k0, 128), pl.ds(zp128, 128))
                s_buf[at] = s[:, v * 128 : v * 128 + 128]
                e_buf[at] = e[:, v * 128 : v * 128 + 128]
                k_buf[at] = k[:, v * 128 : v * 128 + 128]
            fold = lambda a: jnp.sum(a.reshape(16, 8, 256), axis=0)
            return sums[0] + fold(e), sums[1] + fold(k.astype(F32))

        zero = jnp.zeros((8, 256), F32)
        es, ks = lax.fori_loop(0, 8, block, (zero, zero))
        es = jnp.sum(es, axis=0, keepdims=True)
        ks = jnp.sum(ks, axis=0, keepdims=True)
        for v in range(2):
            z_src[0, :, pl.ds(v * 512 + zp128, 128)] = es[:, v * 128 : v * 128 + 128]
            a_src[0, 0, :, pl.ds(v * 512 + zp128, 128)] = ks[:, v * 128 : v * 128 + 128] * (1.0 / PROTOS)

    got(qg.at[1 - c, zl], gs_rsem.at[0])
    scores(zl)
    for i, step in ((1, 3), (2, 1), (0, 2)):
        zp = lax.rem(zl + step, NZL)
        piece = qg.at[c, zp]
        got(piece, g_rsem.at[i])
        remote(piece, piece, gs_ssem, gs_rsem.at[i + 1], sib).start()
        got(qg.at[1 - c, zp], gs_rsem.at[i + 1])
        scores(zp)

    spec_row = jnp.concatenate([qg[0, i, pl.ds(128, 1)] + qg[1, i, pl.ds(128, 1)] for i in range(4)], axis=1)
    group = lax.broadcasted_iota(jnp.int32, (NGROUP, 512), 0)
    onehot = jnp.where(group == jnp.broadcast_to(spec_row, (NGROUP, 512)).astype(jnp.int32), 1.0, 0.0)

    def a_sum(it, between_1=None, between_2=None):
        remote(a_src.at[it, 0], a_c.at[it], a_ssem.at[it, 0], a_rsem.at[it, 0], sib).start()
        if between_1 is not None:
            between_1()
        got(a_c.at[it], a_rsem.at[it, 0])
        part = a_src[it, 0] + a_c[it]
        a_src[it, 1] = part
        for i, to in enumerate(plane_ids):
            remote(a_src.at[it, 1], a_pl.at[it, i], a_ssem.at[it, 1], a_rsem.at[it, 1], to).start()
        if between_2 is not None:
            between_2()
        got(a_pl.at[it], a_rsem.at[it, 1])
        for i in range(NP):
            part = part + a_pl[it, i]
        return part

    def b_sum(it, between=None):
        for i, to in enumerate(y_ids):
            remote(b_src.at[it], b_y.at[it, i], b_ssem.at[it], b_rsem.at[it], to).start()
        if between is not None:
            between()
        got(b_y.at[it], b_rsem.at[it])
        part = b_src[it]
        for i in range(7):
            part = part + b_y[it, i]
        return part

    def send_counts():
        cnt_src[...] = jnp.broadcast_to(jnp.sum(onehot, axis=1, keepdims=True), (NGROUP, 128))
        for i, to in enumerate(y_ids):
            remote(cnt_src, cnt_y.at[i], cnt_ssem, cnt_rsem, to).start()

    def z_first():
        remote(z_src.at[0], z_c, z_ssem.at[0], z_rsem.at[0], sib).start()

    def z_second():
        got(z_c, z_rsem.at[0])
        z_src[1] = z_src[0] + z_c[...]
        for i, to in enumerate(plane_ids):
            remote(z_src.at[1], z_pl.at[i], z_ssem.at[1], z_rsem.at[1], to).start()

    def halves(value, k0, width):
        hi = value.astype(BF16)
        two[pl.ds(k0, width)] = hi
        two[pl.ds(1024 + k0, width)] = (value - hi.astype(F32)).astype(BF16)

    def split_e(v):
        def block(kb, carry):
            k0 = pl.multiple_of(kb * 32, 32)
            halves(e_buf[v, pl.ds(k0, 32)], k0, 32)
            return carry

        lax.fori_loop(0, 32, block, 0)

    def split_t(v):
        for i in range(8):
            p = p_row[:, pl.ds(pl.multiple_of(v * 1024 + i * 128, 128), 128)]
            col = jnp.broadcast_to(p, (128, 128)).T
            t = k_buf[v, pl.ds(i * 128, 128)].astype(F32) * jnp.concatenate([col] * 4, axis=1)
            t_buf[v, pl.ds(i * 128, 128)] = t
            halves(t, i * 128, 128)

    def q_core(step):
        prepare = (split_e, split_t)[step]
        theirs = 1 - c if step == 0 else c
        prepare(theirs)
        c_src[step] = mm(keys_t[...], two[...])
        remote(c_src.at[step], c_rcv.at[step], f_ssem.at[step, 0], f_rsem.at[step, 0], sib).start()
        prepare(1 - theirs)
        x_src[step] = mm(keys_t[...], two[...])

    def q_x(step):
        got(c_rcv.at[step], f_rsem.at[step, 0])
        x_src[step] = x_src[step] + c_rcv[step]
        for i, xx in enumerate(x_of):
            piece = x_src.at[step, pl.ds(pl.multiple_of(xx * 32, 32), 32)]
            remote(piece, x_rcv.at[step, i], f_ssem.at[step, 1], f_rsem.at[step, 1], x_ids[i]).start()

    def q_z(step):
        got(x_rcv.at[step], f_rsem.at[step, 1])
        part = x_src[step, pl.ds(pl.multiple_of(x * 32, 32), 32)]
        for i in range(3):
            part = part + x_rcv[step, i]
        for i in range(4):
            w_src[step, i] = part[:, i * 128 : i * 128 + 128]
        for i, to in enumerate(z_ids):
            piece = w_src.at[step, lax.rem(z_of[i], NZL)]
            remote(piece, w_rcv.at[step, i], f_ssem.at[step, 2], f_rsem.at[step, 2], to).start()

    def q_end(step):
        got(w_rcv.at[step], f_rsem.at[step, 2])
        part = w_src[step, zl]
        for i in range(7):
            part = part + w_rcv[step, i]
        return part

    def columns(it, scale):
        for v in range(2):
            out = mm(split3(scale[:, v * 512 : v * 512 + 512]), k_buf[v], NT)
            b_src[it, :, pl.ds(v * 1024, 1024)] = jnp.sum(out, axis=0, keepdims=True)

    def row_sums(it, scale):
        for v in range(2):
            out = mm(split3(scale[:, v * 1024 : v * 1024 + 1024]), k_buf[v])
            a_src[it, 0, :, pl.ds(v * 512, 512)] = jnp.sum(out, axis=0, keepdims=True)

    def beside_a0():
        send_counts()
        q_core(0)

    def beside_b0():
        z_first()
        q_x(0)

    def beside_b1():
        z_second()
        q_z(0)

    window_scale = 1.0 / a_sum(0, None, beside_a0)
    columns(0, window_scale)
    proto_scale = 1.0 / (PROTOS * b_sum(0, beside_b0))
    row_sums(1, proto_scale)
    window_scale = 1.0 / a_sum(1)
    columns(1, window_scale)
    proto_scale = 1.0 / (PROTOS * b_sum(1, beside_b1))
    row_sums(2, proto_scale)
    window_scale = 1.0 / a_sum(2)
    columns(2, window_scale)
    proto_scale = 1.0 / (PROTOS * b_sum(2))
    row_sums(3, proto_scale)
    p_row[...] = proto_scale

    def cross():
        for v in range(2):

            def block(kb, acc):
                k0 = pl.multiple_of(kb * 32, 32)
                prod = t_buf[1 - v, pl.ds(k0, 32)] * s_buf[v, pl.ds(k0, 32)]
                return acc + jnp.sum(prod.reshape(4, 8, 512), axis=0)

            acc = lax.fori_loop(0, 32, block, jnp.zeros((8, 512), F32))
            x_rows[v] = jnp.sum(acc, axis=0, keepdims=True)

    def beside_a3():
        q_core(1)
        q_x(1)
        cross()

    last = 1.0 / a_sum(3, None, beside_a3)

    got(z_pl, z_rsem.at[1])
    totals = z_src[1]
    for i in range(NP):
        totals = totals + z_pl[i]
    got(cnt_y, cnt_rsem)
    counts = cnt_src[...]
    for i in range(7):
        counts = counts + cnt_y[i]
    seen = jnp.sum(onehot * jnp.concatenate([counts] * 4, axis=1), axis=0, keepdims=True)
    weight = WINDOWS / (NGROUP * seen)
    last_v = [last[:, 0:512], last[:, 512:1024]]
    tot_v = [totals[:, 0:512], totals[:, 512:1024]]
    a_v = [5.0 * weight / tot_v[v] for v in range(2)]
    b_v = [5.0 * weight * last_v[1 - v] for v in range(2)]
    for v in range(2):
        ab_rows[0, v] = a_v[v]
        ab_rows[1, v] = b_v[v]
    terms = jnp.zeros((1, 512), F32)
    for v in range(2):
        terms = terms + 0.5 * weight * (jnp.log(tot_v[v]) / 64.0 - 10.0 * last_v[1 - v] * x_rows[v])
    terms = terms[:, 0:128] + terms[:, 128:256] + terms[:, 256:384] + terms[:, 384:512]
    me_xc = x * NC + c
    l_xc[me_xc] = terms
    for to in xc_ids:
        remote(l_xc.at[me_xc], l_xc.at[me_xc], l_ssem.at[0], l_rsem.at[0], to).start()

    def add_slots(ref):
        out = ref[0]
        for i in range(1, 8):
            out = out + ref[i]
        return out

    def key_part(slot, yy):
        k0 = pl.multiple_of(yy * 128, 128)
        part = jnp.zeros((128, FEAT), F32)
        for v in range(2):
            at = (pl.ds(k0, 128), slice(None))
            g = (e_buf[(v,) + at] * a_v[v] - t_buf[(1 - v,) + at] * b_v[v]).astype(BF16)
            part = part + mm(g, q16[v])
        kg_src[slot] = part

    ahead = lambda j: lax.rem(y + j, NY)
    up1, up2, down1, down2 = (dev(y=ahead(j)) for j in (1, 2, 7, 6))
    key_part(4, ahead(4))
    remote(kg_src.at[4, pl.ds(0, 64)], kg_half.at[0], kg_ssem.at[0], kg_rsem.at[0], up2).start()
    remote(kg_src.at[4, pl.ds(64, 64)], kg_half.at[1], kg_ssem.at[1], kg_rsem.at[1], down2).start()
    key_part(3, ahead(3))
    remote(kg_src.at[3], kg_fwd.at[0], kg_ssem.at[2], kg_rsem.at[2], up1).start()
    key_part(5, ahead(5))
    remote(kg_src.at[5], kg_fwd.at[1], kg_ssem.at[3], kg_rsem.at[3], down1).start()
    key_part(2, ahead(2))
    key_part(6, ahead(6))
    key_part(1, ahead(1))
    remote(kg_src.at[1], kg_y.at[0], kg_ssem.at[4], kg_rsem.at[4], up1).start()
    key_part(7, ahead(7))
    remote(kg_src.at[7], kg_y.at[1], kg_ssem.at[5], kg_rsem.at[5], down1).start()
    key_part(0, y)

    q_z(1)
    got(kg_fwd.at[0], kg_rsem.at[2])
    got(kg_half.at[0], kg_rsem.at[0])
    kg_src[2, pl.ds(0, 64)] = kg_src[2, pl.ds(0, 64)] + kg_fwd[0, pl.ds(0, 64)] + kg_half[0]
    kg_src[2, pl.ds(64, 64)] = kg_src[2, pl.ds(64, 64)] + kg_fwd[0, pl.ds(64, 64)]
    remote(kg_src.at[2], kg_y.at[2], kg_ssem.at[6], kg_rsem.at[6], up2).start()
    got(kg_fwd.at[1], kg_rsem.at[3])
    got(kg_half.at[1], kg_rsem.at[1])
    kg_src[6, pl.ds(0, 64)] = kg_src[6, pl.ds(0, 64)] + kg_fwd[1, pl.ds(0, 64)]
    kg_src[6, pl.ds(64, 64)] = kg_src[6, pl.ds(64, 64)] + kg_fwd[1, pl.ds(64, 64)] + kg_half[1]
    remote(kg_src.at[6], kg_y.at[3], kg_ssem.at[7], kg_rsem.at[7], down2).start()

    got(l_xc.at[pl.ds(0, 7)], l_rsem.at[0])
    l_z[z] = add_slots(l_xc)
    for to in z_ids:
        remote(l_z.at[z], l_z.at[z], l_ssem.at[1], l_rsem.at[1], to).start()

    at = pl.ds(pl.multiple_of(zl * 128, 128), 128)
    part = ab_rows[0, c, :, at] * q_end(0) - ab_rows[1, c, :, at] * q_end(1)
    mine = fin.at[c, pl.ds(pl.multiple_of(x * 32, 32), 32)]
    fin[c, pl.ds(pl.multiple_of(x * 32, 32), 32)] = part
    for to in xc_ids:
        remote(mine, mine, fin_ssem, fin_rsem, to).start()
    got(l_z.at[pl.ds(0, 7)], l_rsem.at[1])
    l_y[y] = add_slots(l_z)
    for to in y_ids:
        remote(l_y.at[y], l_y.at[y], l_ssem.at[2], l_rsem.at[2], to).start()

    part = kg_src[0]
    for i, k in ((0, 4), (1, 5), (2, 6), (3, 7)):
        got(kg_y.at[i], kg_rsem.at[k])
        part = part + kg_y[i]
    pgrad_ref[...] = unit_back(kraw[y].astype(F32), part)

    got(w_rcv.at[0], fin_rsem)
    for v in range(2):
        qt[v] = fin[v].T
    for v in range(2):
        grad = qt[v, pl.ds(pl.multiple_of(c * 64, 64), 64)]
        view_ref[v] = unit_back(pooled[pl.ds(v * 64, 64)], grad)

    got(l_y.at[pl.ds(0, 7)], l_rsem.at[2])
    loss_ref[...] = jnp.sum(add_slots(l_y), axis=1, keepdims=True) * (1.0 / WINDOWS)

    sent(qg.at[0, pl.ds(0, 3)], g_ssem)
    sent(qg.at[0], gs_ssem)
    for it in range(4):
        sent(a_c.at[it], a_ssem.at[it, 0])
        sent(a_pl.at[it], a_ssem.at[it, 1])
    for it in range(3):
        sent(b_y.at[it], b_ssem.at[it])
    sent(z_c, z_ssem.at[0])
    sent(z_pl, z_ssem.at[1])
    sent(cnt_y, cnt_ssem)
    for i in range(2):
        sent(kg_half.at[i], kg_ssem.at[i])
        sent(kg_fwd.at[i], kg_ssem.at[2 + i])
        sent(kg_y.at[i], kg_ssem.at[4 + i])
        sent(kg_y.at[2 + i], kg_ssem.at[6 + i])
        sent(c_rcv.at[i], f_ssem.at[i, 0])
        sent(x_rcv.at[i], f_ssem.at[i, 1])
        sent(w_rcv.at[i], f_ssem.at[i, 2])
    sent(w_rcv.at[0], fin_ssem)
    for i in range(3):
        sent(l_xc.at[pl.ds(0, 7)], l_ssem.at[i])


def on_device(tokens, offsets, species, prototypes):
    vmem = pltpu.VMEM
    dma = pltpu.SemaphoreType.DMA
    anywhere = pl.BlockSpec(memory_space=pl.ANY)
    inside = pl.BlockSpec(memory_space=pltpu.VMEM)
    scratch = [
        vmem((64 * SEQ, FEAT), BF16),
        vmem((8, 128, FEAT), BF16),
        vmem((1024, FEAT), BF16),
        vmem((FEAT, 2048), BF16),
        vmem((128, FEAT), F32),
        vmem((2, 4, 136, FEAT), F32),
        vmem((2, 512, FEAT), BF16),
        vmem((2, 1024, 512), F32),
        vmem((2, 1024, 512), F32),
        vmem((2, 1024, 512), BF16),
        vmem((2, 1024, 512), F32),
        vmem((2048, 512), BF16),
        vmem((4, 2, 1, 1024), F32),
        vmem((4, 1, 1024), F32),
        vmem((4, NP, 1, 1024), F32),
        vmem((3, 1, 2048), F32),
        vmem((3, 7, 1, 2048), F32),
        vmem((2, 1, 1024), F32),
        vmem((1, 1024), F32),
        vmem((NP, 1, 1024), F32),
        vmem((NGROUP, 128), F32),
        vmem((7, NGROUP, 128), F32),
        vmem((8, 128, FEAT), F32),
        vmem((2, 64, FEAT), F32),
        vmem((2, 128, FEAT), F32),
        vmem((4, 128, FEAT), F32),
        vmem((2, FEAT, 512), F32),
        vmem((2, FEAT, 512), F32),
        vmem((2, FEAT, 512), F32),
        vmem((2, 3, 32, 512), F32),
        vmem((2, 4, 32, 128), F32),
        vmem((2, 7, 32, 128), F32),
        vmem((2, FEAT, 128), F32),
        vmem((8, 1, 128), F32),
        vmem((8, 1, 128), F32),
        vmem((8, 1, 128), F32),
        vmem((2, 1, 512), F32),
        vmem((1, 2048), F32),
        vmem((2, 2, 1, 512), F32),
        vmem((2, 128, FEAT), F32),
        dma((2,)),
        dma, dma((3,)), dma, dma((4,)),
        dma((4, 2)), dma((4, 2)), dma((3,)), dma((3,)), dma((2,)), dma((2,)), dma, dma,
        dma((8,)), dma((8,)), dma((2, 3)), dma((2, 3)), dma, dma, dma((3,)), dma((3,)),
    ]
    view_grads, proto_grads, loss = pl.pallas_call(
        kernel,
        out_shape=(
            jax.ShapeDtypeStruct((2, 64, FEAT), F32),
            jax.ShapeDtypeStruct((128, FEAT), F32),
            jax.ShapeDtypeStruct((1, 1), F32),
        ),
        in_specs=[anywhere, inside, inside, anywhere],
        out_specs=(inside, inside, inside),
        scratch_shapes=scratch,
        compiler_params=pltpu.CompilerParams(
            collective_id=0, has_side_effects=True, vmem_limit_bytes=56 * 2**20
        ),
        name="swav_step",
    )(
        tokens.reshape(64 * SEQ, FEAT),
        offsets,
        species.reshape(1, 64),
        prototypes.reshape(8, 8, 128, FEAT),
    )
    return view_grads, proto_grads, loss.reshape(())


def solution(mesh):
    return jax.shard_map(
        on_device,
        mesh=mesh,
        in_specs=(P("dp", None, None), P(None, "dp"), P("dp"), P("proto", None)),
        out_specs=(P(None, "dp", None), P(("proto", "dp"), None), P()),
        check_vma=False,
    )
```

```python
import math

import jax
import jax.numpy as jnp
from jax import lax
from jax.experimental import pallas as pl
from jax.experimental.pallas import tpu as pltpu
from jax.sharding import PartitionSpec as P

MESH = pl.DeviceIdType.MESH
F32 = jnp.float32
BF16 = jnp.bfloat16
NGROUP = 16
CROP = 24
SEQ = 32
FEAT = 128
WINDOWS = 4096
PROTOS = 65536
EPS = 1e-6
NY, NZL, NC, NZH, NX = 8, 4, 2, 2, 4
NZ = NZH * NZL
RING8 = (4, 3, 5, 2, 6, 1, 7)
XC = ((2, 0), (2, 1), (1, 0), (3, 0), (1, 1), (3, 1), (0, 1))
RING4 = (2, 1, 3)
PLANE = tuple(
    sorted(
        ((dx, dz) for dx in range(NX) for dz in range(NZ) if dx or dz),
        key=lambda o: -(min(o[0], NX - o[0]) + min(o[1], NZ - o[1])),
    )
)
NP = len(PLANE)
NT = (((1,), (1,)), ((), ()))
NN = (((1,), (0,)), ((), ()))


def mm(a, b, dims=NN):
    return lax.dot_general(a, b, dims, preferred_element_type=F32)


def split3(row, count=16):
    hi = row.astype(BF16).astype(F32)
    rest = row - hi
    mid = rest.astype(BF16).astype(F32)
    lo = rest - mid
    width = row.shape[1]
    at = lax.broadcasted_iota(jnp.int32, (count, width), 0)
    full = lambda r: jnp.broadcast_to(r, (count, width))
    out = jnp.where(at == 0, full(hi), jnp.where(at == 1, full(mid), jnp.where(at == 2, full(lo), 0.0)))
    return out.astype(BF16)


def unit_scale(rows):
    return lax.rsqrt(jnp.mean(rows * rows, axis=-1, keepdims=True) + EPS)


def unit_back(rows, grad):
    scale = unit_scale(rows)
    along = jnp.mean(rows * grad, axis=-1, keepdims=True)
    return (grad - rows * (along * scale * scale)) * (scale / math.sqrt(FEAT))


def kernel(
    tok_ref, off_ref, spec_ref, proto_ref,
    view_ref, pgrad_ref, loss_ref,
    tok, mask, kraw, kunit, keys, keys_t, pooled, qg, q16, s_buf, e_buf, k_buf, t_buf, two,
    a_src, a_c, a_pl, b_src, b_y, r_src, r_px, r_mem, cnt_src, cnt_y,
    kg_src, kg_half, kg_fwd, kg_y, c_src, c_rcv, x_src, x_rcv, w_src, w_rcv, fin, l_xc, l_z, l_y,
    x_rows, p_row, ab_rows, qt,
    load_sem, g_ssem, g_rsem, gs_ssem, gs_rsem,
    a_ssem, a_rsem, b_ssem, b_rsem, r_ssem, r_rsem, cnt_ssem, cnt_rsem,
    kg_ssem, kg_rsem, f_ssem, f_rsem, fin_ssem, fin_rsem, l_ssem, l_rsem,
):
    dp = lax.axis_index("dp")
    pr = lax.axis_index("proto")
    y, zl, c = lax.div(dp, 8), lax.rem(lax.div(dp, 2), 4), lax.rem(dp, 2)
    zh, x = lax.div(pr, 4), lax.rem(pr, 4)
    z = zh * NZL + zl

    def dev(y=y, z=z, c=c, x=x):
        return ((y * NZL + lax.rem(z, NZL)) * NC + c, lax.div(z, NZL) * NX + x)

    xc_ids = [dev(x=lax.rem(x + dx, NX), c=lax.rem(c + dc, NC)) for dx, dc in XC]
    z_of = [lax.rem(z + j, NZ) for j in RING8]
    z_ids = [dev(z=k) for k in z_of]
    y_of = [lax.rem(y + j, NY) for j in RING8]
    y_ids = [dev(y=k) for k in y_of]
    x_of = [lax.rem(x + j, NX) for j in RING4]
    x_ids = [dev(x=k) for k in x_of]
    sib = dev(c=1 - c)
    plane_ids = [dev(x=lax.rem(x + dx, NX), z=lax.rem(z + dz, NZ)) for dx, dz in PLANE]
    px_ids = [plane_ids[i] for i in range(NP) if PLANE[i][1] % NZL == 0]
    step2 = 2 + 4 * c
    near = [lax.rem(z + step, NZ) for step in (step2, 1, 7)]
    near_ids = [dev(z=k) for k in near]
    near_cross_ids = [dev(z=k, c=1 - c) for k in near]
    far_cross_ids = near_cross_ids + [dev(z=lax.rem(z + 8 - step2, NZ), c=1 - c)]
    cross_ids = [xc_ids[i] for i in range(7) if XC[i][0] and XC[i][1]]

    def remote(src, dst, ssem, rsem, to):
        return pltpu.make_async_remote_copy(
            src_ref=src, dst_ref=dst, send_sem=ssem, recv_sem=rsem, device_id=to, device_id_type=MESH
        )

    def got(ref, sem):
        remote(ref, ref, sem, sem, sib).wait_recv()

    def sent(ref, sem):
        remote(ref, ref, sem, sem, sib).wait_send()

    barrier = pltpu.get_barrier_semaphore()
    load_tok = pltpu.make_async_copy(tok_ref, tok, load_sem.at[0])
    load_key = pltpu.make_async_copy(proto_ref, kraw, load_sem.at[1])
    load_tok.start()
    load_key.start()
    for to in [sib] + plane_ids + cross_ids + far_cross_ids + y_ids:
        pl.semaphore_signal(barrier, inc=1, device_id=to, device_id_type=MESH)

    off = off_ref[...].astype(F32)
    off_row = jnp.concatenate([off[0:1], off[1:2]], axis=1)
    lane = lax.broadcasted_iota(jnp.int32, (128, 128), 1)
    first = jnp.broadcast_to(off_row, (128, 128)).T.astype(jnp.int32)
    row = lax.broadcasted_iota(jnp.int32, (128, 128), 0)
    first = first + (row & 63) * SEQ
    for part in range(16):
        col = part * 128
        inside = (lane + col >= first) & (lane + col < first + CROP)
        mask[:, pl.ds(col, 128)] = jnp.where(inside, 1.0, 0.0).astype(BF16)
    load_tok.wait()
    total = mm(mask[...], tok[...])
    rows = total / CROP
    pooled[...] = rows
    query = (rows * unit_scale(rows) / math.sqrt(FEAT)).astype(BF16)
    qg[c, zl, pl.ds(0, 128)] = query.astype(F32)
    spec = spec_ref[...].astype(F32)
    both = jnp.concatenate([spec, spec], axis=1)
    half = lax.broadcasted_iota(jnp.int32, (8, 128), 1) // 64
    qg[c, zl, pl.ds(128, 8)] = jnp.where(half == c, jnp.broadcast_to(both, (8, 128)), 0.0)

    load_key.wait()

    def normalise(i, carry):
        at = pl.ds(pl.multiple_of(i * 256, 256), 256)
        raw = kraw[at].astype(F32)
        kunit[at] = (raw * unit_scale(raw) / math.sqrt(FEAT)).astype(BF16)
        return carry

    lax.fori_loop(0, 32, normalise, 0)
    pl.semaphore_wait(barrier, 15 + NP)

    mine = qg.at[c, zl]
    for i, to in enumerate(near_ids):
        remote(mine, mine, g_ssem, g_rsem.at[i], to).start()
    remote(mine, mine, gs_ssem, gs_rsem.at[0], sib).start()

    def whole(i, sums):
        at = pl.ds(pl.multiple_of(i * 256, 256), 256)
        e = jnp.exp(mm(kunit[at], query, NT) * 10.0)
        k = (e * e).astype(BF16).astype(F32)
        fold = lambda a: jnp.sum(a.reshape(32, 8, 128), axis=0)
        return sums[0] + fold(k), sums[1] + fold(e)

    zero = jnp.zeros((8, 128), F32)
    ks, es = lax.fori_loop(0, 32, whole, (zero, zero), unroll=2)
    r_src[:, pl.ds(0, 128)] = jnp.sum(ks, axis=0, keepdims=True)
    r_src[:, pl.ds(128, 128)] = jnp.sum(es, axis=0, keepdims=True)
    for i, to in enumerate(px_ids):
        remote(r_src, r_px.at[i], r_ssem.at[0], r_rsem.at[0], to).start()

    for i in range(8):
        block = kunit[pl.ds(pl.multiple_of((i * 8 + zl * NC + c) * 128, 128), 128)]
        keys[pl.ds(i * 128, 128)] = block
        turned = block.astype(F32).T.astype(BF16)
        keys_t[:, pl.ds(i * 128, 128)] = turned
        keys_t[:, pl.ds(1024 + i * 128, 128)] = turned

    def scores(zp):
        zp128 = pl.multiple_of(zp * 128, 128)
        pair = []
        for v in range(2):
            q = jnp.concatenate([qg[0, zp, pl.ds(v * 64, 64)], qg[1, zp, pl.ds(v * 64, 64)]], axis=0).astype(BF16)
            q16[v, pl.ds(zp128, 128)] = q
            pair.append(q)
        rhs = jnp.concatenate(pair, axis=0)

        def block(kb, carry):
            k0 = pl.multiple_of(kb * 128, 128)
            s = mm(keys[pl.ds(k0, 128)], rhs, NT)
            e = jnp.exp(s * 10.0)
            k = (e * e).astype(BF16)
            for v in range(2):
                at = (v, pl.ds(k0, 128), pl.ds(zp128, 128))
                s_buf[at] = s[:, v * 128 : v * 128 + 128]
                e_buf[at] = e[:, v * 128 : v * 128 + 128]
                k_buf[at] = k[:, v * 128 : v * 128 + 128]
            return carry

        lax.fori_loop(0, 8, block, 0)

    got(qg.at[1 - c, zl], gs_rsem.at[0])
    scores(zl)

    def member(i, step):
        zp = lax.rem(zl + step, NZL)
        piece = qg.at[c, zp]
        got(piece, g_rsem.at[i])
        remote(piece, piece, gs_ssem, gs_rsem.at[i + 1], sib).start()
        got(qg.at[1 - c, zp], gs_rsem.at[i + 1])
        scores(zp)

    member(1, 3)
    member(2, 1)
    got(r_px, r_rsem.at[0])
    part = r_src[...]
    for i in range(7):
        part = part + r_px[i]
    mine = r_mem.at[c, zl]
    r_mem[c, zl] = part
    for to in [sib] + near_ids + near_cross_ids:
        remote(mine, mine, r_ssem.at[1], r_rsem.at[1], to).start()
    member(0, 2)
    got(r_px, r_rsem.at[1])
    pairs = [[r_mem[i, j] for i in range(2)] for j in range(NZL)]

    def assemble(base):
        tiles = []
        for v in range(2):
            at = base + v * 64
            for j in range(NZL):
                tiles += [pairs[j][0][:, at : at + 64], pairs[j][1][:, at : at + 64]]
        return jnp.concatenate(tiles, axis=1)

    window_scale = PROTOS / assemble(0)
    totals = assemble(128)

    spec_row = jnp.concatenate([qg[0, i, pl.ds(128, 1)] + qg[1, i, pl.ds(128, 1)] for i in range(4)], axis=1)
    group = lax.broadcasted_iota(jnp.int32, (NGROUP, 512), 0)
    onehot = jnp.where(group == jnp.broadcast_to(spec_row, (NGROUP, 512)).astype(jnp.int32), 1.0, 0.0)

    def a_sum(it, between_1=None, between_2=None):
        remote(a_src.at[it, 0], a_c.at[it], a_ssem.at[it, 0], a_rsem.at[it, 0], sib).start()
        if between_1 is not None:
            between_1()
        got(a_c.at[it], a_rsem.at[it, 0])
        part = a_src[it, 0] + a_c[it]
        a_src[it, 1] = part
        for i, to in enumerate(plane_ids):
            remote(a_src.at[it, 1], a_pl.at[it, i], a_ssem.at[it, 1], a_rsem.at[it, 1], to).start()
        if between_2 is not None:
            between_2()
        got(a_pl.at[it], a_rsem.at[it, 1])
        for i in range(NP):
            part = part + a_pl[it, i]
        return part

    def b_sum(it, between=None):
        for i, to in enumerate(y_ids):
            remote(b_src.at[it], b_y.at[it, i], b_ssem.at[it], b_rsem.at[it], to).start()
        if between is not None:
            between()
        got(b_y.at[it], b_rsem.at[it])
        part = b_src[it]
        for i in range(7):
            part = part + b_y[it, i]
        return part

    def send_counts():
        cnt_src[...] = jnp.broadcast_to(jnp.sum(onehot, axis=1, keepdims=True), (NGROUP, 128))
        for i, to in enumerate(y_ids):
            remote(cnt_src, cnt_y.at[i], cnt_ssem, cnt_rsem, to).start()

    def halves(value, k0, width):
        hi = value.astype(BF16)
        two[pl.ds(k0, width)] = hi
        two[pl.ds(1024 + k0, width)] = (value - hi.astype(F32)).astype(BF16)

    def split_e(v):
        def block(kb, carry):
            k0 = pl.multiple_of(kb * 32, 32)
            halves(e_buf[v, pl.ds(k0, 32)], k0, 32)
            return carry

        lax.fori_loop(0, 32, block, 0)

    def split_t(v):
        for i in range(8):
            p = p_row[:, pl.ds(pl.multiple_of(v * 1024 + i * 128, 128), 128)]
            col = jnp.broadcast_to(p, (128, 128)).T
            t = k_buf[v, pl.ds(i * 128, 128)].astype(F32) * jnp.concatenate([col] * 4, axis=1)
            t_buf[v, pl.ds(i * 128, 128)] = t
            halves(t, i * 128, 128)

    def q_core(step):
        prepare = (split_e, split_t)[step]
        theirs = 1 - c if step == 0 else c
        prepare(theirs)
        c_src[step] = mm(keys_t[...], two[...])
        remote(c_src.at[step], c_rcv.at[step], f_ssem.at[step, 0], f_rsem.at[step, 0], sib).start()
        prepare(1 - theirs)
        x_src[step] = mm(keys_t[...], two[...])

    def q_x(step):
        got(c_rcv.at[step], f_rsem.at[step, 0])
        x_src[step] = x_src[step] + c_rcv[step]
        for i, xx in enumerate(x_of):
            piece = x_src.at[step, pl.ds(pl.multiple_of(xx * 32, 32), 32)]
            remote(piece, x_rcv.at[step, i], f_ssem.at[step, 1], f_rsem.at[step, 1], x_ids[i]).start()

    def q_z(step):
        got(x_rcv.at[step], f_rsem.at[step, 1])
        part = x_src[step, pl.ds(pl.multiple_of(x * 32, 32), 32)]
        for i in range(3):
            part = part + x_rcv[step, i]
        for i in range(4):
            w_src[step, i] = part[:, i * 128 : i * 128 + 128]
        for i, to in enumerate(z_ids):
            piece = w_src.at[step, lax.rem(z_of[i], NZL)]
            remote(piece, w_rcv.at[step, i], f_ssem.at[step, 2], f_rsem.at[step, 2], to).start()

    def q_end(step):
        got(w_rcv.at[step], f_rsem.at[step, 2])
        part = w_src[step, zl]
        for i in range(7):
            part = part + w_rcv[step, i]
        return part

    def columns(it, scale):
        for v in range(2):
            out = mm(split3(scale[:, v * 512 : v * 512 + 512]), k_buf[v], NT)
            b_src[it, :, pl.ds(v * 1024, 1024)] = jnp.sum(out, axis=0, keepdims=True)

    def row_sums(it, scale):
        for v in range(2):
            out = mm(split3(scale[:, v * 1024 : v * 1024 + 1024]), k_buf[v])
            a_src[it, 0, :, pl.ds(v * 512, 512)] = jnp.sum(out, axis=0, keepdims=True)

    def beside_a0():
        send_counts()
        q_core(0)

    columns(0, window_scale)
    proto_scale = 1.0 / (PROTOS * b_sum(0))
    row_sums(0, proto_scale)
    window_scale = 1.0 / a_sum(0, None, beside_a0)
    columns(1, window_scale)
    proto_scale = 1.0 / (PROTOS * b_sum(1, lambda: q_x(0)))
    row_sums(1, proto_scale)
    window_scale = 1.0 / a_sum(1)
    columns(2, window_scale)
    proto_scale = 1.0 / (PROTOS * b_sum(2, lambda: q_z(0)))
    row_sums(2, proto_scale)
    p_row[...] = proto_scale

    def cross():
        for v in range(2):

            def block(kb, acc):
                k0 = pl.multiple_of(kb * 32, 32)
                prod = t_buf[1 - v, pl.ds(k0, 32)] * s_buf[v, pl.ds(k0, 32)]
                return acc + jnp.sum(prod.reshape(4, 8, 512), axis=0)

            acc = lax.fori_loop(0, 32, block, jnp.zeros((8, 512), F32))
            x_rows[v] = jnp.sum(acc, axis=0, keepdims=True)

    def beside_a3():
        q_core(1)
        q_x(1)
        cross()

    last = 1.0 / a_sum(2, None, beside_a3)

    got(cnt_y, cnt_rsem)
    counts = cnt_src[...]
    for i in range(7):
        counts = counts + cnt_y[i]
    seen = jnp.sum(onehot * jnp.concatenate([counts] * 4, axis=1), axis=0, keepdims=True)
    weight = WINDOWS / (NGROUP * seen)
    last_v = [last[:, 0:512], last[:, 512:1024]]
    tot_v = [totals[:, 0:512], totals[:, 512:1024]]
    a_v = [5.0 * weight / tot_v[v] for v in range(2)]
    b_v = [5.0 * weight * last_v[1 - v] for v in range(2)]
    for v in range(2):
        ab_rows[0, v] = a_v[v]
        ab_rows[1, v] = b_v[v]
    terms = jnp.zeros((1, 512), F32)
    for v in range(2):
        terms = terms + 0.5 * weight * (jnp.log(tot_v[v]) / 64.0 - 10.0 * last_v[1 - v] * x_rows[v])
    terms = terms[:, 0:128] + terms[:, 128:256] + terms[:, 256:384] + terms[:, 384:512]
    me_xc = x * NC + c
    l_xc[me_xc] = terms
    for to in xc_ids:
        remote(l_xc.at[me_xc], l_xc.at[me_xc], l_ssem.at[0], l_rsem.at[0], to).start()

    def add_slots(ref):
        out = ref[0]
        for i in range(1, 8):
            out = out + ref[i]
        return out

    def key_part(slot, yy):
        k0 = pl.multiple_of(yy * 128, 128)
        part = jnp.zeros((128, FEAT), F32)
        for v in range(2):
            at = (pl.ds(k0, 128), slice(None))
            g = (e_buf[(v,) + at] * a_v[v] - t_buf[(1 - v,) + at] * b_v[v]).astype(BF16)
            part = part + mm(g, q16[v])
        kg_src[slot] = part

    ahead = lambda j: lax.rem(y + j, NY)
    up1, up2, down1, down2 = (dev(y=ahead(j)) for j in (1, 2, 7, 6))
    key_part(4, ahead(4))
    remote(kg_src.at[4, pl.ds(0, 64)], kg_half.at[0], kg_ssem.at[0], kg_rsem.at[0], up2).start()
    remote(kg_src.at[4, pl.ds(64, 64)], kg_half.at[1], kg_ssem.at[1], kg_rsem.at[1], down2).start()
    key_part(3, ahead(3))
    remote(kg_src.at[3], kg_fwd.at[0], kg_ssem.at[2], kg_rsem.at[2], up1).start()
    key_part(5, ahead(5))
    remote(kg_src.at[5], kg_fwd.at[1], kg_ssem.at[3], kg_rsem.at[3], down1).start()
    key_part(2, ahead(2))
    key_part(6, ahead(6))
    key_part(1, ahead(1))
    remote(kg_src.at[1], kg_y.at[0], kg_ssem.at[4], kg_rsem.at[4], up1).start()
    key_part(7, ahead(7))
    remote(kg_src.at[7], kg_y.at[1], kg_ssem.at[5], kg_rsem.at[5], down1).start()
    key_part(0, y)

    q_z(1)
    got(kg_fwd.at[0], kg_rsem.at[2])
    got(kg_half.at[0], kg_rsem.at[0])
    kg_src[2, pl.ds(0, 64)] = kg_src[2, pl.ds(0, 64)] + kg_fwd[0, pl.ds(0, 64)] + kg_half[0]
    kg_src[2, pl.ds(64, 64)] = kg_src[2, pl.ds(64, 64)] + kg_fwd[0, pl.ds(64, 64)]
    remote(kg_src.at[2], kg_y.at[2], kg_ssem.at[6], kg_rsem.at[6], up2).start()
    got(kg_fwd.at[1], kg_rsem.at[3])
    got(kg_half.at[1], kg_rsem.at[1])
    kg_src[6, pl.ds(0, 64)] = kg_src[6, pl.ds(0, 64)] + kg_fwd[1, pl.ds(0, 64)]
    kg_src[6, pl.ds(64, 64)] = kg_src[6, pl.ds(64, 64)] + kg_fwd[1, pl.ds(64, 64)] + kg_half[1]
    remote(kg_src.at[6], kg_y.at[3], kg_ssem.at[7], kg_rsem.at[7], down2).start()

    got(l_xc.at[pl.ds(0, 7)], l_rsem.at[0])
    l_z[z] = add_slots(l_xc)
    for to in z_ids:
        remote(l_z.at[z], l_z.at[z], l_ssem.at[1], l_rsem.at[1], to).start()

    at = pl.ds(pl.multiple_of(zl * 128, 128), 128)
    part = ab_rows[0, c, :, at] * q_end(0) - ab_rows[1, c, :, at] * q_end(1)
    mine = fin.at[c, pl.ds(pl.multiple_of(x * 32, 32), 32)]
    fin[c, pl.ds(pl.multiple_of(x * 32, 32), 32)] = part
    for to in xc_ids:
        remote(mine, mine, fin_ssem, fin_rsem, to).start()
    got(l_z.at[pl.ds(0, 7)], l_rsem.at[1])
    l_y[y] = add_slots(l_z)
    for to in y_ids:
        remote(l_y.at[y], l_y.at[y], l_ssem.at[2], l_rsem.at[2], to).start()

    part = kg_src[0]
    for i, k in ((0, 4), (1, 5), (2, 6), (3, 7)):
        got(kg_y.at[i], kg_rsem.at[k])
        part = part + kg_y[i]
    own = pl.multiple_of((y * 8 + zl * NC + c) * 128, 128)
    pgrad_ref[...] = unit_back(kraw[pl.ds(own, 128)].astype(F32), part)

    got(w_rcv.at[0], fin_rsem)
    for v in range(2):
        qt[v] = fin[v].T
    for v in range(2):
        grad = qt[v, pl.ds(pl.multiple_of(c * 64, 64), 64)]
        view_ref[v] = unit_back(pooled[pl.ds(v * 64, 64)], grad)

    got(l_y.at[pl.ds(0, 7)], l_rsem.at[2])
    loss_ref[...] = jnp.sum(add_slots(l_y), axis=1, keepdims=True) * (1.0 / WINDOWS)

    sent(qg.at[0, pl.ds(0, 3)], g_ssem)
    sent(qg.at[0], gs_ssem)
    for it in range(3):
        sent(a_c.at[it], a_ssem.at[it, 0])
        sent(a_pl.at[it], a_ssem.at[it, 1])
    for it in range(3):
        sent(b_y.at[it], b_ssem.at[it])
    sent(r_px, r_ssem.at[0])
    sent(r_px, r_ssem.at[1])
    sent(cnt_y, cnt_ssem)
    for i in range(2):
        sent(kg_half.at[i], kg_ssem.at[i])
        sent(kg_fwd.at[i], kg_ssem.at[2 + i])
        sent(kg_y.at[i], kg_ssem.at[4 + i])
        sent(kg_y.at[2 + i], kg_ssem.at[6 + i])
        sent(c_rcv.at[i], f_ssem.at[i, 0])
        sent(x_rcv.at[i], f_ssem.at[i, 1])
        sent(w_rcv.at[i], f_ssem.at[i, 2])
    sent(w_rcv.at[0], fin_ssem)
    for i in range(3):
        sent(l_xc.at[pl.ds(0, 7)], l_ssem.at[i])


def hand_on(view_in, pgrad_in, loss_in, view_ref, pgrad_ref, loss_ref, sem):
    pairs = ((view_in, view_ref), (pgrad_in, pgrad_ref), (loss_in, loss_ref))
    copies = [pltpu.make_async_copy(src, dst, sem.at[i]) for i, (src, dst) in enumerate(pairs)]
    for copy in copies:
        copy.start()
    for copy in copies:
        copy.wait()


def on_device(tokens, offsets, species, prototypes):
    vmem = pltpu.VMEM
    dma = pltpu.SemaphoreType.DMA
    anywhere = pl.BlockSpec(memory_space=pl.ANY)
    inside = pl.BlockSpec(memory_space=pltpu.VMEM)
    scratch = [
        vmem((64 * SEQ, FEAT), BF16),
        vmem((128, 64 * SEQ), BF16),
        vmem((8192, FEAT), BF16),
        vmem((8192, FEAT), BF16),
        vmem((1024, FEAT), BF16),
        vmem((FEAT, 2048), BF16),
        vmem((128, FEAT), F32),
        vmem((2, 4, 136, FEAT), F32),
        vmem((2, 512, FEAT), BF16),
        vmem((2, 1024, 512), F32),
        vmem((2, 1024, 512), F32),
        vmem((2, 1024, 512), BF16),
        vmem((2, 1024, 512), F32),
        vmem((2048, 512), BF16),
        vmem((3, 2, 1, 1024), F32),
        vmem((3, 1, 1024), F32),
        vmem((3, NP, 1, 1024), F32),
        vmem((3, 1, 2048), F32),
        vmem((3, 7, 1, 2048), F32),
        vmem((1, 256), F32),
        vmem((7, 1, 256), F32),
        vmem((2, 4, 1, 256), F32),
        vmem((NGROUP, 128), F32),
        vmem((7, NGROUP, 128), F32),
        vmem((8, 128, FEAT), F32),
        vmem((2, 64, FEAT), F32),
        vmem((2, 128, FEAT), F32),
        vmem((4, 128, FEAT), F32),
        vmem((2, FEAT, 512), F32),
        vmem((2, FEAT, 512), F32),
        vmem((2, FEAT, 512), F32),
        vmem((2, 3, 32, 512), F32),
        vmem((2, 4, 32, 128), F32),
        vmem((2, 7, 32, 128), F32),
        vmem((2, FEAT, 128), F32),
        vmem((8, 1, 128), F32),
        vmem((8, 1, 128), F32),
        vmem((8, 1, 128), F32),
        vmem((2, 1, 512), F32),
        vmem((1, 2048), F32),
        vmem((2, 2, 1, 512), F32),
        vmem((2, 128, FEAT), F32),
        dma((2,)),
        dma, dma((3,)), dma, dma((4,)),
        dma((3, 2)), dma((3, 2)), dma((3,)), dma((3,)), dma((2,)), dma((2,)), dma, dma,
        dma((8,)), dma((8,)), dma((2, 3)), dma((2, 3)), dma, dma, dma((3,)), dma((3,)),
    ]
    view_grads, proto_grads, loss = pl.pallas_call(
        kernel,
        out_shape=(
            jax.ShapeDtypeStruct((2, 64, FEAT), F32),
            jax.ShapeDtypeStruct((128, FEAT), F32),
            jax.ShapeDtypeStruct((1, 1), F32),
        ),
        in_specs=[anywhere, inside, inside, anywhere],
        out_specs=(inside, inside, inside),
        scratch_shapes=scratch,
        compiler_params=pltpu.CompilerParams(
            collective_id=0, has_side_effects=True, vmem_limit_bytes=56 * 2**20
        ),
        name="swav_step",
    )(
        tokens.reshape(64 * SEQ, FEAT),
        offsets,
        species.reshape(1, 64),
        prototypes,
    )
    view_grads, proto_grads, loss = pl.pallas_call(
        hand_on,
        out_shape=(
            jax.ShapeDtypeStruct((2, 64, FEAT), F32),
            jax.ShapeDtypeStruct((128, FEAT), F32),
            jax.ShapeDtypeStruct((1, 1), F32),
        ),
        in_specs=[anywhere] * 3,
        out_specs=(anywhere, anywhere, anywhere),
        scratch_shapes=[dma((3,))],
        compiler_params=pltpu.CompilerParams(vmem_limit_bytes=60 * 2**20),
        name="results",
    )(view_grads, proto_grads, loss)
    return view_grads, proto_grads, loss.reshape(())


def solution(mesh):
    return jax.shard_map(
        on_device,
        mesh=mesh,
        in_specs=(P("dp", None, None), P(None, "dp"), P("dp"), P("proto", None)),
        out_specs=(P(None, "dp", None), P(("proto", "dp"), None), P()),
        check_vma=False,
    )
```

```python
import math

import jax
import jax.numpy as jnp
from jax import lax
from jax.experimental import pallas as pl
from jax.experimental.pallas import tpu as pltpu
from jax.sharding import PartitionSpec as P

MESH = pl.DeviceIdType.MESH
F32 = jnp.float32
BF16 = jnp.bfloat16
NGROUP = 16
CROP = 24
SEQ = 32
FEAT = 128
WINDOWS = 4096
PROTOS = 65536
EPS = 1e-6
NY, NZL, NC, NZH, NX = 8, 4, 2, 2, 4
NZ = NZH * NZL
RING8 = (4, 3, 5, 2, 6, 1, 7)
XC = ((2, 0), (2, 1), (1, 0), (3, 0), (1, 1), (3, 1), (0, 1))
RING4 = (2, 1, 3)
PLANE = tuple(
    sorted(
        ((dx, dz) for dx in range(NX) for dz in range(NZ) if dx or dz),
        key=lambda o: -(min(o[0], NX - o[0]) + min(o[1], NZ - o[1])),
    )
)
NP = len(PLANE)
NT = (((1,), (1,)), ((), ()))
NN = (((1,), (0,)), ((), ()))


def mm(a, b, dims=NN):
    return lax.dot_general(a, b, dims, preferred_element_type=F32)


def split3(row, count=16):
    hi = row.astype(BF16).astype(F32)
    rest = row - hi
    mid = rest.astype(BF16).astype(F32)
    lo = rest - mid
    width = row.shape[1]
    at = lax.broadcasted_iota(jnp.int32, (count, width), 0)
    full = lambda r: jnp.broadcast_to(r, (count, width))
    out = jnp.where(at == 0, full(hi), jnp.where(at == 1, full(mid), jnp.where(at == 2, full(lo), 0.0)))
    return out.astype(BF16)


def unit_scale(rows):
    return lax.rsqrt(jnp.mean(rows * rows, axis=-1, keepdims=True) + EPS)


def unit_back(rows, grad):
    scale = unit_scale(rows)
    along = jnp.mean(rows * grad, axis=-1, keepdims=True)
    return (grad - rows * (along * scale * scale)) * (scale / math.sqrt(FEAT))


def kernel(
    tok_ref, off_ref, spec_ref, proto_ref,
    view_ref, pgrad_ref, loss_ref,
    tok, mask, kraw, kunit, keys, keys_t, pooled, qg, q16, s_buf, e_buf, k_buf, t_buf, two,
    a_src, a_c, a_pl, b_src, b_y, r_src, r_px, r_mem, cnt_src, cnt_y,
    kg_src, kg_half, kg_fwd, kg_y, c_src, c_rcv, x_src, x_rcv, w_src, w_rcv, fin, l_xc, l_z, l_y,
    x_rows, p_row, ab_rows, qt,
    load_sem, g_ssem, g_rsem, gs_ssem, gs_rsem,
    a_ssem, a_rsem, b_ssem, b_rsem, r_ssem, r_rsem, cnt_ssem, cnt_rsem,
    kg_ssem, kg_rsem, f_ssem, f_rsem, fin_ssem, fin_rsem, l_ssem, l_rsem,
):
    dp = lax.axis_index("dp")
    pr = lax.axis_index("proto")
    y, zl, c = lax.div(dp, 8), lax.rem(lax.div(dp, 2), 4), lax.rem(dp, 2)
    zh, x = lax.div(pr, 4), lax.rem(pr, 4)
    z = zh * NZL + zl

    def dev(y=y, z=z, c=c, x=x):
        return ((y * NZL + lax.rem(z, NZL)) * NC + c, lax.div(z, NZL) * NX + x)

    xc_ids = [dev(x=lax.rem(x + dx, NX), c=lax.rem(c + dc, NC)) for dx, dc in XC]
    z_of = [lax.rem(z + j, NZ) for j in RING8]
    z_ids = [dev(z=k) for k in z_of]
    y_of = [lax.rem(y + j, NY) for j in RING8]
    y_ids = [dev(y=k) for k in y_of]
    x_of = [lax.rem(x + j, NX) for j in RING4]
    x_ids = [dev(x=k) for k in x_of]
    sib = dev(c=1 - c)
    plane_ids = [dev(x=lax.rem(x + dx, NX), z=lax.rem(z + dz, NZ)) for dx, dz in PLANE]
    px_ids = [plane_ids[i] for i in range(NP) if PLANE[i][1] % NZL == 0]
    step2 = 2 + 4 * c
    near = [lax.rem(z + step, NZ) for step in (step2, 1, 7)]
    near_ids = [dev(z=k) for k in near]
    near_cross_ids = [dev(z=k, c=1 - c) for k in near]
    far_cross_ids = near_cross_ids + [dev(z=lax.rem(z + 8 - step2, NZ), c=1 - c)]
    cross_ids = [xc_ids[i] for i in range(7) if XC[i][0] and XC[i][1]]

    def remote(src, dst, ssem, rsem, to):
        return pltpu.make_async_remote_copy(
            src_ref=src, dst_ref=dst, send_sem=ssem, recv_sem=rsem, device_id=to, device_id_type=MESH
        )

    def got(ref, sem):
        remote(ref, ref, sem, sem, sib).wait_recv()

    def sent(ref, sem):
        remote(ref, ref, sem, sem, sib).wait_send()

    barrier = pltpu.get_barrier_semaphore()
    load_tok = pltpu.make_async_copy(tok_ref, tok, load_sem.at[0])
    load_key = pltpu.make_async_copy(proto_ref, kraw, load_sem.at[1])
    load_tok.start()
    load_key.start()
    for to in [sib] + plane_ids + cross_ids + far_cross_ids + y_ids:
        pl.semaphore_signal(barrier, inc=1, device_id=to, device_id_type=MESH)

    off = off_ref[...].astype(F32)
    off_row = jnp.concatenate([off[0:1], off[1:2]], axis=1)
    lane = lax.broadcasted_iota(jnp.int32, (128, 128), 1)
    first = jnp.broadcast_to(off_row, (128, 128)).T.astype(jnp.int32)
    row = lax.broadcasted_iota(jnp.int32, (128, 128), 0)
    first = first + (row & 63) * SEQ
    for part in range(16):
        col = part * 128
        inside = (lane + col >= first) & (lane + col < first + CROP)
        mask[:, pl.ds(col, 128)] = jnp.where(inside, 1.0, 0.0).astype(BF16)
    load_tok.wait()
    total = mm(mask[...], tok[...])
    rows = total / CROP
    pooled[...] = rows
    query = (rows * unit_scale(rows) / math.sqrt(FEAT)).astype(BF16)
    qg[c, zl, pl.ds(0, 128)] = query.astype(F32)
    spec = spec_ref[...].astype(F32)
    both = jnp.concatenate([spec, spec], axis=1)
    half = lax.broadcasted_iota(jnp.int32, (8, 128), 1) // 64
    qg[c, zl, pl.ds(128, 8)] = jnp.where(half == c, jnp.broadcast_to(both, (8, 128)), 0.0)

    load_key.wait()

    def normalise(i, carry):
        at = pl.ds(pl.multiple_of(i * 2048, 2048), 2048)
        raw = kraw[at].astype(F32)
        kunit[at] = (raw * (unit_scale(raw) * (1.0 / math.sqrt(FEAT)))).astype(BF16)
        return carry

    lax.fori_loop(0, 4, normalise, 0)
    pl.semaphore_wait(barrier, 15 + NP)

    mine = qg.at[c, zl]
    for i, to in enumerate(near_ids):
        remote(mine, mine, g_ssem, g_rsem.at[i], to).start()
    remote(mine, mine, gs_ssem, gs_rsem.at[0], sib).start()

    def whole(i, sums):
        at = pl.ds(pl.multiple_of(i * 4096, 4096), 4096)
        e = jnp.exp(mm(kunit[at], query, NT) * 10.0)
        k = (e * e).astype(BF16).astype(F32)
        fold = lambda a: jnp.sum(a.reshape(512, 8, 128), axis=0)
        return sums[0] + fold(k), sums[1] + fold(e)

    zero = jnp.zeros((8, 128), F32)
    ks, es = lax.fori_loop(0, 2, whole, (zero, zero))
    r_src[:, pl.ds(0, 128)] = jnp.sum(ks, axis=0, keepdims=True)
    r_src[:, pl.ds(128, 128)] = jnp.sum(es, axis=0, keepdims=True)
    for i, to in enumerate(px_ids):
        remote(r_src, r_px.at[i], r_ssem.at[0], r_rsem.at[0], to).start()

    for i in range(8):
        block = kunit[pl.ds(pl.multiple_of((i * 8 + zl * NC + c) * 128, 128), 128)]
        keys[pl.ds(i * 128, 128)] = block
        turned = block.astype(F32).T.astype(BF16)
        keys_t[:, pl.ds(i * 128, 128)] = turned
        keys_t[:, pl.ds(1024 + i * 128, 128)] = turned

    def scores(zp):
        zp128 = pl.multiple_of(zp * 128, 128)
        pair = []
        for v in range(2):
            q = jnp.concatenate([qg[0, zp, pl.ds(v * 64, 64)], qg[1, zp, pl.ds(v * 64, 64)]], axis=0).astype(BF16)
            q16[v, pl.ds(zp128, 128)] = q
            pair.append(q)
        rhs = jnp.concatenate(pair, axis=0)

        out = mm(keys[...], rhs, NT)
        e = jnp.exp(out * 10.0)
        k = (e * e).astype(BF16)
        for v in range(2):
            at = (v, slice(None), pl.ds(zp128, 128))
            s_buf[at] = out[:, v * 128 : v * 128 + 128]
            e_buf[at] = e[:, v * 128 : v * 128 + 128]
            k_buf[at] = k[:, v * 128 : v * 128 + 128]

    got(qg.at[1 - c, zl], gs_rsem.at[0])
    scores(zl)

    def member(i, step):
        zp = lax.rem(zl + step, NZL)
        piece = qg.at[c, zp]
        got(piece, g_rsem.at[i])
        remote(piece, piece, gs_ssem, gs_rsem.at[i + 1], sib).start()
        got(qg.at[1 - c, zp], gs_rsem.at[i + 1])
        scores(zp)

    member(1, 3)
    member(2, 1)
    got(r_px, r_rsem.at[0])
    part = r_src[...]
    for i in range(7):
        part = part + r_px[i]
    mine = r_mem.at[c, zl]
    r_mem[c, zl] = part
    for to in [sib] + near_ids + near_cross_ids:
        remote(mine, mine, r_ssem.at[1], r_rsem.at[1], to).start()
    member(0, 2)
    got(r_px, r_rsem.at[1])
    pairs = [[r_mem[i, j] for i in range(2)] for j in range(NZL)]

    def assemble(base):
        tiles = []
        for v in range(2):
            at = base + v * 64
            for j in range(NZL):
                tiles += [pairs[j][0][:, at : at + 64], pairs[j][1][:, at : at + 64]]
        return jnp.concatenate(tiles, axis=1)

    window_scale = PROTOS / assemble(0)
    totals = assemble(128)

    spec_row = jnp.concatenate([qg[0, i, pl.ds(128, 1)] + qg[1, i, pl.ds(128, 1)] for i in range(4)], axis=1)
    group = lax.broadcasted_iota(jnp.int32, (NGROUP, 512), 0)
    onehot = jnp.where(group == jnp.broadcast_to(spec_row, (NGROUP, 512)).astype(jnp.int32), 1.0, 0.0)

    def a_sum(it, between_1=None, between_2=None):
        remote(a_src.at[it, 0], a_c.at[it], a_ssem.at[it, 0], a_rsem.at[it, 0], sib).start()
        if between_1 is not None:
            between_1()
        got(a_c.at[it], a_rsem.at[it, 0])
        part = a_src[it, 0] + a_c[it]
        a_src[it, 1] = part
        for i, to in enumerate(plane_ids):
            remote(a_src.at[it, 1], a_pl.at[it, i], a_ssem.at[it, 1], a_rsem.at[it, 1], to).start()
        if between_2 is not None:
            between_2()
        got(a_pl.at[it], a_rsem.at[it, 1])
        for i in range(NP):
            part = part + a_pl[it, i]
        return part

    def b_sum(it, between=None):
        for i, to in enumerate(y_ids):
            remote(b_src.at[it], b_y.at[it, i], b_ssem.at[it], b_rsem.at[it], to).start()
        if between is not None:
            between()
        got(b_y.at[it], b_rsem.at[it])
        part = b_src[it]
        for i in range(7):
            part = part + b_y[it, i]
        return part

    def send_counts():
        cnt_src[...] = jnp.broadcast_to(jnp.sum(onehot, axis=1, keepdims=True), (NGROUP, 128))
        for i, to in enumerate(y_ids):
            remote(cnt_src, cnt_y.at[i], cnt_ssem, cnt_rsem, to).start()

    def halves(value, k0, width):
        hi = value.astype(BF16)
        two[pl.ds(k0, width)] = hi
        two[pl.ds(1024 + k0, width)] = (value - hi.astype(F32)).astype(BF16)

    def split_e(v):
        def block(kb, carry):
            k0 = pl.multiple_of(kb * 32, 32)
            halves(e_buf[v, pl.ds(k0, 32)], k0, 32)
            return carry

        lax.fori_loop(0, 32, block, 0)

    def split_t(v):
        for i in range(8):
            p = p_row[:, pl.ds(pl.multiple_of(v * 1024 + i * 128, 128), 128)]
            col = jnp.broadcast_to(p, (128, 128)).T
            t = k_buf[v, pl.ds(i * 128, 128)].astype(F32) * jnp.concatenate([col] * 4, axis=1)
            t_buf[v, pl.ds(i * 128, 128)] = t
            halves(t, i * 128, 128)

    def q_core(step):
        prepare = (split_e, split_t)[step]
        theirs = 1 - c if step == 0 else c
        prepare(theirs)
        c_src[step] = mm(keys_t[...], two[...])
        remote(c_src.at[step], c_rcv.at[step], f_ssem.at[step, 0], f_rsem.at[step, 0], sib).start()
        prepare(1 - theirs)
        x_src[step] = mm(keys_t[...], two[...])

    def q_x(step):
        got(c_rcv.at[step], f_rsem.at[step, 0])
        x_src[step] = x_src[step] + c_rcv[step]
        for i, xx in enumerate(x_of):
            piece = x_src.at[step, pl.ds(pl.multiple_of(xx * 32, 32), 32)]
            remote(piece, x_rcv.at[step, i], f_ssem.at[step, 1], f_rsem.at[step, 1], x_ids[i]).start()

    def q_z(step):
        got(x_rcv.at[step], f_rsem.at[step, 1])
        part = x_src[step, pl.ds(pl.multiple_of(x * 32, 32), 32)]
        for i in range(3):
            part = part + x_rcv[step, i]
        for i in range(4):
            w_src[step, i] = part[:, i * 128 : i * 128 + 128]
        for i, to in enumerate(z_ids):
            piece = w_src.at[step, lax.rem(z_of[i], NZL)]
            remote(piece, w_rcv.at[step, i], f_ssem.at[step, 2], f_rsem.at[step, 2], to).start()

    def q_end(step):
        got(w_rcv.at[step], f_rsem.at[step, 2])
        part = w_src[step, zl]
        for i in range(7):
            part = part + w_rcv[step, i]
        return part

    def columns(it, scale):
        for v in range(2):
            out = mm(split3(scale[:, v * 512 : v * 512 + 512]), k_buf[v], NT)
            b_src[it, :, pl.ds(v * 1024, 1024)] = jnp.sum(out, axis=0, keepdims=True)

    def row_sums(it, scale):
        for v in range(2):
            out = mm(split3(scale[:, v * 1024 : v * 1024 + 1024]), k_buf[v])
            a_src[it, 0, :, pl.ds(v * 512, 512)] = jnp.sum(out, axis=0, keepdims=True)

    def beside_a0():
        send_counts()
        q_core(0)

    columns(0, window_scale)
    proto_scale = 1.0 / (PROTOS * b_sum(0))
    row_sums(0, proto_scale)
    window_scale = 1.0 / a_sum(0, None, beside_a0)
    columns(1, window_scale)
    proto_scale = 1.0 / (PROTOS * b_sum(1, lambda: q_x(0)))
    row_sums(1, proto_scale)
    window_scale = 1.0 / a_sum(1)
    columns(2, window_scale)
    proto_scale = 1.0 / (PROTOS * b_sum(2, lambda: q_z(0)))
    row_sums(2, proto_scale)
    p_row[...] = proto_scale

    def cross():
        for v in range(2):

            def block(kb, acc):
                k0 = pl.multiple_of(kb * 32, 32)
                prod = t_buf[1 - v, pl.ds(k0, 32)] * s_buf[v, pl.ds(k0, 32)]
                return acc + jnp.sum(prod.reshape(4, 8, 512), axis=0)

            acc = lax.fori_loop(0, 32, block, jnp.zeros((8, 512), F32))
            x_rows[v] = jnp.sum(acc, axis=0, keepdims=True)

    def beside_a3():
        q_core(1)
        q_x(1)
        cross()

    last = 1.0 / a_sum(2, None, beside_a3)

    got(cnt_y, cnt_rsem)
    counts = cnt_src[...]
    for i in range(7):
        counts = counts + cnt_y[i]
    seen = jnp.sum(onehot * jnp.concatenate([counts] * 4, axis=1), axis=0, keepdims=True)
    weight = WINDOWS / (NGROUP * seen)
    last_v = [last[:, 0:512], last[:, 512:1024]]
    tot_v = [totals[:, 0:512], totals[:, 512:1024]]
    a_v = [5.0 * weight / tot_v[v] for v in range(2)]
    b_v = [5.0 * weight * last_v[1 - v] for v in range(2)]
    for v in range(2):
        ab_rows[0, v] = a_v[v]
        ab_rows[1, v] = b_v[v]
    terms = jnp.zeros((1, 512), F32)
    for v in range(2):
        terms = terms + 0.5 * weight * (jnp.log(tot_v[v]) / 64.0 - 10.0 * last_v[1 - v] * x_rows[v])
    terms = terms[:, 0:128] + terms[:, 128:256] + terms[:, 256:384] + terms[:, 384:512]
    me_xc = x * NC + c
    l_xc[me_xc] = terms
    for to in xc_ids:
        remote(l_xc.at[me_xc], l_xc.at[me_xc], l_ssem.at[0], l_rsem.at[0], to).start()

    def add_slots(ref):
        out = ref[0]
        for i in range(1, 8):
            out = out + ref[i]
        return out

    def key_part(slot, yy):
        k0 = pl.multiple_of(yy * 128, 128)
        part = jnp.zeros((128, FEAT), F32)
        for v in range(2):
            at = (pl.ds(k0, 128), slice(None))
            g = (e_buf[(v,) + at] * a_v[v] - t_buf[(1 - v,) + at] * b_v[v]).astype(BF16)
            part = part + mm(g, q16[v])
        kg_src[slot] = part

    ahead = lambda j: lax.rem(y + j, NY)
    up1, up2, down1, down2 = (dev(y=ahead(j)) for j in (1, 2, 7, 6))
    key_part(4, ahead(4))
    remote(kg_src.at[4, pl.ds(0, 64)], kg_half.at[0], kg_ssem.at[0], kg_rsem.at[0], up2).start()
    remote(kg_src.at[4, pl.ds(64, 64)], kg_half.at[1], kg_ssem.at[1], kg_rsem.at[1], down2).start()
    key_part(3, ahead(3))
    remote(kg_src.at[3], kg_fwd.at[0], kg_ssem.at[2], kg_rsem.at[2], up1).start()
    key_part(5, ahead(5))
    remote(kg_src.at[5], kg_fwd.at[1], kg_ssem.at[3], kg_rsem.at[3], down1).start()
    key_part(2, ahead(2))
    key_part(6, ahead(6))
    key_part(1, ahead(1))
    remote(kg_src.at[1], kg_y.at[0], kg_ssem.at[4], kg_rsem.at[4], up1).start()
    key_part(7, ahead(7))
    remote(kg_src.at[7], kg_y.at[1], kg_ssem.at[5], kg_rsem.at[5], down1).start()
    key_part(0, y)

    q_z(1)
    got(kg_fwd.at[0], kg_rsem.at[2])
    got(kg_half.at[0], kg_rsem.at[0])
    kg_src[2, pl.ds(0, 64)] = kg_src[2, pl.ds(0, 64)] + kg_fwd[0, pl.ds(0, 64)] + kg_half[0]
    kg_src[2, pl.ds(64, 64)] = kg_src[2, pl.ds(64, 64)] + kg_fwd[0, pl.ds(64, 64)]
    remote(kg_src.at[2], kg_y.at[2], kg_ssem.at[6], kg_rsem.at[6], up2).start()
    got(kg_fwd.at[1], kg_rsem.at[3])
    got(kg_half.at[1], kg_rsem.at[1])
    kg_src[6, pl.ds(0, 64)] = kg_src[6, pl.ds(0, 64)] + kg_fwd[1, pl.ds(0, 64)]
    kg_src[6, pl.ds(64, 64)] = kg_src[6, pl.ds(64, 64)] + kg_fwd[1, pl.ds(64, 64)] + kg_half[1]
    remote(kg_src.at[6], kg_y.at[3], kg_ssem.at[7], kg_rsem.at[7], down2).start()

    got(l_xc.at[pl.ds(0, 7)], l_rsem.at[0])
    l_z[z] = add_slots(l_xc)
    for to in z_ids:
        remote(l_z.at[z], l_z.at[z], l_ssem.at[1], l_rsem.at[1], to).start()

    at = pl.ds(pl.multiple_of(zl * 128, 128), 128)
    part = ab_rows[0, c, :, at] * q_end(0) - ab_rows[1, c, :, at] * q_end(1)
    mine = fin.at[c, pl.ds(pl.multiple_of(x * 32, 32), 32)]
    fin[c, pl.ds(pl.multiple_of(x * 32, 32), 32)] = part
    for to in xc_ids:
        remote(mine, mine, fin_ssem, fin_rsem, to).start()
    got(l_z.at[pl.ds(0, 7)], l_rsem.at[1])
    l_y[y] = add_slots(l_z)
    for to in y_ids:
        remote(l_y.at[y], l_y.at[y], l_ssem.at[2], l_rsem.at[2], to).start()

    part = kg_src[0]
    for i, k in ((0, 4), (1, 5), (2, 6), (3, 7)):
        got(kg_y.at[i], kg_rsem.at[k])
        part = part + kg_y[i]
    own = pl.multiple_of((y * 8 + zl * NC + c) * 128, 128)
    pgrad_ref[...] = unit_back(kraw[pl.ds(own, 128)].astype(F32), part)

    got(w_rcv.at[0], fin_rsem)
    for v in range(2):
        qt[v] = fin[v].T
    for v in range(2):
        grad = qt[v, pl.ds(pl.multiple_of(c * 64, 64), 64)]
        view_ref[v] = unit_back(pooled[pl.ds(v * 64, 64)], grad)

    got(l_y.at[pl.ds(0, 7)], l_rsem.at[2])
    loss_ref[...] = jnp.sum(add_slots(l_y), axis=1, keepdims=True) * (1.0 / WINDOWS)

    sent(qg.at[0, pl.ds(0, 3)], g_ssem)
    sent(qg.at[0], gs_ssem)
    for it in range(3):
        sent(a_c.at[it], a_ssem.at[it, 0])
        sent(a_pl.at[it], a_ssem.at[it, 1])
    for it in range(3):
        sent(b_y.at[it], b_ssem.at[it])
    sent(r_px, r_ssem.at[0])
    sent(r_px, r_ssem.at[1])
    sent(cnt_y, cnt_ssem)
    for i in range(2):
        sent(kg_half.at[i], kg_ssem.at[i])
        sent(kg_fwd.at[i], kg_ssem.at[2 + i])
        sent(kg_y.at[i], kg_ssem.at[4 + i])
        sent(kg_y.at[2 + i], kg_ssem.at[6 + i])
        sent(c_rcv.at[i], f_ssem.at[i, 0])
        sent(x_rcv.at[i], f_ssem.at[i, 1])
        sent(w_rcv.at[i], f_ssem.at[i, 2])
    sent(w_rcv.at[0], fin_ssem)
    for i in range(3):
        sent(l_xc.at[pl.ds(0, 7)], l_ssem.at[i])


def hand_on(view_in, pgrad_in, loss_in, view_ref, pgrad_ref, loss_ref):
    view_ref[...] = view_in[...]
    pgrad_ref[...] = pgrad_in[...]
    loss_ref[...] = loss_in[...]


def on_device(tokens, offsets, species, prototypes):
    vmem = pltpu.VMEM
    dma = pltpu.SemaphoreType.DMA
    anywhere = pl.BlockSpec(memory_space=pl.ANY)
    inside = pl.BlockSpec(memory_space=pltpu.VMEM)
    scratch = [
        vmem((64 * SEQ, FEAT), BF16),
        vmem((128, 64 * SEQ), BF16),
        vmem((8192, FEAT), BF16),
        vmem((8192, FEAT), BF16),
        vmem((1024, FEAT), BF16),
        vmem((FEAT, 2048), BF16),
        vmem((128, FEAT), F32),
        vmem((2, 4, 136, FEAT), F32),
        vmem((2, 512, FEAT), BF16),
        vmem((2, 1024, 512), F32),
        vmem((2, 1024, 512), F32),
        vmem((2, 1024, 512), BF16),
        vmem((2, 1024, 512), F32),
        vmem((2048, 512), BF16),
        vmem((3, 2, 1, 1024), F32),
        vmem((3, 1, 1024), F32),
        vmem((3, NP, 1, 1024), F32),
        vmem((3, 1, 2048), F32),
        vmem((3, 7, 1, 2048), F32),
        vmem((1, 256), F32),
        vmem((7, 1, 256), F32),
        vmem((2, 4, 1, 256), F32),
        vmem((NGROUP, 128), F32),
        vmem((7, NGROUP, 128), F32),
        vmem((8, 128, FEAT), F32),
        vmem((2, 64, FEAT), F32),
        vmem((2, 128, FEAT), F32),
        vmem((4, 128, FEAT), F32),
        vmem((2, FEAT, 512), F32),
        vmem((2, FEAT, 512), F32),
        vmem((2, FEAT, 512), F32),
        vmem((2, 3, 32, 512), F32),
        vmem((2, 4, 32, 128), F32),
        vmem((2, 7, 32, 128), F32),
        vmem((2, FEAT, 128), F32),
        vmem((8, 1, 128), F32),
        vmem((8, 1, 128), F32),
        vmem((8, 1, 128), F32),
        vmem((2, 1, 512), F32),
        vmem((1, 2048), F32),
        vmem((2, 2, 1, 512), F32),
        vmem((2, 128, FEAT), F32),
        dma((2,)),
        dma, dma((3,)), dma, dma((4,)),
        dma((3, 2)), dma((3, 2)), dma((3,)), dma((3,)), dma((2,)), dma((2,)), dma, dma,
        dma((8,)), dma((8,)), dma((2, 3)), dma((2, 3)), dma, dma, dma((3,)), dma((3,)),
    ]
    view_grads, proto_grads, loss = pl.pallas_call(
        kernel,
        out_shape=(
            jax.ShapeDtypeStruct((2, 64, FEAT), F32),
            jax.ShapeDtypeStruct((128, FEAT), F32),
            jax.ShapeDtypeStruct((1, 1), F32),
        ),
        in_specs=[anywhere, inside, inside, anywhere],
        out_specs=(inside, inside, inside),
        scratch_shapes=scratch,
        compiler_params=pltpu.CompilerParams(
            collective_id=0, has_side_effects=True, vmem_limit_bytes=56 * 2**20
        ),
        name="swav_step",
    )(
        tokens.reshape(64 * SEQ, FEAT),
        offsets,
        species.reshape(1, 64),
        prototypes,
    )
    view_grads, proto_grads, loss = pl.pallas_call(
        hand_on,
        out_shape=(
            jax.ShapeDtypeStruct((2, 64, FEAT), F32),
            jax.ShapeDtypeStruct((128, FEAT), F32),
            jax.ShapeDtypeStruct((1, 1), F32),
        ),
        in_specs=[inside] * 3,
        out_specs=(inside, inside, inside),
        compiler_params=pltpu.CompilerParams(vmem_limit_bytes=60 * 2**20),
        name="results",
    )(view_grads, proto_grads, loss)
    return view_grads, proto_grads, loss.reshape(())


def solution(mesh):
    return jax.shard_map(
        on_device,
        mesh=mesh,
        in_specs=(P("dp", None, None), P(None, "dp"), P("dp"), P("proto", None)),
        out_specs=(P(None, "dp", None), P(("proto", "dp"), None), P()),
        check_vma=False,
    )
```

```python
import math

import jax
import jax.numpy as jnp
from jax import lax
from jax.experimental import pallas as pl
from jax.experimental.pallas import tpu as pltpu
from jax.sharding import PartitionSpec as P

MESH = pl.DeviceIdType.MESH
F32 = jnp.float32
BF16 = jnp.bfloat16
NGROUP = 16
CROP = 24
SEQ = 32
FEAT = 128
WINDOWS = 4096
PROTOS = 65536
EPS = 1e-6
NY, NZL, NC, NZH, NX = 8, 4, 2, 2, 4
NZ = NZH * NZL
RING8 = (4, 3, 5, 2, 6, 1, 7)
XC = ((2, 0), (2, 1), (1, 0), (3, 0), (1, 1), (3, 1), (0, 1))
RING4 = (2, 1, 3)
PLANE = tuple(
    sorted(
        ((dx, dz) for dx in range(NX) for dz in range(NZ) if dx or dz),
        key=lambda o: -(min(o[0], NX - o[0]) + min(o[1], NZ - o[1])),
    )
)
NP = len(PLANE)
NT = (((1,), (1,)), ((), ()))
NN = (((1,), (0,)), ((), ()))


def mm(a, b, dims=NN):
    return lax.dot_general(a, b, dims, preferred_element_type=F32)


def split3(row, count=16):
    hi = row.astype(BF16).astype(F32)
    rest = row - hi
    mid = rest.astype(BF16).astype(F32)
    lo = rest - mid
    width = row.shape[1]
    at = lax.broadcasted_iota(jnp.int32, (count, width), 0)
    full = lambda r: jnp.broadcast_to(r, (count, width))
    out = jnp.where(at == 0, full(hi), jnp.where(at == 1, full(mid), jnp.where(at == 2, full(lo), 0.0)))
    return out.astype(BF16)


def unit_scale(rows):
    return lax.rsqrt(jnp.mean(rows * rows, axis=-1, keepdims=True) + EPS)


def unit_back(rows, grad):
    scale = unit_scale(rows)
    along = jnp.mean(rows * grad, axis=-1, keepdims=True)
    return (grad - rows * (along * scale * scale)) * (scale / math.sqrt(FEAT))


def kernel(
    tok_ref, off_ref, spec_ref, proto_ref,
    view_ref, pgrad_ref, loss_ref,
    tok, mask, kraw, kunit, keys, keys_t, pooled, qg, q16, s_buf, e_buf, k_buf, kt_buf, t_buf, two,
    a_src, a_c, a_pl, b_src, b_y, r_two, r_pl, r_mem, cnt_src, cnt_y,
    kg_src, kg_half, kg_fwd, kg_y, c_src, c_rcv, x_src, x_rcv, w_src, w_rcv, fin, l_xc, l_z, l_y,
    x_rows, p_row, ab_rows, qt,
    load_sem, g_ssem, g_rsem, gs_ssem, gs_rsem,
    a_ssem, a_rsem, b_ssem, b_rsem, r_ssem, r_rsem, cnt_ssem, cnt_rsem,
    kg_ssem, kg_rsem, f_ssem, f_rsem, fin_ssem, fin_rsem, l_ssem, l_rsem,
):
    dp = lax.axis_index("dp")
    pr = lax.axis_index("proto")
    y, zl, c = lax.div(dp, 8), lax.rem(lax.div(dp, 2), 4), lax.rem(dp, 2)
    zh, x = lax.div(pr, 4), lax.rem(pr, 4)
    z = zh * NZL + zl

    def dev(y=y, z=z, c=c, x=x):
        return ((y * NZL + lax.rem(z, NZL)) * NC + c, lax.div(z, NZL) * NX + x)

    xc_ids = [dev(x=lax.rem(x + dx, NX), c=lax.rem(c + dc, NC)) for dx, dc in XC]
    z_of = [lax.rem(z + j, NZ) for j in RING8]
    z_ids = [dev(z=k) for k in z_of]
    y_of = [lax.rem(y + j, NY) for j in RING8]
    y_ids = [dev(y=k) for k in y_of]
    x_of = [lax.rem(x + j, NX) for j in RING4]
    x_ids = [dev(x=k) for k in x_of]
    sib = dev(c=1 - c)
    plane_ids = [dev(x=lax.rem(x + dx, NX), z=lax.rem(z + dz, NZ)) for dx, dz in PLANE]
    step2 = 2 + 4 * c
    near = [lax.rem(z + step, NZ) for step in (step2, 1, 7)]
    near_ids = [dev(z=k) for k in near]
    cross_ids = [xc_ids[i] for i in range(7) if XC[i][0] and XC[i][1]]

    def remote(src, dst, ssem, rsem, to):
        return pltpu.make_async_remote_copy(
            src_ref=src, dst_ref=dst, send_sem=ssem, recv_sem=rsem, device_id=to, device_id_type=MESH
        )

    def got(ref, sem):
        remote(ref, ref, sem, sem, sib).wait_recv()

    def sent(ref, sem):
        remote(ref, ref, sem, sem, sib).wait_send()

    barrier = pltpu.get_barrier_semaphore()
    load_tok = pltpu.make_async_copy(tok_ref, tok, load_sem.at[0])
    load_key = pltpu.make_async_copy(proto_ref, kraw, load_sem.at[1])
    load_tok.start()
    load_key.start()
    for to in plane_ids + y_ids + cross_ids + [sib]:
        pl.semaphore_signal(barrier, inc=1, device_id=to, device_id_type=MESH)

    off = off_ref[...].astype(F32)
    off_row = jnp.concatenate([off[0:1], off[1:2]], axis=1)
    lane = lax.broadcasted_iota(jnp.int32, (128, 128), 1)
    first = jnp.broadcast_to(off_row, (128, 128)).T.astype(jnp.int32)
    row = lax.broadcasted_iota(jnp.int32, (128, 128), 0)
    first = first + (row & 63) * SEQ
    for part in range(16):
        col = part * 128
        inside = (lane + col >= first) & (lane + col < first + CROP)
        mask[:, pl.ds(col, 128)] = jnp.where(inside, 1.0, 0.0).astype(BF16)
    load_tok.wait()
    total = mm(mask[...], tok[...])
    rows = total / CROP
    pooled[...] = rows
    query = (rows * unit_scale(rows) / math.sqrt(FEAT)).astype(BF16)
    qg[c, zl, pl.ds(0, 128)] = query.astype(F32)
    spec = spec_ref[...].astype(F32)
    both = jnp.concatenate([spec, spec], axis=1)
    half = lax.broadcasted_iota(jnp.int32, (8, 128), 1) // 64
    qg[c, zl, pl.ds(128, 8)] = jnp.where(half == c, jnp.broadcast_to(both, (8, 128)), 0.0)

    load_key.wait()

    def normalise(i, carry):
        at = pl.ds(pl.multiple_of(i * 2048, 2048), 2048)
        raw = kraw[at].astype(F32)
        kunit[at] = (raw * (unit_scale(raw) * (1.0 / math.sqrt(FEAT)))).astype(BF16)
        return carry

    lax.fori_loop(0, 4, normalise, 0)
    def whole(i, sums):
        at = pl.ds(pl.multiple_of(i * 4096, 4096), 4096)
        e = jnp.exp(mm(kunit[at], query, NT) * 10.0)
        k = (e * e).astype(BF16).astype(F32)
        fold = lambda a: jnp.sum(a.reshape(512, 8, 128), axis=0)
        return sums[0] + fold(k), sums[1] + fold(e)

    zero = jnp.zeros((8, 128), F32)
    ks, es = lax.fori_loop(0, 2, whole, (zero, zero))
    r_two[c, :, pl.ds(0, 128)] = jnp.sum(ks, axis=0, keepdims=True)
    r_two[c, :, pl.ds(128, 128)] = jnp.sum(es, axis=0, keepdims=True)

    pl.semaphore_wait(barrier, 11 + NP)
    remote(r_two.at[c], r_two.at[c], r_ssem.at[0], r_rsem.at[0], sib).start()

    mine = qg.at[c, zl]
    for i, to in enumerate(near_ids):
        remote(mine, mine, g_ssem, g_rsem.at[i], to).start()
    remote(mine, mine, gs_ssem, gs_rsem.at[0], sib).start()

    got(r_two.at[1 - c], r_rsem.at[0])
    for i, to in enumerate(plane_ids):
        remote(r_two, r_pl.at[i], r_ssem.at[1], r_rsem.at[1], to).start()

    for i in range(8):
        block = kunit[pl.ds(pl.multiple_of((i * 8 + zl * NC + c) * 128, 128), 128)]
        keys[pl.ds(i * 128, 128)] = block
        turned = block.astype(F32).T.astype(BF16)
        keys_t[:, pl.ds(i * 128, 128)] = turned
        keys_t[:, pl.ds(1024 + i * 128, 128)] = turned

    def scores(zp):
        zp128 = pl.multiple_of(zp * 128, 128)
        pair = []
        for v in range(2):
            q = jnp.concatenate([qg[0, zp, pl.ds(v * 64, 64)], qg[1, zp, pl.ds(v * 64, 64)]], axis=0).astype(BF16)
            q16[v, pl.ds(zp128, 128)] = q
            pair.append(q)
        rhs = jnp.concatenate(pair, axis=0)

        out = mm(keys[...], rhs, NT)
        e = jnp.exp(out * 10.0)
        k = (e * e).astype(BF16)
        for v in range(2):
            at = (v, slice(None), pl.ds(zp128, 128))
            s_buf[at] = out[:, v * 128 : v * 128 + 128]
            e_buf[at] = e[:, v * 128 : v * 128 + 128]
            k_buf[at] = k[:, v * 128 : v * 128 + 128]

    got(qg.at[1 - c, zl], gs_rsem.at[0])
    scores(zl)

    def member(i, step):
        zp = lax.rem(zl + step, NZL)
        piece = qg.at[c, zp]
        got(piece, g_rsem.at[i])
        remote(piece, piece, gs_ssem, gs_rsem.at[i + 1], sib).start()
        got(qg.at[1 - c, zp], gs_rsem.at[i + 1])
        scores(zp)

    member(1, 3)
    member(2, 1)
    member(0, 2)
    got(r_pl, r_rsem.at[1])
    for step in range(NZL):
        part = r_two[...] if step == 0 else None
        for i, (dx, dz) in enumerate(PLANE):
            if dz % NZL == step:
                part = r_pl[i] if part is None else part + r_pl[i]
        r_mem[lax.rem(zl + NZL - step, NZL)] = part
    pairs = [r_mem[j] for j in range(NZL)]

    def assemble(base):
        tiles = []
        for v in range(2):
            at = base + v * 64
            for j in range(NZL):
                tiles += [pairs[j][0][:, at : at + 64], pairs[j][1][:, at : at + 64]]
        return jnp.concatenate(tiles, axis=1)

    window_scale = PROTOS / assemble(0)
    totals = assemble(128)

    spec_row = jnp.concatenate([qg[0, i, pl.ds(128, 1)] + qg[1, i, pl.ds(128, 1)] for i in range(4)], axis=1)
    group = lax.broadcasted_iota(jnp.int32, (NGROUP, 512), 0)
    onehot = jnp.where(group == jnp.broadcast_to(spec_row, (NGROUP, 512)).astype(jnp.int32), 1.0, 0.0)

    def a_sum(it, between_1=None, between_2=None):
        remote(a_src.at[it, 0], a_c.at[it], a_ssem.at[it, 0], a_rsem.at[it, 0], sib).start()
        if between_1 is not None:
            between_1()
        got(a_c.at[it], a_rsem.at[it, 0])
        part = a_src[it, 0] + a_c[it]
        a_src[it, 1] = part
        for i, to in enumerate(plane_ids):
            remote(a_src.at[it, 1], a_pl.at[it, i], a_ssem.at[it, 1], a_rsem.at[it, 1], to).start()
        if between_2 is not None:
            between_2()
        got(a_pl.at[it], a_rsem.at[it, 1])
        for i in range(NP):
            part = part + a_pl[it, i]
        return part

    def b_sum(it, between=None):
        for i, to in enumerate(y_ids):
            remote(b_src.at[it], b_y.at[it, i], b_ssem.at[it], b_rsem.at[it], to).start()
        if between is not None:
            between()
        got(b_y.at[it], b_rsem.at[it])
        part = b_src[it]
        for i in range(7):
            part = part + b_y[it, i]
        return part

    def send_counts():
        cnt_src[...] = jnp.broadcast_to(jnp.sum(onehot, axis=1, keepdims=True), (NGROUP, 128))
        for i, to in enumerate(y_ids):
            remote(cnt_src, cnt_y.at[i], cnt_ssem, cnt_rsem, to).start()

    def halves(value, k0, width):
        hi = value.astype(BF16)
        two[pl.ds(k0, width)] = hi
        two[pl.ds(1024 + k0, width)] = (value - hi.astype(F32)).astype(BF16)

    def split_e(v):
        def block(kb, carry):
            k0 = pl.multiple_of(kb * 32, 32)
            halves(e_buf[v, pl.ds(k0, 32)], k0, 32)
            return carry

        lax.fori_loop(0, 32, block, 0)

    def split_t(v):
        for i in range(8):
            p = p_row[:, pl.ds(pl.multiple_of(v * 1024 + i * 128, 128), 128)]
            col = jnp.broadcast_to(p, (128, 128)).T
            t = k_buf[v, pl.ds(i * 128, 128)].astype(F32) * jnp.concatenate([col] * 4, axis=1)
            t_buf[v, pl.ds(i * 128, 128)] = t
            halves(t, i * 128, 128)

    def q_theirs(step):
        theirs = 1 - c if step == 0 else c
        (split_e, split_t)[step](theirs)
        c_src[step] = mm(keys_t[...], two[...])
        remote(c_src.at[step], c_rcv.at[step], f_ssem.at[step, 0], f_rsem.at[step, 0], sib).start()

    def q_own(step):
        (split_e, split_t)[step](c if step == 0 else 1 - c)
        x_src[step] = mm(keys_t[...], two[...])

    def q_x(step):
        got(c_rcv.at[step], f_rsem.at[step, 0])
        x_src[step] = x_src[step] + c_rcv[step]
        for i, xx in enumerate(x_of):
            piece = x_src.at[step, pl.ds(pl.multiple_of(xx * 32, 32), 32)]
            remote(piece, x_rcv.at[step, i], f_ssem.at[step, 1], f_rsem.at[step, 1], x_ids[i]).start()

    def q_z(step):
        got(x_rcv.at[step], f_rsem.at[step, 1])
        part = x_src[step, pl.ds(pl.multiple_of(x * 32, 32), 32)]
        for i in range(3):
            part = part + x_rcv[step, i]
        for i in range(4):
            w_src[step, i] = part[:, i * 128 : i * 128 + 128]
        for i, to in enumerate(z_ids):
            piece = w_src.at[step, lax.rem(z_of[i], NZL)]
            remote(piece, w_rcv.at[step, i], f_ssem.at[step, 2], f_rsem.at[step, 2], to).start()

    def q_end(step):
        got(w_rcv.at[step], f_rsem.at[step, 2])
        part = w_src[step, zl]
        for i in range(7):
            part = part + w_rcv[step, i]
        return part

    def columns(it, scale):
        for v in range(2):
            parts = split3(scale[:, v * 512 : v * 512 + 512])
            out = mm(parts, k_buf[v], NT) if it == 0 else mm(parts, kt_buf[v])
            b_src[it, :, pl.ds(v * 1024, 1024)] = jnp.sum(out, axis=0, keepdims=True)

    def row_sums(it, scale):
        for v in range(2):
            out = mm(split3(scale[:, v * 1024 : v * 1024 + 1024]), k_buf[v])
            a_src[it, 0, :, pl.ds(v * 512, 512)] = jnp.sum(out, axis=0, keepdims=True)

    def beside_a0():
        send_counts()
        q_theirs(0)
        q_own(0)

    def turn():
        for v in range(2):
            kt_buf[v] = k_buf[v].T

    columns(0, window_scale)
    proto_scale = 1.0 / (PROTOS * b_sum(0, turn))
    row_sums(0, proto_scale)
    window_scale = 1.0 / a_sum(0, None, beside_a0)
    columns(1, window_scale)
    proto_scale = 1.0 / (PROTOS * b_sum(1, lambda: q_x(0)))
    row_sums(1, proto_scale)
    window_scale = 1.0 / a_sum(1)
    columns(2, window_scale)
    proto_scale = 1.0 / (PROTOS * b_sum(2, lambda: q_z(0)))
    row_sums(2, proto_scale)
    p_row[...] = proto_scale

    def cross():
        for v in range(2):

            def block(kb, acc):
                k0 = pl.multiple_of(kb * 32, 32)
                prod = t_buf[1 - v, pl.ds(k0, 32)] * s_buf[v, pl.ds(k0, 32)]
                return acc + jnp.sum(prod.reshape(4, 8, 512), axis=0)

            acc = lax.fori_loop(0, 32, block, jnp.zeros((8, 512), F32))
            x_rows[v] = jnp.sum(acc, axis=0, keepdims=True)

    def beside_a2():
        q_own(1)
        q_x(1)
        cross()

    last = 1.0 / a_sum(2, lambda: q_theirs(1), beside_a2)

    got(cnt_y, cnt_rsem)
    counts = cnt_src[...]
    for i in range(7):
        counts = counts + cnt_y[i]
    seen = jnp.sum(onehot * jnp.concatenate([counts] * 4, axis=1), axis=0, keepdims=True)
    weight = WINDOWS / (NGROUP * seen)
    last_v = [last[:, 0:512], last[:, 512:1024]]
    tot_v = [totals[:, 0:512], totals[:, 512:1024]]
    a_v = [5.0 * weight / tot_v[v] for v in range(2)]
    b_v = [5.0 * weight * last_v[1 - v] for v in range(2)]
    for v in range(2):
        ab_rows[0, v] = a_v[v]
        ab_rows[1, v] = b_v[v]
    terms = jnp.zeros((1, 512), F32)
    for v in range(2):
        terms = terms + 0.5 * weight * (jnp.log(tot_v[v]) / 64.0 - 10.0 * last_v[1 - v] * x_rows[v])
    terms = terms[:, 0:128] + terms[:, 128:256] + terms[:, 256:384] + terms[:, 384:512]
    me_xc = x * NC + c
    l_xc[me_xc] = terms
    for to in xc_ids:
        remote(l_xc.at[me_xc], l_xc.at[me_xc], l_ssem.at[0], l_rsem.at[0], to).start()

    def add_slots(ref):
        out = ref[0]
        for i in range(1, 8):
            out = out + ref[i]
        return out

    def key_part(slot, yy):
        k0 = pl.multiple_of(yy * 128, 128)
        part = jnp.zeros((128, FEAT), F32)
        for v in range(2):
            at = (pl.ds(k0, 128), slice(None))
            g = (e_buf[(v,) + at] * a_v[v] - t_buf[(1 - v,) + at] * b_v[v]).astype(BF16)
            part = part + mm(g, q16[v])
        kg_src[slot] = part

    ahead = lambda j: lax.rem(y + j, NY)
    up1, up2, down1, down2 = (dev(y=ahead(j)) for j in (1, 2, 7, 6))
    key_part(4, ahead(4))
    remote(kg_src.at[4, pl.ds(0, 64)], kg_half.at[0], kg_ssem.at[0], kg_rsem.at[0], up2).start()
    remote(kg_src.at[4, pl.ds(64, 64)], kg_half.at[1], kg_ssem.at[1], kg_rsem.at[1], down2).start()
    key_part(3, ahead(3))
    remote(kg_src.at[3], kg_fwd.at[0], kg_ssem.at[2], kg_rsem.at[2], up1).start()
    key_part(5, ahead(5))
    remote(kg_src.at[5], kg_fwd.at[1], kg_ssem.at[3], kg_rsem.at[3], down1).start()
    key_part(2, ahead(2))
    key_part(6, ahead(6))
    key_part(1, ahead(1))
    remote(kg_src.at[1], kg_y.at[0], kg_ssem.at[4], kg_rsem.at[4], up1).start()
    key_part(7, ahead(7))
    remote(kg_src.at[7], kg_y.at[1], kg_ssem.at[5], kg_rsem.at[5], down1).start()
    key_part(0, y)

    q_z(1)
    got(kg_fwd.at[0], kg_rsem.at[2])
    got(kg_half.at[0], kg_rsem.at[0])
    kg_src[2, pl.ds(0, 64)] = kg_src[2, pl.ds(0, 64)] + kg_fwd[0, pl.ds(0, 64)] + kg_half[0]
    kg_src[2, pl.ds(64, 64)] = kg_src[2, pl.ds(64, 64)] + kg_fwd[0, pl.ds(64, 64)]
    remote(kg_src.at[2], kg_y.at[2], kg_ssem.at[6], kg_rsem.at[6], up2).start()
    got(kg_fwd.at[1], kg_rsem.at[3])
    got(kg_half.at[1], kg_rsem.at[1])
    kg_src[6, pl.ds(0, 64)] = kg_src[6, pl.ds(0, 64)] + kg_fwd[1, pl.ds(0, 64)]
    kg_src[6, pl.ds(64, 64)] = kg_src[6, pl.ds(64, 64)] + kg_fwd[1, pl.ds(64, 64)] + kg_half[1]
    remote(kg_src.at[6], kg_y.at[3], kg_ssem.at[7], kg_rsem.at[7], down2).start()

    got(l_xc.at[pl.ds(0, 7)], l_rsem.at[0])
    l_z[z] = add_slots(l_xc)
    for to in z_ids:
        remote(l_z.at[z], l_z.at[z], l_ssem.at[1], l_rsem.at[1], to).start()

    at = pl.ds(pl.multiple_of(zl * 128, 128), 128)
    part = ab_rows[0, c, :, at] * q_end(0) - ab_rows[1, c, :, at] * q_end(1)
    mine = fin.at[c, pl.ds(pl.multiple_of(x * 32, 32), 32)]
    fin[c, pl.ds(pl.multiple_of(x * 32, 32), 32)] = part
    for to in xc_ids:
        remote(mine, mine, fin_ssem, fin_rsem, to).start()
    got(l_z.at[pl.ds(0, 7)], l_rsem.at[1])
    l_y[y] = add_slots(l_z)
    for to in y_ids:
        remote(l_y.at[y], l_y.at[y], l_ssem.at[2], l_rsem.at[2], to).start()

    part = kg_src[0]
    for i, k in ((0, 4), (1, 5), (2, 6), (3, 7)):
        got(kg_y.at[i], kg_rsem.at[k])
        part = part + kg_y[i]
    own = pl.multiple_of((y * 8 + zl * NC + c) * 128, 128)
    pgrad_ref[...] = unit_back(kraw[pl.ds(own, 128)].astype(F32), part)

    got(w_rcv.at[0], fin_rsem)
    for v in range(2):
        qt[v] = fin[v].T
    for v in range(2):
        grad = qt[v, pl.ds(pl.multiple_of(c * 64, 64), 64)]
        view_ref[v] = unit_back(pooled[pl.ds(v * 64, 64)], grad)

    got(l_y.at[pl.ds(0, 7)], l_rsem.at[2])
    loss_ref[...] = jnp.sum(add_slots(l_y), axis=1, keepdims=True) * (1.0 / WINDOWS)

    sent(qg.at[0, pl.ds(0, 3)], g_ssem)
    sent(qg.at[0], gs_ssem)
    for it in range(3):
        sent(a_c.at[it], a_ssem.at[it, 0])
        sent(a_pl.at[it], a_ssem.at[it, 1])
    for it in range(3):
        sent(b_y.at[it], b_ssem.at[it])
    sent(r_two.at[0], r_ssem.at[0])
    sent(r_pl, r_ssem.at[1])
    sent(cnt_y, cnt_ssem)
    for i in range(2):
        sent(kg_half.at[i], kg_ssem.at[i])
        sent(kg_fwd.at[i], kg_ssem.at[2 + i])
        sent(kg_y.at[i], kg_ssem.at[4 + i])
        sent(kg_y.at[2 + i], kg_ssem.at[6 + i])
        sent(c_rcv.at[i], f_ssem.at[i, 0])
        sent(x_rcv.at[i], f_ssem.at[i, 1])
        sent(w_rcv.at[i], f_ssem.at[i, 2])
    sent(w_rcv.at[0], fin_ssem)
    for i in range(3):
        sent(l_xc.at[pl.ds(0, 7)], l_ssem.at[i])


def hand_on(view_in, pgrad_in, loss_in, view_ref, pgrad_ref, loss_ref):
    view_ref[...] = view_in[...]
    pgrad_ref[...] = pgrad_in[...]
    loss_ref[...] = loss_in[...]


def on_device(tokens, offsets, species, prototypes):
    vmem = pltpu.VMEM
    dma = pltpu.SemaphoreType.DMA
    anywhere = pl.BlockSpec(memory_space=pl.ANY)
    inside = pl.BlockSpec(memory_space=pltpu.VMEM)
    scratch = [
        vmem((64 * SEQ, FEAT), BF16),
        vmem((128, 64 * SEQ), BF16),
        vmem((8192, FEAT), BF16),
        vmem((8192, FEAT), BF16),
        vmem((1024, FEAT), BF16),
        vmem((FEAT, 2048), BF16),
        vmem((128, FEAT), F32),
        vmem((2, 4, 136, FEAT), F32),
        vmem((2, 512, FEAT), BF16),
        vmem((2, 1024, 512), F32),
        vmem((2, 1024, 512), F32),
        vmem((2, 1024, 512), BF16),
        vmem((2, 512, 1024), BF16),
        vmem((2, 1024, 512), F32),
        vmem((2048, 512), BF16),
        vmem((3, 2, 1, 1024), F32),
        vmem((3, 1, 1024), F32),
        vmem((3, NP, 1, 1024), F32),
        vmem((3, 1, 2048), F32),
        vmem((3, 7, 1, 2048), F32),
        vmem((2, 1, 256), F32),
        vmem((NP, 2, 1, 256), F32),
        vmem((4, 2, 1, 256), F32),
        vmem((NGROUP, 128), F32),
        vmem((7, NGROUP, 128), F32),
        vmem((8, 128, FEAT), F32),
        vmem((2, 64, FEAT), F32),
        vmem((2, 128, FEAT), F32),
        vmem((4, 128, FEAT), F32),
        vmem((2, FEAT, 512), F32),
        vmem((2, FEAT, 512), F32),
        vmem((2, FEAT, 512), F32),
        vmem((2, 3, 32, 512), F32),
        vmem((2, 4, 32, 128), F32),
        vmem((2, 7, 32, 128), F32),
        vmem((2, FEAT, 128), F32),
        vmem((8, 1, 128), F32),
        vmem((8, 1, 128), F32),
        vmem((8, 1, 128), F32),
        vmem((2, 1, 512), F32),
        vmem((1, 2048), F32),
        vmem((2, 2, 1, 512), F32),
        vmem((2, 128, FEAT), F32),
        dma((2,)),
        dma, dma((3,)), dma, dma((4,)),
        dma((3, 2)), dma((3, 2)), dma((3,)), dma((3,)), dma((2,)), dma((2,)), dma, dma,
        dma((8,)), dma((8,)), dma((2, 3)), dma((2, 3)), dma, dma, dma((3,)), dma((3,)),
    ]
    view_grads, proto_grads, loss = pl.pallas_call(
        kernel,
        out_shape=(
            jax.ShapeDtypeStruct((2, 64, FEAT), F32),
            jax.ShapeDtypeStruct((128, FEAT), F32),
            jax.ShapeDtypeStruct((1, 1), F32),
        ),
        in_specs=[anywhere, inside, inside, anywhere],
        out_specs=(inside, inside, inside),
        scratch_shapes=scratch,
        compiler_params=pltpu.CompilerParams(
            collective_id=0, has_side_effects=True, vmem_limit_bytes=56 * 2**20
        ),
        name="swav_step",
    )(
        tokens.reshape(64 * SEQ, FEAT),
        offsets,
        species.reshape(1, 64),
        prototypes,
    )
    view_grads, proto_grads, loss = pl.pallas_call(
        hand_on,
        out_shape=(
            jax.ShapeDtypeStruct((2, 64, FEAT), F32),
            jax.ShapeDtypeStruct((128, FEAT), F32),
            jax.ShapeDtypeStruct((1, 1), F32),
        ),
        in_specs=[inside] * 3,
        out_specs=(inside, inside, inside),
        compiler_params=pltpu.CompilerParams(vmem_limit_bytes=60 * 2**20),
        name="results",
    )(view_grads, proto_grads, loss)
    return view_grads, proto_grads, loss.reshape(())


def solution(mesh):
    return jax.shard_map(
        on_device,
        mesh=mesh,
        in_specs=(P("dp", None, None), P(None, "dp"), P("dp"), P("proto", None)),
        out_specs=(P(None, "dp", None), P(("proto", "dp"), None), P()),
        check_vma=False,
    )
```

```python
import math

import jax
import jax.numpy as jnp
from jax import lax
from jax.experimental import pallas as pl
from jax.experimental.pallas import tpu as pltpu
from jax.sharding import PartitionSpec as P

MESH = pl.DeviceIdType.MESH
F32 = jnp.float32
BF16 = jnp.bfloat16
NGROUP = 16
CROP = 24
SEQ = 32
FEAT = 128
WINDOWS = 4096
PROTOS = 65536
EPS = 1e-6
NY, NZL, NC, NZH, NX = 8, 4, 2, 2, 4
NZ = NZH * NZL
RING8 = (4, 3, 5, 2, 6, 1, 7)
XC = ((2, 0), (2, 1), (1, 0), (3, 0), (1, 1), (3, 1), (0, 1))
RING4 = (2, 1, 3)
PLANE = tuple(
    sorted(
        ((dx, dz) for dx in range(NX) for dz in range(NZ) if dx or dz),
        key=lambda o: -(min(o[0], NX - o[0]) + min(o[1], NZ - o[1])),
    )
)
NP = len(PLANE)
NT = (((1,), (1,)), ((), ()))
NN = (((1,), (0,)), ((), ()))


def mm(a, b, dims=NN):
    return lax.dot_general(a, b, dims, preferred_element_type=F32)


def split3(row, count=16):
    hi = row.astype(BF16).astype(F32)
    rest = row - hi
    mid = rest.astype(BF16).astype(F32)
    lo = rest - mid
    width = row.shape[1]
    at = lax.broadcasted_iota(jnp.int32, (count, width), 0)
    full = lambda r: jnp.broadcast_to(r, (count, width))
    out = jnp.where(at == 0, full(hi), jnp.where(at == 1, full(mid), jnp.where(at == 2, full(lo), 0.0)))
    return out.astype(BF16)


def unit_scale(rows):
    return lax.rsqrt(jnp.mean(rows * rows, axis=-1, keepdims=True) + EPS)


def unit_back(rows, grad):
    scale = unit_scale(rows)
    along = jnp.mean(rows * grad, axis=-1, keepdims=True)
    return (grad - rows * (along * scale * scale)) * (scale / math.sqrt(FEAT))


def kernel(
    tok_ref, off_ref, spec_ref, proto_ref,
    view_ref, pgrad_ref, loss_ref,
    tok, mask, kraw, kunit, keys, keys_t, pooled, qg, q16, s_buf, e_buf, k_buf, kt_buf, t_buf, two,
    a_src, a_c, a_pl, b_src, b_y, r_two, r_pl, cnt_src, cnt_y,
    kg_src, kg_half, kg_fwd, kg_y, c_src, c_rcv, x_src, x_rcv, w_src, w_rcv, fin, l_y,
    x_own, x_c, x_pl, p_row, ab_rows, qt,
    load_sem, g_ssem, g_rsem, gs_ssem, gs_rsem,
    a_ssem, a_rsem, b_ssem, b_rsem, r_ssem, r_rsem, cnt_ssem, cnt_rsem,
    kg_ssem, kg_rsem, f_ssem, f_rsem, fin_ssem, fin_rsem, l_ssem, l_rsem,
):
    dp = lax.axis_index("dp")
    pr = lax.axis_index("proto")
    y, zl, c = lax.div(dp, 8), lax.rem(lax.div(dp, 2), 4), lax.rem(dp, 2)
    zh, x = lax.div(pr, 4), lax.rem(pr, 4)
    z = zh * NZL + zl

    def dev(y=y, z=z, c=c, x=x):
        return ((y * NZL + lax.rem(z, NZL)) * NC + c, lax.div(z, NZL) * NX + x)

    xc_ids = [dev(x=lax.rem(x + dx, NX), c=lax.rem(c + dc, NC)) for dx, dc in XC]
    z_of = [lax.rem(z + j, NZ) for j in RING8]
    z_ids = [dev(z=k) for k in z_of]
    y_of = [lax.rem(y + j, NY) for j in RING8]
    y_ids = [dev(y=k) for k in y_of]
    x_of = [lax.rem(x + j, NX) for j in RING4]
    x_ids = [dev(x=k) for k in x_of]
    sib = dev(c=1 - c)
    plane_ids = [dev(x=lax.rem(x + dx, NX), z=lax.rem(z + dz, NZ)) for dx, dz in PLANE]
    step2 = 2 + 4 * c
    near = [lax.rem(z + step, NZ) for step in (step2, 1, 7)]
    near_ids = [dev(z=k) for k in near]
    here = z * NX + x
    cross_ids = [xc_ids[i] for i in range(7) if XC[i][0] and XC[i][1]]

    def remote(src, dst, ssem, rsem, to):
        return pltpu.make_async_remote_copy(
            src_ref=src, dst_ref=dst, send_sem=ssem, recv_sem=rsem, device_id=to, device_id_type=MESH
        )

    def got(ref, sem):
        remote(ref, ref, sem, sem, sib).wait_recv()

    def sent(ref, sem):
        remote(ref, ref, sem, sem, sib).wait_send()

    barrier = pltpu.get_barrier_semaphore()
    load_tok = pltpu.make_async_copy(tok_ref, tok, load_sem.at[0])
    load_key = pltpu.make_async_copy(proto_ref, kraw, load_sem.at[1])
    load_tok.start()
    load_key.start()
    for to in plane_ids + y_ids + cross_ids + [sib]:
        pl.semaphore_signal(barrier, inc=1, device_id=to, device_id_type=MESH)

    off = off_ref[...].astype(F32)
    off_row = jnp.concatenate([off[0:1], off[1:2]], axis=1)
    lane = lax.broadcasted_iota(jnp.int32, (128, 128), 1)
    first = jnp.broadcast_to(off_row, (128, 128)).T.astype(jnp.int32)
    row = lax.broadcasted_iota(jnp.int32, (128, 128), 0)
    first = first + (row & 63) * SEQ
    for part in range(16):
        col = part * 128
        inside = (lane + col >= first) & (lane + col < first + CROP)
        mask[:, pl.ds(col, 128)] = jnp.where(inside, 1.0, 0.0).astype(BF16)
    load_tok.wait()
    total = mm(mask[...], tok[...])
    rows = total / CROP
    pooled[...] = rows
    query = (rows * unit_scale(rows) / math.sqrt(FEAT)).astype(BF16)
    qg[c, zl, pl.ds(0, 128)] = query.astype(F32)
    spec = spec_ref[...].astype(F32)
    both = jnp.concatenate([spec, spec], axis=1)
    half = lax.broadcasted_iota(jnp.int32, (8, 128), 1) // 64
    qg[c, zl, pl.ds(128, 8)] = jnp.where(half == c, jnp.broadcast_to(both, (8, 128)), 0.0)

    load_key.wait()

    def normalise(i, carry):
        at = pl.ds(pl.multiple_of(i * 2048, 2048), 2048)
        raw = kraw[at].astype(F32)
        kunit[at] = (raw * (unit_scale(raw) * (1.0 / math.sqrt(FEAT)))).astype(BF16)
        return carry

    lax.fori_loop(0, 4, normalise, 0)
    def whole(i, sums):
        at = pl.ds(pl.multiple_of(i * 4096, 4096), 4096)
        e = jnp.exp(mm(kunit[at], query, NT) * 10.0)
        k = (e * e).astype(BF16).astype(F32)
        fold = lambda a: jnp.sum(a.reshape(512, 8, 128), axis=0)
        return sums[0] + fold(k), sums[1] + fold(e)

    zero = jnp.zeros((8, 128), F32)
    ks, es = lax.fori_loop(0, 2, whole, (zero, zero))
    r_two[c, :, pl.ds(0, 128)] = jnp.sum(ks, axis=0, keepdims=True)
    r_two[c, :, pl.ds(128, 128)] = jnp.sum(es, axis=0, keepdims=True)

    pl.semaphore_wait(barrier, 11 + NP)
    remote(r_two.at[c], r_two.at[c], r_ssem.at[0], r_rsem.at[0], sib).start()

    mine = qg.at[c, zl]
    for i, to in enumerate(near_ids):
        remote(mine, mine, g_ssem, g_rsem.at[i], to).start()
    remote(mine, mine, gs_ssem, gs_rsem.at[0], sib).start()

    got(r_two.at[1 - c], r_rsem.at[0])
    r_pl[here] = r_two[...]
    for to in plane_ids:
        remote(r_pl.at[here], r_pl.at[here], r_ssem.at[1], r_rsem.at[1], to).start()

    for i in range(8):
        block = kunit[pl.ds(pl.multiple_of((i * 8 + zl * NC + c) * 128, 128), 128)]
        keys[pl.ds(i * 128, 128)] = block
        turned = block.astype(F32).T.astype(BF16)
        keys_t[:, pl.ds(i * 128, 128)] = turned
        keys_t[:, pl.ds(1024 + i * 128, 128)] = turned

    def scores(zp):
        zp128 = pl.multiple_of(zp * 128, 128)
        pair = []
        for v in range(2):
            q = jnp.concatenate([qg[0, zp, pl.ds(v * 64, 64)], qg[1, zp, pl.ds(v * 64, 64)]], axis=0).astype(BF16)
            q16[v, pl.ds(zp128, 128)] = q
            pair.append(q)
        rhs = jnp.concatenate(pair, axis=0)

        out = mm(keys[...], rhs, NT)
        e = jnp.exp(out * 10.0)
        k = (e * e).astype(BF16)
        for v in range(2):
            at = (v, slice(None), pl.ds(zp128, 128))
            s_buf[at] = out[:, v * 128 : v * 128 + 128]
            e_buf[at] = e[:, v * 128 : v * 128 + 128]
            k_buf[at] = k[:, v * 128 : v * 128 + 128]

    got(qg.at[1 - c, zl], gs_rsem.at[0])
    scores(zl)

    def member(i, step):
        zp = lax.rem(zl + step, NZL)
        piece = qg.at[c, zp]
        got(piece, g_rsem.at[i])
        remote(piece, piece, gs_ssem, gs_rsem.at[i + 1], sib).start()
        got(qg.at[1 - c, zp], gs_rsem.at[i + 1])
        scores(zp)

    member(1, 3)
    member(2, 1)
    member(0, 2)
    got(r_pl.at[pl.ds(0, NP)], r_rsem.at[1])
    pairs = []
    for j in range(NZL):
        part = None
        for i in range(NZ * NX):
            if (i // NX) % NZL == j:
                part = r_pl[i] if part is None else part + r_pl[i]
        pairs.append(part)

    def assemble(base):
        tiles = []
        for v in range(2):
            at = base + v * 64
            for j in range(NZL):
                tiles += [pairs[j][0][:, at : at + 64], pairs[j][1][:, at : at + 64]]
        return jnp.concatenate(tiles, axis=1)

    window_scale = PROTOS / assemble(0)
    totals = assemble(128)

    spec_row = jnp.concatenate([qg[0, i, pl.ds(128, 1)] + qg[1, i, pl.ds(128, 1)] for i in range(4)], axis=1)
    group = lax.broadcasted_iota(jnp.int32, (NGROUP, 512), 0)
    onehot = jnp.where(group == jnp.broadcast_to(spec_row, (NGROUP, 512)).astype(jnp.int32), 1.0, 0.0)

    def plane_sum(own, slots, ssem, rsem, between):
        slots[here] = own
        for to in plane_ids:
            remote(slots.at[here], slots.at[here], ssem, rsem, to).start()
        between()

        def result():
            got(slots.at[pl.ds(0, NP)], rsem)
            part = slots[0]
            for i in range(1, NP + 1):
                part = part + slots[i]
            return part

        return result

    def nothing():
        pass

    def a_sum(it, between_1=nothing, between_2=nothing):
        remote(a_src.at[it], a_c.at[it], a_ssem.at[it, 0], a_rsem.at[it, 0], sib).start()
        between_1()
        got(a_c.at[it], a_rsem.at[it, 0])
        part = a_src[it] + a_c[it]
        return plane_sum(part, a_pl.at[it], a_ssem.at[it, 1], a_rsem.at[it, 1], between_2)()

    def b_sum(it, between=None):
        for i, to in enumerate(y_ids):
            remote(b_src.at[it], b_y.at[it, i], b_ssem.at[it], b_rsem.at[it], to).start()
        if between is not None:
            between()
        got(b_y.at[it], b_rsem.at[it])
        part = b_src[it]
        for i in range(7):
            part = part + b_y[it, i]
        return part

    def send_counts():
        cnt_src[...] = jnp.broadcast_to(jnp.sum(onehot, axis=1, keepdims=True), (NGROUP, 128))
        for i, to in enumerate(y_ids):
            remote(cnt_src, cnt_y.at[i], cnt_ssem, cnt_rsem, to).start()

    def halves(value, k0, width):
        hi = value.astype(BF16)
        two[pl.ds(k0, width)] = hi
        two[pl.ds(1024 + k0, width)] = (value - hi.astype(F32)).astype(BF16)

    def split_e(v):
        def block(kb, carry):
            k0 = pl.multiple_of(kb * 32, 32)
            halves(e_buf[v, pl.ds(k0, 32)], k0, 32)
            return carry

        lax.fori_loop(0, 32, block, 0)

    def split_t(v):
        for i in range(8):
            p = p_row[:, pl.ds(pl.multiple_of(v * 1024 + i * 128, 128), 128)]
            col = jnp.broadcast_to(p, (128, 128)).T
            t = k_buf[v, pl.ds(i * 128, 128)].astype(F32) * jnp.concatenate([col] * 4, axis=1)
            t_buf[v, pl.ds(i * 128, 128)] = t
            halves(t, i * 128, 128)

    def q_theirs(step):
        theirs = 1 - c if step == 0 else c
        (split_e, split_t)[step](theirs)
        c_src[step] = mm(keys_t[...], two[...])
        remote(c_src.at[step], c_rcv.at[step], f_ssem.at[step, 0], f_rsem.at[step, 0], sib).start()

    def q_own(step):
        (split_e, split_t)[step](c if step == 0 else 1 - c)
        x_src[step] = mm(keys_t[...], two[...])

    def q_x(step):
        got(c_rcv.at[step], f_rsem.at[step, 0])
        x_src[step] = x_src[step] + c_rcv[step]
        for h in range(2):
            for i, xx in enumerate(x_of):
                piece = x_src.at[step, pl.ds(pl.multiple_of(xx * 32 + h * 16, 16), 16)]
                remote(piece, x_rcv.at[step, h, i], f_ssem.at[step, 1 + h], f_rsem.at[step, 1 + h], x_ids[i]).start()

    def q_z(step, h):
        got(x_rcv.at[step, h], f_rsem.at[step, 1 + h])
        part = x_src[step, pl.ds(pl.multiple_of(x * 32 + h * 16, 16), 16)]
        for i in range(3):
            part = part + x_rcv[step, h, i]
        for i in range(4):
            w_src[step, h, i] = part[:, i * 128 : i * 128 + 128]
        for i, to in enumerate(z_ids):
            piece = w_src.at[step, h, lax.rem(z_of[i], NZL)]
            remote(piece, w_rcv.at[step, h, i], f_ssem.at[step, 3 + h], f_rsem.at[step, 3 + h], to).start()

    def q_end(step, h):
        got(w_rcv.at[step, h], f_rsem.at[step, 3 + h])
        part = w_src[step, h, zl]
        for i in range(7):
            part = part + w_rcv[step, h, i]
        return part

    def columns(it, scale):
        for v in range(2):
            parts = split3(scale[:, v * 512 : v * 512 + 512])
            out = mm(parts, k_buf[v], NT) if it == 0 else mm(parts, kt_buf[v])
            b_src[it, :, pl.ds(v * 1024, 1024)] = jnp.sum(out, axis=0, keepdims=True)

    def row_sums(it, scale):
        for v in range(2):
            out = mm(split3(scale[:, v * 1024 : v * 1024 + 1024]), k_buf[v])
            a_src[it, :, pl.ds(v * 512, 512)] = jnp.sum(out, axis=0, keepdims=True)

    def both_z():
        q_z(0, 0)
        q_z(0, 1)

    def beside_a0():
        send_counts()
        q_theirs(0)
        q_own(0)

    def turn():
        for v in range(2):
            kt_buf[v] = k_buf[v].T

    columns(0, window_scale)
    proto_scale = 1.0 / (PROTOS * b_sum(0, turn))
    row_sums(0, proto_scale)
    window_scale = 1.0 / a_sum(0, nothing, beside_a0)
    columns(1, window_scale)
    proto_scale = 1.0 / (PROTOS * b_sum(1, lambda: q_x(0)))
    row_sums(1, proto_scale)
    window_scale = 1.0 / a_sum(1)
    columns(2, window_scale)
    proto_scale = 1.0 / (PROTOS * b_sum(2, both_z))
    row_sums(2, proto_scale)
    p_row[...] = proto_scale

    def cross():
        for v in range(2):

            def block(kb, acc):
                k0 = pl.multiple_of(kb * 32, 32)
                prod = t_buf[1 - v, pl.ds(k0, 32)] * s_buf[v, pl.ds(k0, 32)]
                return acc + jnp.sum(prod.reshape(4, 8, 512), axis=0)

            acc = lax.fori_loop(0, 32, block, jnp.zeros((8, 512), F32))
            x_own[:, pl.ds(v * 512, 512)] = jnp.sum(acc, axis=0, keepdims=True)

    def beside_a2():
        q_own(1)
        q_x(1)
        cross()
        remote(x_own, x_c, l_ssem.at[0], l_rsem.at[0], sib).start()
        got(x_c, l_rsem.at[0])
        cross_sum.append(plane_sum(x_own[...] + x_c[...], x_pl, l_ssem.at[1], l_rsem.at[1], nothing))

    cross_sum = []
    last = 1.0 / a_sum(2, lambda: q_theirs(1), beside_a2)

    got(cnt_y, cnt_rsem)
    counts = cnt_src[...]
    for i in range(7):
        counts = counts + cnt_y[i]
    seen = jnp.sum(onehot * jnp.concatenate([counts] * 4, axis=1), axis=0, keepdims=True)
    weight = WINDOWS / (NGROUP * seen)
    last_v = [last[:, 0:512], last[:, 512:1024]]
    tot_v = [totals[:, 0:512], totals[:, 512:1024]]
    a_v = [5.0 * weight / tot_v[v] for v in range(2)]
    b_v = [5.0 * weight * last_v[1 - v] for v in range(2)]
    for v in range(2):
        ab_rows[0, v] = a_v[v]
        ab_rows[1, v] = b_v[v]
    def add_slots(ref):
        out = ref[0]
        for i in range(1, 8):
            out = out + ref[i]
        return out

    def key_part(slot, yy):
        k0 = pl.multiple_of(yy * 128, 128)
        part = jnp.zeros((128, FEAT), F32)
        for v in range(2):
            at = (pl.ds(k0, 128), slice(None))
            g = (e_buf[(v,) + at] * a_v[v] - t_buf[(1 - v,) + at] * b_v[v]).astype(BF16)
            part = part + mm(g, q16[v])
        kg_src[slot] = part

    ahead = lambda j: lax.rem(y + j, NY)
    up1, up2, down1, down2 = (dev(y=ahead(j)) for j in (1, 2, 7, 6))
    key_part(4, ahead(4))
    remote(kg_src.at[4, pl.ds(0, 64)], kg_half.at[0], kg_ssem.at[0], kg_rsem.at[0], up2).start()
    remote(kg_src.at[4, pl.ds(64, 64)], kg_half.at[1], kg_ssem.at[1], kg_rsem.at[1], down2).start()
    key_part(3, ahead(3))
    remote(kg_src.at[3], kg_fwd.at[0], kg_ssem.at[2], kg_rsem.at[2], up1).start()
    key_part(5, ahead(5))
    remote(kg_src.at[5], kg_fwd.at[1], kg_ssem.at[3], kg_rsem.at[3], down1).start()
    key_part(2, ahead(2))
    key_part(6, ahead(6))
    key_part(1, ahead(1))
    remote(kg_src.at[1], kg_y.at[0], kg_ssem.at[4], kg_rsem.at[4], up1).start()
    key_part(7, ahead(7))
    remote(kg_src.at[7], kg_y.at[1], kg_ssem.at[5], kg_rsem.at[5], down1).start()
    key_part(0, y)

    q_z(1, 0)
    q_z(1, 1)

    shared = cross_sum[0]()
    terms = jnp.zeros((1, 512), F32)
    for v in range(2):
        x_row = shared[:, v * 512 : v * 512 + 512]
        terms = terms + 0.5 * weight * (jnp.log(tot_v[v]) - 10.0 * last_v[1 - v] * x_row)
    l_y[y] = terms[:, 0:128] + terms[:, 128:256] + terms[:, 256:384] + terms[:, 384:512]
    for to in y_ids:
        remote(l_y.at[y], l_y.at[y], l_ssem.at[2], l_rsem.at[2], to).start()

    got(kg_fwd.at[0], kg_rsem.at[2])
    got(kg_half.at[0], kg_rsem.at[0])
    kg_src[2, pl.ds(0, 64)] = kg_src[2, pl.ds(0, 64)] + kg_fwd[0, pl.ds(0, 64)] + kg_half[0]
    kg_src[2, pl.ds(64, 64)] = kg_src[2, pl.ds(64, 64)] + kg_fwd[0, pl.ds(64, 64)]
    remote(kg_src.at[2], kg_y.at[2], kg_ssem.at[6], kg_rsem.at[6], up2).start()
    got(kg_fwd.at[1], kg_rsem.at[3])
    got(kg_half.at[1], kg_rsem.at[1])
    kg_src[6, pl.ds(0, 64)] = kg_src[6, pl.ds(0, 64)] + kg_fwd[1, pl.ds(0, 64)]
    kg_src[6, pl.ds(64, 64)] = kg_src[6, pl.ds(64, 64)] + kg_fwd[1, pl.ds(64, 64)] + kg_half[1]
    remote(kg_src.at[6], kg_y.at[3], kg_ssem.at[7], kg_rsem.at[7], down2).start()

    at = pl.ds(pl.multiple_of(zl * 128, 128), 128)
    for h in range(2):
        part = ab_rows[0, c, :, at] * q_end(0, h) - ab_rows[1, c, :, at] * q_end(1, h)
        feats = pl.ds(pl.multiple_of(x * 32 + h * 16, 16), 16)
        mine = fin.at[c, feats]
        fin[c, feats] = part
        for to in xc_ids:
            remote(mine, mine, fin_ssem.at[h], fin_rsem.at[h], to).start()

    part = kg_src[0]
    for i, k in ((0, 4), (1, 5), (2, 6), (3, 7)):
        got(kg_y.at[i], kg_rsem.at[k])
        part = part + kg_y[i]
    own = pl.multiple_of((y * 8 + zl * NC + c) * 128, 128)
    pgrad_ref[...] = unit_back(kraw[pl.ds(own, 128)].astype(F32), part)

    for h in range(2):
        got(w_rcv.at[0, h], fin_rsem.at[h])
    for v in range(2):
        qt[v] = fin[v].T
    for v in range(2):
        grad = qt[v, pl.ds(pl.multiple_of(c * 64, 64), 64)]
        view_ref[v] = unit_back(pooled[pl.ds(v * 64, 64)], grad)

    got(l_y.at[pl.ds(0, 7)], l_rsem.at[2])
    loss_ref[...] = jnp.sum(add_slots(l_y), axis=1, keepdims=True) * (1.0 / WINDOWS)

    sent(qg.at[0, pl.ds(0, 3)], g_ssem)
    sent(qg.at[0], gs_ssem)
    for it in range(3):
        sent(a_c.at[it], a_ssem.at[it, 0])
        sent(a_pl.at[it, pl.ds(0, NP)], a_ssem.at[it, 1])
    for it in range(3):
        sent(b_y.at[it], b_ssem.at[it])
    sent(r_two.at[0], r_ssem.at[0])
    sent(r_pl.at[pl.ds(0, NP)], r_ssem.at[1])
    sent(cnt_y, cnt_ssem)
    for i in range(2):
        sent(kg_half.at[i], kg_ssem.at[i])
        sent(kg_fwd.at[i], kg_ssem.at[2 + i])
        sent(kg_y.at[i], kg_ssem.at[4 + i])
        sent(kg_y.at[2 + i], kg_ssem.at[6 + i])
        sent(c_rcv.at[i], f_ssem.at[i, 0])
        for h in range(2):
            sent(x_rcv.at[i, h], f_ssem.at[i, 1 + h])
            sent(w_rcv.at[i, h], f_ssem.at[i, 3 + h])
        sent(w_rcv.at[0, i], fin_ssem.at[i])
    sent(x_c, l_ssem.at[0])
    sent(x_pl.at[pl.ds(0, NP)], l_ssem.at[1])
    sent(l_y.at[pl.ds(0, 7)], l_ssem.at[2])


def hand_on(view_in, pgrad_in, loss_in, view_ref, pgrad_ref, loss_ref):
    view_ref[...] = view_in[...]
    pgrad_ref[...] = pgrad_in[...]
    loss_ref[...] = loss_in[...]


def on_device(tokens, offsets, species, prototypes):
    vmem = pltpu.VMEM
    dma = pltpu.SemaphoreType.DMA
    anywhere = pl.BlockSpec(memory_space=pl.ANY)
    inside = pl.BlockSpec(memory_space=pltpu.VMEM)
    scratch = [
        vmem((64 * SEQ, FEAT), BF16),
        vmem((128, 64 * SEQ), BF16),
        vmem((8192, FEAT), BF16),
        vmem((8192, FEAT), BF16),
        vmem((1024, FEAT), BF16),
        vmem((FEAT, 2048), BF16),
        vmem((128, FEAT), F32),
        vmem((2, 4, 136, FEAT), F32),
        vmem((2, 512, FEAT), BF16),
        vmem((2, 1024, 512), F32),
        vmem((2, 1024, 512), F32),
        vmem((2, 1024, 512), BF16),
        vmem((2, 512, 1024), BF16),
        vmem((2, 1024, 512), F32),
        vmem((2048, 512), BF16),
        vmem((3, 1, 1024), F32),
        vmem((3, 1, 1024), F32),
        vmem((3, NP + 1, 1, 1024), F32),
        vmem((3, 1, 2048), F32),
        vmem((3, 7, 1, 2048), F32),
        vmem((2, 1, 256), F32),
        vmem((NP + 1, 2, 1, 256), F32),
        vmem((NGROUP, 128), F32),
        vmem((7, NGROUP, 128), F32),
        vmem((8, 128, FEAT), F32),
        vmem((2, 64, FEAT), F32),
        vmem((2, 128, FEAT), F32),
        vmem((4, 128, FEAT), F32),
        vmem((2, FEAT, 512), F32),
        vmem((2, FEAT, 512), F32),
        vmem((2, FEAT, 512), F32),
        vmem((2, 2, 3, 16, 512), F32),
        vmem((2, 2, 4, 16, 128), F32),
        vmem((2, 2, 7, 16, 128), F32),
        vmem((2, FEAT, 128), F32),
        vmem((8, 1, 128), F32),
        vmem((1, 1024), F32),
        vmem((1, 1024), F32),
        vmem((NP + 1, 1, 1024), F32),
        vmem((1, 2048), F32),
        vmem((2, 2, 1, 512), F32),
        vmem((2, 128, FEAT), F32),
        dma((2,)),
        dma, dma((3,)), dma, dma((4,)),
        dma((3, 2)), dma((3, 2)), dma((3,)), dma((3,)), dma((2,)), dma((2,)), dma, dma,
        dma((8,)), dma((8,)), dma((2, 5)), dma((2, 5)), dma((2,)), dma((2,)), dma((3,)), dma((3,)),
    ]
    view_grads, proto_grads, loss = pl.pallas_call(
        kernel,
        out_shape=(
            jax.ShapeDtypeStruct((2, 64, FEAT), F32),
            jax.ShapeDtypeStruct((128, FEAT), F32),
            jax.ShapeDtypeStruct((1, 1), F32),
        ),
        in_specs=[anywhere, inside, inside, anywhere],
        out_specs=(inside, inside, inside),
        scratch_shapes=scratch,
        compiler_params=pltpu.CompilerParams(
            collective_id=0, has_side_effects=True, vmem_limit_bytes=56 * 2**20
        ),
        name="swav_step",
    )(
        tokens.reshape(64 * SEQ, FEAT),
        offsets,
        species.reshape(1, 64),
        prototypes,
    )
    view_grads, proto_grads, loss = pl.pallas_call(
        hand_on,
        out_shape=(
            jax.ShapeDtypeStruct((2, 64, FEAT), F32),
            jax.ShapeDtypeStruct((128, FEAT), F32),
            jax.ShapeDtypeStruct((1, 1), F32),
        ),
        in_specs=[inside] * 3,
        out_specs=(inside, inside, inside),
        compiler_params=pltpu.CompilerParams(vmem_limit_bytes=60 * 2**20),
        name="results",
    )(view_grads, proto_grads, loss)
    return view_grads, proto_grads, loss.reshape(())


def solution(mesh):
    return jax.shard_map(
        on_device,
        mesh=mesh,
        in_specs=(P("dp", None, None), P(None, "dp"), P("dp"), P("proto", None)),
        out_specs=(P(None, "dp", None), P(("proto", "dp"), None), P()),
        check_vma=False,
    )
```

```python
import math

import jax
import jax.numpy as jnp
from jax import lax
from jax.experimental import pallas as pl
from jax.experimental.pallas import tpu as pltpu
from jax.sharding import PartitionSpec as P

MESH = pl.DeviceIdType.MESH
F32 = jnp.float32
BF16 = jnp.bfloat16
NGROUP = 16
CROP = 24
SEQ = 32
FEAT = 128
WINDOWS = 4096
PROTOS = 65536
EPS = 1e-6
NY, NZL, NC, NZH, NX = 8, 4, 2, 2, 4
NZ = NZH * NZL
RING8 = (4, 3, 5, 2, 6, 1, 7)
XC = ((2, 0), (2, 1), (1, 0), (3, 0), (1, 1), (3, 1), (0, 1))
RING4 = (2, 1, 3)
PLANE = tuple(
    sorted(
        ((dx, dz) for dx in range(NX) for dz in range(NZ) if dx or dz),
        key=lambda o: -(min(o[0], NX - o[0]) + min(o[1], NZ - o[1])),
    )
)
NP = len(PLANE)
NT = (((1,), (1,)), ((), ()))
NN = (((1,), (0,)), ((), ()))


def mm(a, b, dims=NN):
    return lax.dot_general(a, b, dims, preferred_element_type=F32)


def split3(row, count=16):
    hi = row.astype(BF16).astype(F32)
    rest = row - hi
    mid = rest.astype(BF16).astype(F32)
    lo = rest - mid
    width = row.shape[1]
    at = lax.broadcasted_iota(jnp.int32, (count, width), 0)
    full = lambda r: jnp.broadcast_to(r, (count, width))
    out = jnp.where(at == 0, full(hi), jnp.where(at == 1, full(mid), jnp.where(at == 2, full(lo), 0.0)))
    return out.astype(BF16)


def unit_scale(rows):
    return lax.rsqrt(jnp.mean(rows * rows, axis=-1, keepdims=True) + EPS)


def unit_back(rows, grad):
    scale = unit_scale(rows)
    along = jnp.mean(rows * grad, axis=-1, keepdims=True)
    return (grad - rows * (along * scale * scale)) * (scale / math.sqrt(FEAT))


def kernel(
    tok_ref, off_ref, spec_ref, proto_ref,
    view_ref, pgrad_ref, loss_ref,
    tok, mask, kraw, kunit, keys, keys_t, pooled, qg, q16, s_buf, e_buf, k_buf, kt_buf, t_buf, two,
    a_src, a_c, a_pl, b_src, b_y, r_two, r_pl, cnt_src, cnt_y,
    kg_src, kg_half, kg_fwd, kg_y, c_src, c_rcv, x_src, x_rcv, w_src, w_rcv, fin, l_y,
    x_own, x_c, x_pl, p_row, ab_rows, qt,
    load_sem, g_ssem, g_rsem, gs_ssem, gs_rsem,
    a_ssem, a_rsem, b_ssem, b_rsem, r_ssem, r_rsem, cnt_ssem, cnt_rsem,
    kg_ssem, kg_rsem, f_ssem, f_rsem, fin_ssem, fin_rsem, l_ssem, l_rsem,
):
    dp = lax.axis_index("dp")
    pr = lax.axis_index("proto")
    y, zl, c = lax.div(dp, 8), lax.rem(lax.div(dp, 2), 4), lax.rem(dp, 2)
    zh, x = lax.div(pr, 4), lax.rem(pr, 4)
    z = zh * NZL + zl

    def dev(y=y, z=z, c=c, x=x):
        return ((y * NZL + lax.rem(z, NZL)) * NC + c, lax.div(z, NZL) * NX + x)

    xc_ids = [dev(x=lax.rem(x + dx, NX), c=lax.rem(c + dc, NC)) for dx, dc in XC]
    z_of = [lax.rem(z + j, NZ) for j in RING8]
    z_ids = [dev(z=k) for k in z_of]
    y_of = [lax.rem(y + j, NY) for j in RING8]
    y_ids = [dev(y=k) for k in y_of]
    x_of = [lax.rem(x + j, NX) for j in RING4]
    x_ids = [dev(x=k) for k in x_of]
    sib = dev(c=1 - c)
    plane_ids = [dev(x=lax.rem(x + dx, NX), z=lax.rem(z + dz, NZ)) for dx, dz in PLANE]
    step2 = 2 + 4 * c
    near = [lax.rem(z + step, NZ) for step in (step2, 1, 7)]
    near_ids = [dev(z=k) for k in near]
    here = z * NX + x
    cross_ids = [xc_ids[i] for i in range(7) if XC[i][0] and XC[i][1]]

    def remote(src, dst, ssem, rsem, to):
        return pltpu.make_async_remote_copy(
            src_ref=src, dst_ref=dst, send_sem=ssem, recv_sem=rsem, device_id=to, device_id_type=MESH
        )

    def got(ref, sem):
        remote(ref, ref, sem, sem, sib).wait_recv()

    def sent(ref, sem):
        remote(ref, ref, sem, sem, sib).wait_send()

    barrier = pltpu.get_barrier_semaphore()
    load_tok = pltpu.make_async_copy(tok_ref, tok, load_sem.at[0])
    load_key = pltpu.make_async_copy(proto_ref, kraw, load_sem.at[1])
    load_tok.start()
    load_key.start()
    for to in plane_ids + y_ids + cross_ids + [sib]:
        pl.semaphore_signal(barrier, inc=1, device_id=to, device_id_type=MESH)

    off = off_ref[...].astype(F32)
    off_row = jnp.concatenate([off[0:1], off[1:2]], axis=1)
    lane = lax.broadcasted_iota(jnp.int32, (128, 128), 1)
    first = jnp.broadcast_to(off_row, (128, 128)).T.astype(jnp.int32)
    row = lax.broadcasted_iota(jnp.int32, (128, 128), 0)
    first = first + (row & 63) * SEQ
    for part in range(16):
        col = part * 128
        inside = (lane + col >= first) & (lane + col < first + CROP)
        mask[:, pl.ds(col, 128)] = jnp.where(inside, 1.0, 0.0).astype(BF16)
    load_tok.wait()
    total = mm(mask[...], tok[...])
    rows = total / CROP
    pooled[...] = rows
    query = (rows * unit_scale(rows) / math.sqrt(FEAT)).astype(BF16)
    qg[c, zl, pl.ds(0, 128)] = query.astype(F32)
    spec = spec_ref[...].astype(F32)
    both = jnp.concatenate([spec, spec], axis=1)
    half = lax.broadcasted_iota(jnp.int32, (8, 128), 1) // 64
    qg[c, zl, pl.ds(128, 8)] = jnp.where(half == c, jnp.broadcast_to(both, (8, 128)), 0.0)

    load_key.wait()

    def whole(i, sums):
        at = pl.ds(pl.multiple_of(i * 4096, 4096), 4096)
        raw = kraw[at].astype(F32)
        unit = (raw * (unit_scale(raw) * (1.0 / math.sqrt(FEAT)))).astype(BF16)
        kunit[at] = unit
        e = jnp.exp(mm(unit, query, NT) * 10.0)
        k = (e * e).astype(BF16).astype(F32)
        fold = lambda a: jnp.sum(a.reshape(512, 8, 128), axis=0)
        return sums[0] + fold(k), sums[1] + fold(e)

    zero = jnp.zeros((8, 128), F32)
    ks, es = lax.fori_loop(0, 2, whole, (zero, zero))
    r_two[c, :, pl.ds(0, 128)] = jnp.sum(ks, axis=0, keepdims=True)
    r_two[c, :, pl.ds(128, 128)] = jnp.sum(es, axis=0, keepdims=True)

    pl.semaphore_wait(barrier, 11 + NP)
    remote(r_two.at[c], r_two.at[c], r_ssem.at[0], r_rsem.at[0], sib).start()

    mine = qg.at[c, zl]
    for i, to in enumerate(near_ids):
        remote(mine, mine, g_ssem, g_rsem.at[i], to).start()
    remote(mine, mine, gs_ssem, gs_rsem.at[0], sib).start()

    got(r_two.at[1 - c], r_rsem.at[0])
    r_pl[here] = r_two[...]
    for to in plane_ids:
        remote(r_pl.at[here], r_pl.at[here], r_ssem.at[1], r_rsem.at[1], to).start()

    for i in range(8):
        block = kunit[pl.ds(pl.multiple_of((i * 8 + zl * NC + c) * 128, 128), 128)]
        keys[pl.ds(i * 128, 128)] = block
        turned = block.astype(F32).T.astype(BF16)
        keys_t[:, pl.ds(i * 128, 128)] = turned
        keys_t[:, pl.ds(1024 + i * 128, 128)] = turned

    def scores(zp):
        zp128 = pl.multiple_of(zp * 128, 128)
        pair = []
        for v in range(2):
            q = jnp.concatenate([qg[0, zp, pl.ds(v * 64, 64)], qg[1, zp, pl.ds(v * 64, 64)]], axis=0).astype(BF16)
            q16[v, pl.ds(zp128, 128)] = q
            pair.append(q)
        rhs = jnp.concatenate(pair, axis=0)

        out = mm(keys[...], rhs, NT)
        e = jnp.exp(out * 10.0)
        k = (e * e).astype(BF16)
        for v in range(2):
            at = (v, slice(None), pl.ds(zp128, 128))
            s_buf[at] = out[:, v * 128 : v * 128 + 128]
            e_buf[at] = e[:, v * 128 : v * 128 + 128]
            k_buf[at] = k[:, v * 128 : v * 128 + 128]

    got(qg.at[1 - c, zl], gs_rsem.at[0])
    scores(zl)

    steps = ((1, 3), (2, 1), (0, 2))
    for i, step in steps:
        piece = qg.at[c, lax.rem(zl + step, NZL)]
        got(piece, g_rsem.at[i])
        remote(piece, piece, gs_ssem, gs_rsem.at[i + 1], sib).start()
    for i, step in steps:
        zp = lax.rem(zl + step, NZL)
        got(qg.at[1 - c, zp], gs_rsem.at[i + 1])
        scores(zp)

    got(r_pl.at[pl.ds(0, NP)], r_rsem.at[1])
    pairs = []
    for j in range(NZL):
        part = None
        for i in range(NZ * NX):
            if (i // NX) % NZL == j:
                part = r_pl[i] if part is None else part + r_pl[i]
        pairs.append(part)

    def assemble(base):
        tiles = []
        for v in range(2):
            at = base + v * 64
            for j in range(NZL):
                tiles += [pairs[j][0][:, at : at + 64], pairs[j][1][:, at : at + 64]]
        return jnp.concatenate(tiles, axis=1)

    window_scale = PROTOS / assemble(0)
    totals = assemble(128)

    spec_row = jnp.concatenate([qg[0, i, pl.ds(128, 1)] + qg[1, i, pl.ds(128, 1)] for i in range(4)], axis=1)
    group = lax.broadcasted_iota(jnp.int32, (NGROUP, 512), 0)
    onehot = jnp.where(group == jnp.broadcast_to(spec_row, (NGROUP, 512)).astype(jnp.int32), 1.0, 0.0)

    def plane_sum(own, slots, ssem, rsem, between):
        slots[here] = own
        for to in plane_ids:
            remote(slots.at[here], slots.at[here], ssem, rsem, to).start()
        between()

        def result():
            got(slots.at[pl.ds(0, NP)], rsem)
            part = slots[0]
            for i in range(1, NP + 1):
                part = part + slots[i]
            return part

        return result

    def nothing():
        pass

    def a_sum(it, between_1=nothing, between_2=nothing):
        remote(a_src.at[it], a_c.at[it], a_ssem.at[it, 0], a_rsem.at[it, 0], sib).start()
        between_1()
        got(a_c.at[it], a_rsem.at[it, 0])
        part = a_src[it] + a_c[it]
        return plane_sum(part, a_pl.at[it], a_ssem.at[it, 1], a_rsem.at[it, 1], between_2)()

    def b_sum(it, between=None):
        for i, to in enumerate(y_ids):
            remote(b_src.at[it], b_y.at[it, i], b_ssem.at[it], b_rsem.at[it], to).start()
        if between is not None:
            between()
        got(b_y.at[it], b_rsem.at[it])
        part = b_src[it]
        for i in range(7):
            part = part + b_y[it, i]
        return part

    def send_counts():
        cnt_src[...] = jnp.broadcast_to(jnp.sum(onehot, axis=1, keepdims=True), (NGROUP, 128))
        for i, to in enumerate(y_ids):
            remote(cnt_src, cnt_y.at[i], cnt_ssem, cnt_rsem, to).start()

    def halves(value, k0, width):
        hi = value.astype(BF16)
        two[pl.ds(k0, width)] = hi
        two[pl.ds(1024 + k0, width)] = (value - hi.astype(F32)).astype(BF16)

    def split_e(v):
        def block(kb, carry):
            k0 = pl.multiple_of(kb * 32, 32)
            halves(e_buf[v, pl.ds(k0, 32)], k0, 32)
            return carry

        lax.fori_loop(0, 32, block, 0)

    def split_t(v):
        for i in range(8):
            p = p_row[:, pl.ds(pl.multiple_of(v * 1024 + i * 128, 128), 128)]
            col = jnp.broadcast_to(p, (128, 128)).T
            t = k_buf[v, pl.ds(i * 128, 128)].astype(F32) * jnp.concatenate([col] * 4, axis=1)
            t_buf[v, pl.ds(i * 128, 128)] = t
            halves(t, i * 128, 128)

    def q_theirs(step):
        theirs = 1 - c if step == 0 else c
        (split_e, split_t)[step](theirs)
        c_src[step] = mm(keys_t[...], two[...])
        remote(c_src.at[step], c_rcv.at[step], f_ssem.at[step, 0], f_rsem.at[step, 0], sib).start()

    def q_own(step):
        (split_e, split_t)[step](c if step == 0 else 1 - c)
        x_src[step] = mm(keys_t[...], two[...])

    def q_x(step):
        got(c_rcv.at[step], f_rsem.at[step, 0])
        x_src[step] = x_src[step] + c_rcv[step]
        for h in range(2):
            for i, xx in enumerate(x_of):
                piece = x_src.at[step, pl.ds(pl.multiple_of(xx * 32 + h * 16, 16), 16)]
                remote(piece, x_rcv.at[step, h, i], f_ssem.at[step, 1 + h], f_rsem.at[step, 1 + h], x_ids[i]).start()

    def q_z(step, h):
        got(x_rcv.at[step, h], f_rsem.at[step, 1 + h])
        part = x_src[step, pl.ds(pl.multiple_of(x * 32 + h * 16, 16), 16)]
        for i in range(3):
            part = part + x_rcv[step, h, i]
        for i in range(4):
            w_src[step, h, i] = part[:, i * 128 : i * 128 + 128]
        for i, to in enumerate(z_ids):
            piece = w_src.at[step, h, lax.rem(z_of[i], NZL)]
            remote(piece, w_rcv.at[step, h, i], f_ssem.at[step, 3 + h], f_rsem.at[step, 3 + h], to).start()

    def q_end(step, h):
        got(w_rcv.at[step, h], f_rsem.at[step, 3 + h])
        part = w_src[step, h, zl]
        for i in range(7):
            part = part + w_rcv[step, h, i]
        return part

    def columns(it, scale):
        for v in range(2):
            parts = split3(scale[:, v * 512 : v * 512 + 512])
            out = mm(parts, k_buf[v], NT) if it == 0 else mm(parts, kt_buf[v])
            b_src[it, :, pl.ds(v * 1024, 1024)] = jnp.sum(out, axis=0, keepdims=True)

    def row_sums(it, scale):
        for v in range(2):
            out = mm(split3(scale[:, v * 1024 : v * 1024 + 1024]), k_buf[v])
            a_src[it, :, pl.ds(v * 512, 512)] = jnp.sum(out, axis=0, keepdims=True)

    def both_z():
        q_z(0, 0)
        q_z(0, 1)

    def beside_a0():
        send_counts()
        q_theirs(0)
        q_own(0)

    def turn():
        for v in range(2):
            kt_buf[v] = k_buf[v].T

    columns(0, window_scale)
    proto_scale = 1.0 / (PROTOS * b_sum(0, turn))
    row_sums(0, proto_scale)
    window_scale = 1.0 / a_sum(0, nothing, beside_a0)
    columns(1, window_scale)
    proto_scale = 1.0 / (PROTOS * b_sum(1, lambda: q_x(0)))
    row_sums(1, proto_scale)
    window_scale = 1.0 / a_sum(1)
    columns(2, window_scale)
    proto_scale = 1.0 / (PROTOS * b_sum(2, both_z))
    row_sums(2, proto_scale)
    p_row[...] = proto_scale

    def cross():
        for v in range(2):

            def block(kb, acc):
                k0 = pl.multiple_of(kb * 32, 32)
                prod = t_buf[1 - v, pl.ds(k0, 32)] * s_buf[v, pl.ds(k0, 32)]
                return acc + jnp.sum(prod.reshape(4, 8, 512), axis=0)

            acc = lax.fori_loop(0, 32, block, jnp.zeros((8, 512), F32))
            x_own[:, pl.ds(v * 512, 512)] = jnp.sum(acc, axis=0, keepdims=True)

    def beside_a2():
        q_own(1)
        q_x(1)
        cross()
        remote(x_own, x_c, l_ssem.at[0], l_rsem.at[0], sib).start()
        got(x_c, l_rsem.at[0])
        cross_sum.append(plane_sum(x_own[...] + x_c[...], x_pl, l_ssem.at[1], l_rsem.at[1], nothing))

    cross_sum = []
    last = 1.0 / a_sum(2, lambda: q_theirs(1), beside_a2)

    got(cnt_y, cnt_rsem)
    counts = cnt_src[...]
    for i in range(7):
        counts = counts + cnt_y[i]
    seen = jnp.sum(onehot * jnp.concatenate([counts] * 4, axis=1), axis=0, keepdims=True)
    weight = WINDOWS / (NGROUP * seen)
    last_v = [last[:, 0:512], last[:, 512:1024]]
    tot_v = [totals[:, 0:512], totals[:, 512:1024]]
    a_v = [5.0 * weight / tot_v[v] for v in range(2)]
    b_v = [5.0 * weight * last_v[1 - v] for v in range(2)]
    for v in range(2):
        ab_rows[0, v] = a_v[v]
        ab_rows[1, v] = b_v[v]
    def add_slots(ref):
        out = ref[0]
        for i in range(1, 8):
            out = out + ref[i]
        return out

    def key_part(slot, yy):
        k0 = pl.multiple_of(yy * 128, 128)
        part = jnp.zeros((128, FEAT), F32)
        for v in range(2):
            at = (pl.ds(k0, 128), slice(None))
            g = (e_buf[(v,) + at] * a_v[v] - t_buf[(1 - v,) + at] * b_v[v]).astype(BF16)
            part = part + mm(g, q16[v])
        kg_src[slot] = part

    ahead = lambda j: lax.rem(y + j, NY)
    up1, up2, down1, down2 = (dev(y=ahead(j)) for j in (1, 2, 7, 6))
    key_part(4, ahead(4))
    remote(kg_src.at[4, pl.ds(0, 64)], kg_half.at[0], kg_ssem.at[0], kg_rsem.at[0], up2).start()
    remote(kg_src.at[4, pl.ds(64, 64)], kg_half.at[1], kg_ssem.at[1], kg_rsem.at[1], down2).start()
    key_part(3, ahead(3))
    remote(kg_src.at[3], kg_fwd.at[0], kg_ssem.at[2], kg_rsem.at[2], up1).start()
    key_part(5, ahead(5))
    remote(kg_src.at[5], kg_fwd.at[1], kg_ssem.at[3], kg_rsem.at[3], down1).start()
    key_part(2, ahead(2))
    key_part(6, ahead(6))
    key_part(1, ahead(1))
    remote(kg_src.at[1], kg_y.at[0], kg_ssem.at[4], kg_rsem.at[4], up1).start()
    key_part(7, ahead(7))
    remote(kg_src.at[7], kg_y.at[1], kg_ssem.at[5], kg_rsem.at[5], down1).start()
    key_part(0, y)

    q_z(1, 0)
    q_z(1, 1)

    shared = cross_sum[0]()
    terms = jnp.zeros((1, 512), F32)
    for v in range(2):
        x_row = shared[:, v * 512 : v * 512 + 512]
        terms = terms + 0.5 * weight * (jnp.log(tot_v[v]) - 10.0 * last_v[1 - v] * x_row)
    l_y[y] = terms[:, 0:128] + terms[:, 128:256] + terms[:, 256:384] + terms[:, 384:512]
    for to in y_ids:
        remote(l_y.at[y], l_y.at[y], l_ssem.at[2], l_rsem.at[2], to).start()

    got(kg_fwd.at[0], kg_rsem.at[2])
    got(kg_half.at[0], kg_rsem.at[0])
    kg_src[2, pl.ds(0, 64)] = kg_src[2, pl.ds(0, 64)] + kg_fwd[0, pl.ds(0, 64)] + kg_half[0]
    kg_src[2, pl.ds(64, 64)] = kg_src[2, pl.ds(64, 64)] + kg_fwd[0, pl.ds(64, 64)]
    remote(kg_src.at[2], kg_y.at[2], kg_ssem.at[6], kg_rsem.at[6], up2).start()
    got(kg_fwd.at[1], kg_rsem.at[3])
    got(kg_half.at[1], kg_rsem.at[1])
    kg_src[6, pl.ds(0, 64)] = kg_src[6, pl.ds(0, 64)] + kg_fwd[1, pl.ds(0, 64)]
    kg_src[6, pl.ds(64, 64)] = kg_src[6, pl.ds(64, 64)] + kg_fwd[1, pl.ds(64, 64)] + kg_half[1]
    remote(kg_src.at[6], kg_y.at[3], kg_ssem.at[7], kg_rsem.at[7], down2).start()

    at = pl.ds(pl.multiple_of(zl * 128, 128), 128)
    for h in range(2):
        part = ab_rows[0, c, :, at] * q_end(0, h) - ab_rows[1, c, :, at] * q_end(1, h)
        feats = pl.ds(pl.multiple_of(x * 32 + h * 16, 16), 16)
        mine = fin.at[c, feats]
        fin[c, feats] = part
        for to in xc_ids:
            remote(mine, mine, fin_ssem.at[h], fin_rsem.at[h], to).start()

    part = kg_src[0]
    for i, k in ((0, 4), (1, 5), (2, 6), (3, 7)):
        got(kg_y.at[i], kg_rsem.at[k])
        part = part + kg_y[i]
    own = pl.multiple_of((y * 8 + zl * NC + c) * 128, 128)
    pgrad_ref[...] = unit_back(kraw[pl.ds(own, 128)].astype(F32), part)

    for h in range(2):
        got(w_rcv.at[0, h], fin_rsem.at[h])
    for v in range(2):
        qt[v] = fin[v].T
    for v in range(2):
        grad = qt[v, pl.ds(pl.multiple_of(c * 64, 64), 64)]
        view_ref[v] = unit_back(pooled[pl.ds(v * 64, 64)], grad)

    got(l_y.at[pl.ds(0, 7)], l_rsem.at[2])
    loss_ref[...] = jnp.sum(add_slots(l_y), axis=1, keepdims=True) * (1.0 / WINDOWS)

    sent(qg.at[0, pl.ds(0, 3)], g_ssem)
    sent(qg.at[0], gs_ssem)
    for it in range(3):
        sent(a_c.at[it], a_ssem.at[it, 0])
        sent(a_pl.at[it, pl.ds(0, NP)], a_ssem.at[it, 1])
    for it in range(3):
        sent(b_y.at[it], b_ssem.at[it])
    sent(r_two.at[0], r_ssem.at[0])
    sent(r_pl.at[pl.ds(0, NP)], r_ssem.at[1])
    sent(cnt_y, cnt_ssem)
    for i in range(2):
        sent(kg_half.at[i], kg_ssem.at[i])
        sent(kg_fwd.at[i], kg_ssem.at[2 + i])
        sent(kg_y.at[i], kg_ssem.at[4 + i])
        sent(kg_y.at[2 + i], kg_ssem.at[6 + i])
        sent(c_rcv.at[i], f_ssem.at[i, 0])
        for h in range(2):
            sent(x_rcv.at[i, h], f_ssem.at[i, 1 + h])
            sent(w_rcv.at[i, h], f_ssem.at[i, 3 + h])
        sent(w_rcv.at[0, i], fin_ssem.at[i])
    sent(x_c, l_ssem.at[0])
    sent(x_pl.at[pl.ds(0, NP)], l_ssem.at[1])
    sent(l_y.at[pl.ds(0, 7)], l_ssem.at[2])


def hand_on(view_in, pgrad_in, loss_in, view_ref, pgrad_ref, loss_ref):
    view_ref[...] = view_in[...]
    pgrad_ref[...] = pgrad_in[...]
    loss_ref[...] = loss_in[...]


def on_device(tokens, offsets, species, prototypes):
    vmem = pltpu.VMEM
    dma = pltpu.SemaphoreType.DMA
    anywhere = pl.BlockSpec(memory_space=pl.ANY)
    inside = pl.BlockSpec(memory_space=pltpu.VMEM)
    scratch = [
        vmem((64 * SEQ, FEAT), BF16),
        vmem((128, 64 * SEQ), BF16),
        vmem((8192, FEAT), BF16),
        vmem((8192, FEAT), BF16),
        vmem((1024, FEAT), BF16),
        vmem((FEAT, 2048), BF16),
        vmem((128, FEAT), F32),
        vmem((2, 4, 136, FEAT), F32),
        vmem((2, 512, FEAT), BF16),
        vmem((2, 1024, 512), F32),
        vmem((2, 1024, 512), F32),
        vmem((2, 1024, 512), BF16),
        vmem((2, 512, 1024), BF16),
        vmem((2, 1024, 512), F32),
        vmem((2048, 512), BF16),
        vmem((3, 1, 1024), F32),
        vmem((3, 1, 1024), F32),
        vmem((3, NP + 1, 1, 1024), F32),
        vmem((3, 1, 2048), F32),
        vmem((3, 7, 1, 2048), F32),
        vmem((2, 1, 256), F32),
        vmem((NP + 1, 2, 1, 256), F32),
        vmem((NGROUP, 128), F32),
        vmem((7, NGROUP, 128), F32),
        vmem((8, 128, FEAT), F32),
        vmem((2, 64, FEAT), F32),
        vmem((2, 128, FEAT), F32),
        vmem((4, 128, FEAT), F32),
        vmem((2, FEAT, 512), F32),
        vmem((2, FEAT, 512), F32),
        vmem((2, FEAT, 512), F32),
        vmem((2, 2, 3, 16, 512), F32),
        vmem((2, 2, 4, 16, 128), F32),
        vmem((2, 2, 7, 16, 128), F32),
        vmem((2, FEAT, 128), F32),
        vmem((8, 1, 128), F32),
        vmem((1, 1024), F32),
        vmem((1, 1024), F32),
        vmem((NP + 1, 1, 1024), F32),
        vmem((1, 2048), F32),
        vmem((2, 2, 1, 512), F32),
        vmem((2, 128, FEAT), F32),
        dma((2,)),
        dma, dma((3,)), dma, dma((4,)),
        dma((3, 2)), dma((3, 2)), dma((3,)), dma((3,)), dma((2,)), dma((2,)), dma, dma,
        dma((8,)), dma((8,)), dma((2, 5)), dma((2, 5)), dma((2,)), dma((2,)), dma((3,)), dma((3,)),
    ]
    view_grads, proto_grads, loss = pl.pallas_call(
        kernel,
        out_shape=(
            jax.ShapeDtypeStruct((2, 64, FEAT), F32),
            jax.ShapeDtypeStruct((128, FEAT), F32),
            jax.ShapeDtypeStruct((1, 1), F32),
        ),
        in_specs=[anywhere, inside, inside, anywhere],
        out_specs=(inside, inside, inside),
        scratch_shapes=scratch,
        compiler_params=pltpu.CompilerParams(
            collective_id=0, has_side_effects=True, vmem_limit_bytes=56 * 2**20
        ),
        name="swav_step",
    )(
        tokens.reshape(64 * SEQ, FEAT),
        offsets,
        species.reshape(1, 64),
        prototypes,
    )
    view_grads, proto_grads, loss = pl.pallas_call(
        hand_on,
        out_shape=(
            jax.ShapeDtypeStruct((2, 64, FEAT), F32),
            jax.ShapeDtypeStruct((128, FEAT), F32),
            jax.ShapeDtypeStruct((1, 1), F32),
        ),
        in_specs=[inside] * 3,
        out_specs=(inside, inside, inside),
        compiler_params=pltpu.CompilerParams(vmem_limit_bytes=60 * 2**20),
        name="results",
    )(view_grads, proto_grads, loss)
    return view_grads, proto_grads, loss.reshape(())


def solution(mesh):
    return jax.shard_map(
        on_device,
        mesh=mesh,
        in_specs=(P("dp", None, None), P(None, "dp"), P("dp"), P("proto", None)),
        out_specs=(P(None, "dp", None), P(("proto", "dp"), None), P()),
        check_vma=False,
    )
```

```python
import math

import jax
import jax.numpy as jnp
from jax import lax
from jax.experimental import pallas as pl
from jax.experimental.pallas import tpu as pltpu
from jax.sharding import PartitionSpec as P

MESH = pl.DeviceIdType.MESH
F32 = jnp.float32
BF16 = jnp.bfloat16
NGROUP = 16
CROP = 24
SEQ = 32
FEAT = 128
WINDOWS = 4096
PROTOS = 65536
EPS = 1e-6
NY, NZL, NC, NZH, NX = 8, 4, 2, 2, 4
NZ = NZH * NZL
RING8 = (4, 3, 5, 2, 6, 1, 7)
XC = ((2, 0), (2, 1), (1, 0), (3, 0), (1, 1), (3, 1), (0, 1))
RING4 = (2, 1, 3)
PLANE = tuple(
    sorted(
        ((dx, dz) for dx in range(NX) for dz in range(NZ) if dx or dz),
        key=lambda o: -(min(o[0], NX - o[0]) + min(o[1], NZ - o[1])),
    )
)
NP = len(PLANE)
NT = (((1,), (1,)), ((), ()))
NN = (((1,), (0,)), ((), ()))


def mm(a, b, dims=NN):
    return lax.dot_general(a, b, dims, preferred_element_type=F32)


def split3(row, count=16):
    hi = row.astype(BF16).astype(F32)
    rest = row - hi
    mid = rest.astype(BF16).astype(F32)
    lo = rest - mid
    width = row.shape[1]
    at = lax.broadcasted_iota(jnp.int32, (count, width), 0)
    full = lambda r: jnp.broadcast_to(r, (count, width))
    out = jnp.where(at == 0, full(hi), jnp.where(at == 1, full(mid), jnp.where(at == 2, full(lo), 0.0)))
    return out.astype(BF16)


def unit_scale(rows):
    return lax.rsqrt(jnp.mean(rows * rows, axis=-1, keepdims=True) + EPS)


def unit_back(rows, grad):
    scale = unit_scale(rows)
    along = jnp.mean(rows * grad, axis=-1, keepdims=True)
    return (grad - rows * (along * scale * scale)) * (scale / math.sqrt(FEAT))


def kernel(
    tok_ref, off_ref, spec_ref, proto_ref,
    view_ref, pgrad_ref, loss_ref,
    tok, mask, kraw, kunit, keys, keys_t, pooled, qg, q16, s_buf, e_buf, k_buf, kt_buf, t_buf, two,
    a_src, a_c, a_pl, b_src, b_y, r_two, r_pl, cnt_src, cnt_y,
    kg_src, kg_half, kg_fwd, kg_y, c_src, c_rcv, x_src, x_rcv, w_src, w_rcv, fin, l_y,
    x_own, x_c, x_pl, p_row, ab_rows, qt,
    load_sem, g_ssem, g_rsem, gs_ssem, gs_rsem,
    a_ssem, a_rsem, b_ssem, b_rsem, r_ssem, r_rsem, cnt_ssem, cnt_rsem,
    kg_ssem, kg_rsem, f_ssem, f_rsem, fin_ssem, fin_rsem, l_ssem, l_rsem,
):
    dp = lax.axis_index("dp")
    pr = lax.axis_index("proto")
    y, zl, c = lax.div(dp, 8), lax.rem(lax.div(dp, 2), 4), lax.rem(dp, 2)
    zh, x = lax.div(pr, 4), lax.rem(pr, 4)
    z = zh * NZL + zl

    def dev(y=y, z=z, c=c, x=x):
        return ((y * NZL + lax.rem(z, NZL)) * NC + c, lax.div(z, NZL) * NX + x)

    xc_ids = [dev(x=lax.rem(x + dx, NX), c=lax.rem(c + dc, NC)) for dx, dc in XC]
    z_of = [lax.rem(z + j, NZ) for j in RING8]
    z_ids = [dev(z=k) for k in z_of]
    y_of = [lax.rem(y + j, NY) for j in RING8]
    y_ids = [dev(y=k) for k in y_of]
    x_of = [lax.rem(x + j, NX) for j in RING4]
    x_ids = [dev(x=k) for k in x_of]
    sib = dev(c=1 - c)
    plane_ids = [dev(x=lax.rem(x + dx, NX), z=lax.rem(z + dz, NZ)) for dx, dz in PLANE]
    step2 = 2 + 4 * c
    near = [lax.rem(z + step, NZ) for step in (step2, 1, 7)]
    near_ids = [dev(z=k) for k in near]
    here = z * NX + x
    cross_ids = [xc_ids[i] for i in range(7) if XC[i][0] and XC[i][1]]

    def remote(src, dst, ssem, rsem, to):
        return pltpu.make_async_remote_copy(
            src_ref=src, dst_ref=dst, send_sem=ssem, recv_sem=rsem, device_id=to, device_id_type=MESH
        )

    def got(ref, sem):
        remote(ref, ref, sem, sem, sib).wait_recv()

    def sent(ref, sem):
        remote(ref, ref, sem, sem, sib).wait_send()

    barrier = pltpu.get_barrier_semaphore()
    load_tok = pltpu.make_async_copy(tok_ref, tok, load_sem.at[0])
    load_key = pltpu.make_async_copy(proto_ref, kraw, load_sem.at[1])
    load_tok.start()
    load_key.start()
    for to in plane_ids + y_ids + cross_ids + [sib]:
        pl.semaphore_signal(barrier, inc=1, device_id=to, device_id_type=MESH)

    off = off_ref[...].astype(F32)
    off_row = jnp.concatenate([off[0:1], off[1:2]], axis=1)
    lane = lax.broadcasted_iota(jnp.int32, (128, 128), 1)
    first = jnp.broadcast_to(off_row, (128, 128)).T.astype(jnp.int32)
    row = lax.broadcasted_iota(jnp.int32, (128, 128), 0)
    first = first + (row & 63) * SEQ
    for part in range(16):
        col = part * 128
        inside = (lane + col >= first) & (lane + col < first + CROP)
        mask[:, pl.ds(col, 128)] = jnp.where(inside, 1.0, 0.0).astype(BF16)
    load_tok.wait()
    total = mm(mask[...], tok[...])
    rows = total / CROP
    pooled[...] = rows
    query = (rows * unit_scale(rows) / math.sqrt(FEAT)).astype(BF16)
    qg[c, zl, pl.ds(0, 128)] = query.astype(F32)
    spec = spec_ref[...].astype(F32)
    both = jnp.concatenate([spec, spec], axis=1)
    half = lax.broadcasted_iota(jnp.int32, (8, 128), 1) // 64
    qg[c, zl, pl.ds(128, 8)] = jnp.where(half == c, jnp.broadcast_to(both, (8, 128)), 0.0)

    load_key.wait()

    def whole(i, sums):
        at = pl.ds(pl.multiple_of(i * 4096, 4096), 4096)
        raw = kraw[at].astype(F32)
        unit = (raw * (unit_scale(raw) * (1.0 / math.sqrt(FEAT)))).astype(BF16)
        kunit[at] = unit
        e = jnp.exp(mm(unit, query, NT) * 10.0)
        k = (e * e).astype(BF16).astype(F32)
        fold = lambda a: jnp.sum(a.reshape(512, 8, 128), axis=0)
        return sums[0] + fold(k), sums[1] + fold(e)

    zero = jnp.zeros((8, 128), F32)
    ks, es = lax.fori_loop(0, 2, whole, (zero, zero))
    r_two[c, :, pl.ds(0, 128)] = jnp.sum(ks, axis=0, keepdims=True)
    r_two[c, :, pl.ds(128, 128)] = jnp.sum(es, axis=0, keepdims=True)

    pl.semaphore_wait(barrier, 11 + NP)
    remote(r_two.at[c], r_two.at[c], r_ssem.at[0], r_rsem.at[0], sib).start()

    mine = qg.at[c, zl]
    for i, to in enumerate(near_ids):
        remote(mine, mine, g_ssem, g_rsem.at[i], to).start()
    remote(mine, mine, gs_ssem, gs_rsem.at[0], sib).start()

    got(r_two.at[1 - c], r_rsem.at[0])
    r_pl[here] = r_two[...]
    for to in plane_ids:
        remote(r_pl.at[here], r_pl.at[here], r_ssem.at[1], r_rsem.at[1], to).start()

    for i in range(8):
        block = kunit[pl.ds(pl.multiple_of((i * 8 + zl * NC + c) * 128, 128), 128)]
        keys[pl.ds(i * 128, 128)] = block
        turned = block.astype(F32).T.astype(BF16)
        keys_t[:, pl.ds(i * 128, 128)] = turned
        keys_t[:, pl.ds(1024 + i * 128, 128)] = turned

    def scores(zp):
        zp128 = pl.multiple_of(zp * 128, 128)
        pair = []
        for v in range(2):
            q = jnp.concatenate([qg[0, zp, pl.ds(v * 64, 64)], qg[1, zp, pl.ds(v * 64, 64)]], axis=0).astype(BF16)
            q16[v, pl.ds(zp128, 128)] = q
            pair.append(q)
        rhs = jnp.concatenate(pair, axis=0)

        out = mm(keys[...], rhs, NT)
        e = jnp.exp(out * 10.0)
        k = (e * e).astype(BF16)
        for v in range(2):
            at = (v, slice(None), pl.ds(zp128, 128))
            s_buf[at] = out[:, v * 128 : v * 128 + 128]
            e_buf[at] = e[:, v * 128 : v * 128 + 128]
            k_buf[at] = k[:, v * 128 : v * 128 + 128]

    got(qg.at[1 - c, zl], gs_rsem.at[0])
    scores(zl)

    steps = ((1, 3), (2, 1), (0, 2))
    for i, step in steps:
        piece = qg.at[c, lax.rem(zl + step, NZL)]
        got(piece, g_rsem.at[i])
        remote(piece, piece, gs_ssem, gs_rsem.at[i + 1], sib).start()
    for i, step in steps:
        zp = lax.rem(zl + step, NZL)
        got(qg.at[1 - c, zp], gs_rsem.at[i + 1])
        scores(zp)

    got(r_pl.at[pl.ds(0, NP)], r_rsem.at[1])
    pairs = []
    for j in range(NZL):
        part = None
        for i in range(NZ * NX):
            if (i // NX) % NZL == j:
                part = r_pl[i] if part is None else part + r_pl[i]
        pairs.append(part)

    def assemble(base):
        tiles = []
        for v in range(2):
            at = base + v * 64
            for j in range(NZL):
                tiles += [pairs[j][0][:, at : at + 64], pairs[j][1][:, at : at + 64]]
        return jnp.concatenate(tiles, axis=1)

    window_scale = PROTOS / assemble(0)
    totals = assemble(128)

    spec_row = jnp.concatenate([qg[0, i, pl.ds(128, 1)] + qg[1, i, pl.ds(128, 1)] for i in range(4)], axis=1)
    group = lax.broadcasted_iota(jnp.int32, (NGROUP, 512), 0)
    onehot = jnp.where(group == jnp.broadcast_to(spec_row, (NGROUP, 512)).astype(jnp.int32), 1.0, 0.0)

    def plane_sum(own, slots, ssem, rsem, between):
        slots[here] = own
        for to in plane_ids:
            remote(slots.at[here], slots.at[here], ssem, rsem, to).start()
        between()

        def result():
            got(slots.at[pl.ds(0, NP)], rsem)
            part = slots[0]
            for i in range(1, NP + 1):
                part = part + slots[i]
            return part

        return result

    def nothing():
        pass

    def a_sum(it, between_1=nothing, between_2=nothing):
        remote(a_src.at[it], a_c.at[it], a_ssem.at[it, 0], a_rsem.at[it, 0], sib).start()
        between_1()
        got(a_c.at[it], a_rsem.at[it, 0])
        part = a_src[it] + a_c[it]
        return plane_sum(part, a_pl.at[it], a_ssem.at[it, 1], a_rsem.at[it, 1], between_2)()

    def b_sum(it, between=None):
        for i, to in enumerate(y_ids):
            remote(b_src.at[it], b_y.at[it, i], b_ssem.at[it], b_rsem.at[it], to).start()
        if between is not None:
            between()
        got(b_y.at[it], b_rsem.at[it])
        part = b_src[it]
        for i in range(7):
            part = part + b_y[it, i]
        return part

    def send_counts():
        cnt_src[...] = jnp.broadcast_to(jnp.sum(onehot, axis=1, keepdims=True), (NGROUP, 128))
        for i, to in enumerate(y_ids):
            remote(cnt_src, cnt_y.at[i], cnt_ssem, cnt_rsem, to).start()

    def halves(value, k0, width):
        hi = value.astype(BF16)
        two[pl.ds(k0, width)] = hi
        two[pl.ds(1024 + k0, width)] = (value - hi.astype(F32)).astype(BF16)

    def split_e(v):
        def block(kb, carry):
            k0 = pl.multiple_of(kb * 32, 32)
            halves(e_buf[v, pl.ds(k0, 32)], k0, 32)
            return carry

        lax.fori_loop(0, 32, block, 0)

    def split_t(v):
        for i in range(8):
            p = p_row[:, pl.ds(pl.multiple_of(v * 1024 + i * 128, 128), 128)]
            col = jnp.broadcast_to(p, (128, 128)).T
            t = k_buf[v, pl.ds(i * 128, 128)].astype(F32) * jnp.concatenate([col] * 4, axis=1)
            t_buf[v, pl.ds(i * 128, 128)] = t
            halves(t, i * 128, 128)

    def q_theirs(step):
        theirs = 1 - c if step == 0 else c
        (split_e, split_t)[step](theirs)
        c_src[step] = mm(keys_t[...], two[...])
        remote(c_src.at[step], c_rcv.at[step], f_ssem.at[step, 0], f_rsem.at[step, 0], sib).start()

    def q_own(step):
        (split_e, split_t)[step](c if step == 0 else 1 - c)
        x_src[step] = mm(keys_t[...], two[...])

    def q_x(step):
        got(c_rcv.at[step], f_rsem.at[step, 0])
        x_src[step] = x_src[step] + c_rcv[step]
        for h in range(2):
            for i, xx in enumerate(x_of):
                piece = x_src.at[step, pl.ds(pl.multiple_of(xx * 32 + h * 16, 16), 16)]
                remote(piece, x_rcv.at[step, h, i], f_ssem.at[step, 1 + h], f_rsem.at[step, 1 + h], x_ids[i]).start()

    def q_z(step, h):
        got(x_rcv.at[step, h], f_rsem.at[step, 1 + h])
        part = x_src[step, pl.ds(pl.multiple_of(x * 32 + h * 16, 16), 16)]
        for i in range(3):
            part = part + x_rcv[step, h, i]
        for i in range(4):
            w_src[step, h, i] = part[:, i * 128 : i * 128 + 128]
        for i, to in enumerate(z_ids):
            piece = w_src.at[step, h, lax.rem(z_of[i], NZL)]
            remote(piece, w_rcv.at[step, h, i], f_ssem.at[step, 3 + h], f_rsem.at[step, 3 + h], to).start()

    def q_end(step, h):
        got(w_rcv.at[step, h], f_rsem.at[step, 3 + h])
        part = w_src[step, h, zl]
        for i in range(7):
            part = part + w_rcv[step, h, i]
        return part

    def columns(it, scale):
        for v in range(2):
            parts = split3(scale[:, v * 512 : v * 512 + 512])
            out = mm(parts, k_buf[v], NT) if it == 0 else mm(parts, kt_buf[v])
            b_src[it, :, pl.ds(v * 1024, 1024)] = jnp.sum(out, axis=0, keepdims=True)

    def row_sums(it, scale):
        for v in range(2):
            out = mm(split3(scale[:, v * 1024 : v * 1024 + 1024]), k_buf[v])
            a_src[it, :, pl.ds(v * 512, 512)] = jnp.sum(out, axis=0, keepdims=True)

    def both_z():
        q_z(0, 0)
        q_z(0, 1)

    def beside_a0():
        send_counts()
        q_theirs(0)
        q_own(0)

    def turn():
        for v in range(2):
            kt_buf[v] = k_buf[v].T

    columns(0, window_scale)
    proto_scale = 1.0 / (PROTOS * b_sum(0, turn))
    row_sums(0, proto_scale)
    window_scale = 1.0 / a_sum(0, nothing, beside_a0)
    columns(1, window_scale)
    proto_scale = 1.0 / (PROTOS * b_sum(1, lambda: q_x(0)))
    row_sums(1, proto_scale)
    window_scale = 1.0 / a_sum(1)
    columns(2, window_scale)
    proto_scale = 1.0 / (PROTOS * b_sum(2, both_z))
    row_sums(2, proto_scale)
    p_row[...] = proto_scale

    def cross():
        for v in range(2):

            def block(kb, acc):
                k0 = pl.multiple_of(kb * 32, 32)
                prod = t_buf[1 - v, pl.ds(k0, 32)] * s_buf[v, pl.ds(k0, 32)]
                return acc + jnp.sum(prod.reshape(4, 8, 512), axis=0)

            acc = lax.fori_loop(0, 32, block, jnp.zeros((8, 512), F32))
            x_own[:, pl.ds(v * 512, 512)] = jnp.sum(acc, axis=0, keepdims=True)

    def beside_a2():
        q_own(1)
        q_x(1)
        cross()
        remote(x_own, x_c, l_ssem.at[0], l_rsem.at[0], sib).start()
        got(x_c, l_rsem.at[0])
        cross_sum.append(plane_sum(x_own[...] + x_c[...], x_pl, l_ssem.at[1], l_rsem.at[1], nothing))
        got(cnt_y, cnt_rsem)
        counts = cnt_src[...]
        for i in range(7):
            counts = counts + cnt_y[i]
        seen = jnp.sum(onehot * jnp.concatenate([counts] * 4, axis=1), axis=0, keepdims=True)
        weight = WINDOWS / (NGROUP * seen)
        tot_v = [totals[:, 0:512], totals[:, 512:1024]]
        known.extend((weight, tot_v, [5.0 * weight / tot_v[v] for v in range(2)]))

    cross_sum, known = [], []
    last = 1.0 / a_sum(2, lambda: q_theirs(1), beside_a2)

    weight, tot_v, a_v = known
    last_v = [last[:, 0:512], last[:, 512:1024]]
    b_v = [5.0 * weight * last_v[1 - v] for v in range(2)]
    for v in range(2):
        ab_rows[0, v] = a_v[v]
        ab_rows[1, v] = b_v[v]

    def add_slots(ref):
        out = ref[0]
        for i in range(1, 8):
            out = out + ref[i]
        return out

    def key_part(slot, yy):
        k0 = pl.multiple_of(yy * 128, 128)
        part = jnp.zeros((128, FEAT), F32)
        for v in range(2):
            at = (pl.ds(k0, 128), slice(None))
            g = (e_buf[(v,) + at] * a_v[v] - t_buf[(1 - v,) + at] * b_v[v]).astype(BF16)
            part = part + mm(g, q16[v])
        kg_src[slot] = part

    ahead = lambda j: lax.rem(y + j, NY)
    up1, up2, down1, down2 = (dev(y=ahead(j)) for j in (1, 2, 7, 6))
    key_part(4, ahead(4))
    remote(kg_src.at[4, pl.ds(0, 64)], kg_half.at[0], kg_ssem.at[0], kg_rsem.at[0], up2).start()
    remote(kg_src.at[4, pl.ds(64, 64)], kg_half.at[1], kg_ssem.at[1], kg_rsem.at[1], down2).start()
    key_part(3, ahead(3))
    remote(kg_src.at[3], kg_fwd.at[0], kg_ssem.at[2], kg_rsem.at[2], up1).start()
    key_part(5, ahead(5))
    remote(kg_src.at[5], kg_fwd.at[1], kg_ssem.at[3], kg_rsem.at[3], down1).start()
    key_part(2, ahead(2))
    key_part(6, ahead(6))
    key_part(1, ahead(1))
    remote(kg_src.at[1], kg_y.at[0], kg_ssem.at[4], kg_rsem.at[4], up1).start()
    key_part(7, ahead(7))
    remote(kg_src.at[7], kg_y.at[1], kg_ssem.at[5], kg_rsem.at[5], down1).start()
    key_part(0, y)

    q_z(1, 0)
    q_z(1, 1)

    shared = cross_sum[0]()
    terms = jnp.zeros((1, 512), F32)
    for v in range(2):
        x_row = shared[:, v * 512 : v * 512 + 512]
        terms = terms + 0.5 * weight * (jnp.log(tot_v[v]) - 10.0 * last_v[1 - v] * x_row)
    l_y[y] = terms[:, 0:128] + terms[:, 128:256] + terms[:, 256:384] + terms[:, 384:512]
    for to in y_ids:
        remote(l_y.at[y], l_y.at[y], l_ssem.at[2], l_rsem.at[2], to).start()

    got(kg_fwd.at[0], kg_rsem.at[2])
    got(kg_half.at[0], kg_rsem.at[0])
    kg_src[2, pl.ds(0, 64)] = kg_src[2, pl.ds(0, 64)] + kg_fwd[0, pl.ds(0, 64)] + kg_half[0]
    kg_src[2, pl.ds(64, 64)] = kg_src[2, pl.ds(64, 64)] + kg_fwd[0, pl.ds(64, 64)]
    remote(kg_src.at[2], kg_y.at[2], kg_ssem.at[6], kg_rsem.at[6], up2).start()
    got(kg_fwd.at[1], kg_rsem.at[3])
    got(kg_half.at[1], kg_rsem.at[1])
    kg_src[6, pl.ds(0, 64)] = kg_src[6, pl.ds(0, 64)] + kg_fwd[1, pl.ds(0, 64)]
    kg_src[6, pl.ds(64, 64)] = kg_src[6, pl.ds(64, 64)] + kg_fwd[1, pl.ds(64, 64)] + kg_half[1]
    remote(kg_src.at[6], kg_y.at[3], kg_ssem.at[7], kg_rsem.at[7], down2).start()

    at = pl.ds(pl.multiple_of(zl * 128, 128), 128)
    for h in range(2):
        part = ab_rows[0, c, :, at] * q_end(0, h) - ab_rows[1, c, :, at] * q_end(1, h)
        feats = pl.ds(pl.multiple_of(x * 32 + h * 16, 16), 16)
        mine = fin.at[c, feats]
        fin[c, feats] = part
        for to in xc_ids:
            remote(mine, mine, fin_ssem.at[h], fin_rsem.at[h], to).start()

    part = kg_src[0]
    for i, k in ((0, 4), (1, 5), (2, 6), (3, 7)):
        got(kg_y.at[i], kg_rsem.at[k])
        part = part + kg_y[i]
    own = pl.multiple_of((y * 8 + zl * NC + c) * 128, 128)
    pgrad_ref[...] = unit_back(kraw[pl.ds(own, 128)].astype(F32), part)

    for h in range(2):
        got(w_rcv.at[0, h], fin_rsem.at[h])
    for v in range(2):
        qt[v] = fin[v].T
    for v in range(2):
        grad = qt[v, pl.ds(pl.multiple_of(c * 64, 64), 64)]
        view_ref[v] = unit_back(pooled[pl.ds(v * 64, 64)], grad)

    got(l_y.at[pl.ds(0, 7)], l_rsem.at[2])
    loss_ref[...] = jnp.sum(add_slots(l_y), axis=1, keepdims=True) * (1.0 / WINDOWS)

    sent(qg.at[0, pl.ds(0, 3)], g_ssem)
    sent(qg.at[0], gs_ssem)
    for it in range(3):
        sent(a_c.at[it], a_ssem.at[it, 0])
        sent(a_pl.at[it, pl.ds(0, NP)], a_ssem.at[it, 1])
    for it in range(3):
        sent(b_y.at[it], b_ssem.at[it])
    sent(r_two.at[0], r_ssem.at[0])
    sent(r_pl.at[pl.ds(0, NP)], r_ssem.at[1])
    sent(cnt_y, cnt_ssem)
    for i in range(2):
        sent(kg_half.at[i], kg_ssem.at[i])
        sent(kg_fwd.at[i], kg_ssem.at[2 + i])
        sent(kg_y.at[i], kg_ssem.at[4 + i])
        sent(kg_y.at[2 + i], kg_ssem.at[6 + i])
        sent(c_rcv.at[i], f_ssem.at[i, 0])
        for h in range(2):
            sent(x_rcv.at[i, h], f_ssem.at[i, 1 + h])
            sent(w_rcv.at[i, h], f_ssem.at[i, 3 + h])
        sent(w_rcv.at[0, i], fin_ssem.at[i])
    sent(x_c, l_ssem.at[0])
    sent(x_pl.at[pl.ds(0, NP)], l_ssem.at[1])
    sent(l_y.at[pl.ds(0, 7)], l_ssem.at[2])


def hand_on(view_in, pgrad_in, loss_in, view_ref, pgrad_ref, loss_ref):
    view_ref[...] = view_in[...]
    pgrad_ref[...] = pgrad_in[...]
    loss_ref[...] = loss_in[...]


def on_device(tokens, offsets, species, prototypes):
    vmem = pltpu.VMEM
    dma = pltpu.SemaphoreType.DMA
    anywhere = pl.BlockSpec(memory_space=pl.ANY)
    inside = pl.BlockSpec(memory_space=pltpu.VMEM)
    scratch = [
        vmem((64 * SEQ, FEAT), BF16),
        vmem((128, 64 * SEQ), BF16),
        vmem((8192, FEAT), BF16),
        vmem((8192, FEAT), BF16),
        vmem((1024, FEAT), BF16),
        vmem((FEAT, 2048), BF16),
        vmem((128, FEAT), F32),
        vmem((2, 4, 136, FEAT), F32),
        vmem((2, 512, FEAT), BF16),
        vmem((2, 1024, 512), F32),
        vmem((2, 1024, 512), F32),
        vmem((2, 1024, 512), BF16),
        vmem((2, 512, 1024), BF16),
        vmem((2, 1024, 512), F32),
        vmem((2048, 512), BF16),
        vmem((3, 1, 1024), F32),
        vmem((3, 1, 1024), F32),
        vmem((3, NP + 1, 1, 1024), F32),
        vmem((3, 1, 2048), F32),
        vmem((3, 7, 1, 2048), F32),
        vmem((2, 1, 256), F32),
        vmem((NP + 1, 2, 1, 256), F32),
        vmem((NGROUP, 128), F32),
        vmem((7, NGROUP, 128), F32),
        vmem((8, 128, FEAT), F32),
        vmem((2, 64, FEAT), F32),
        vmem((2, 128, FEAT), F32),
        vmem((4, 128, FEAT), F32),
        vmem((2, FEAT, 512), F32),
        vmem((2, FEAT, 512), F32),
        vmem((2, FEAT, 512), F32),
        vmem((2, 2, 3, 16, 512), F32),
        vmem((2, 2, 4, 16, 128), F32),
        vmem((2, 2, 7, 16, 128), F32),
        vmem((2, FEAT, 128), F32),
        vmem((8, 1, 128), F32),
        vmem((1, 1024), F32),
        vmem((1, 1024), F32),
        vmem((NP + 1, 1, 1024), F32),
        vmem((1, 2048), F32),
        vmem((2, 2, 1, 512), F32),
        vmem((2, 128, FEAT), F32),
        dma((2,)),
        dma, dma((3,)), dma, dma((4,)),
        dma((3, 2)), dma((3, 2)), dma((3,)), dma((3,)), dma((2,)), dma((2,)), dma, dma,
        dma((8,)), dma((8,)), dma((2, 5)), dma((2, 5)), dma((2,)), dma((2,)), dma((3,)), dma((3,)),
    ]
    view_grads, proto_grads, loss = pl.pallas_call(
        kernel,
        out_shape=(vmem((2, 64, FEAT), F32), vmem((128, FEAT), F32), vmem((1, 1), F32)),
        in_specs=[anywhere, inside, inside, anywhere],
        out_specs=(inside, inside, inside),
        scratch_shapes=scratch,
        compiler_params=pltpu.CompilerParams(
            collective_id=0, has_side_effects=True, vmem_limit_bytes=60 * 2**20
        ),
        name="swav_step",
    )(
        tokens.reshape(64 * SEQ, FEAT),
        offsets,
        species.reshape(1, 64),
        prototypes,
    )
    view_grads, proto_grads, loss = pl.pallas_call(
        hand_on,
        out_shape=(
            jax.ShapeDtypeStruct((2, 64, FEAT), F32),
            jax.ShapeDtypeStruct((128, FEAT), F32),
            jax.ShapeDtypeStruct((1, 1), F32),
        ),
        in_specs=[inside] * 3,
        out_specs=(inside, inside, inside),
        compiler_params=pltpu.CompilerParams(vmem_limit_bytes=16 * 2**20),
        name="results",
    )(*(pltpu.with_memory_space_constraint(a, pltpu.VMEM) for a in (view_grads, proto_grads, loss)))
    return view_grads, proto_grads, loss.reshape(())


def solution(mesh):
    return jax.shard_map(
        on_device,
        mesh=mesh,
        in_specs=(P("dp", None, None), P(None, "dp"), P("dp"), P("proto", None)),
        out_specs=(P(None, "dp", None), P(("proto", "dp"), None), P()),
        check_vma=False,
    )
```

```python
import math

import jax
import jax.numpy as jnp
from jax import lax
from jax.experimental import pallas as pl
from jax.experimental.pallas import tpu as pltpu
from jax.sharding import PartitionSpec as P

MESH = pl.DeviceIdType.MESH
F32 = jnp.float32
BF16 = jnp.bfloat16
NGROUP = 16
CROP = 24
SEQ = 32
FEAT = 128
WINDOWS = 4096
PROTOS = 65536
EPS = 1e-6
NY, NZL, NC, NZH, NX = 8, 4, 2, 2, 4
NZ = NZH * NZL
RING8 = (4, 3, 5, 2, 6, 1, 7)
XC = ((2, 0), (2, 1), (1, 0), (3, 0), (1, 1), (3, 1), (0, 1))
RING4 = (2, 1, 3)
PLANE = tuple(
    sorted(
        ((dx, dz) for dx in range(NX) for dz in range(NZ) if dx or dz),
        key=lambda o: -(min(o[0], NX - o[0]) + min(o[1], NZ - o[1])),
    )
)
NP = len(PLANE)
NT = (((1,), (1,)), ((), ()))
NN = (((1,), (0,)), ((), ()))


def mm(a, b, dims=NN):
    return lax.dot_general(a, b, dims, preferred_element_type=F32)


def split3(row, count=16):
    hi = row.astype(BF16).astype(F32)
    rest = row - hi
    mid = rest.astype(BF16).astype(F32)
    lo = rest - mid
    width = row.shape[1]
    at = lax.broadcasted_iota(jnp.int32, (count, width), 0)
    full = lambda r: jnp.broadcast_to(r, (count, width))
    out = jnp.where(at == 0, full(hi), jnp.where(at == 1, full(mid), jnp.where(at == 2, full(lo), 0.0)))
    return out.astype(BF16)


def unit_scale(rows):
    return lax.rsqrt(jnp.mean(rows * rows, axis=-1, keepdims=True) + EPS)


def unit_back(rows, grad):
    scale = unit_scale(rows)
    along = jnp.mean(rows * grad, axis=-1, keepdims=True)
    return (grad - rows * (along * scale * scale)) * (scale / math.sqrt(FEAT))


def kernel(
    tok_ref, off_ref, spec_ref, proto_ref,
    view_ref, pgrad_ref, loss_ref,
    tok, mask, kraw, kunit, keys, keys_t, pooled, qg, q16, s_buf, e_buf, k_buf, kt_buf, t_buf, two,
    a_src, a_c, a_pl, b_src, b_y, r_two, r_pl, cnt_src, cnt_y,
    kg_src, kg_half, kg_fwd, kg_y, c_src, c_rcv, x_src, x_rcv, w_src, w_rcv, fin, l_y,
    x_own, x_c, x_pl, p_row, ab_rows, qt,
    load_sem, g_ssem, g_rsem, gs_ssem, gs_rsem,
    a_ssem, a_rsem, b_ssem, b_rsem, r_ssem, r_rsem, cnt_ssem, cnt_rsem,
    kg_ssem, kg_rsem, f_ssem, f_rsem, fin_ssem, fin_rsem, l_ssem, l_rsem,
):
    dp = lax.axis_index("dp")
    pr = lax.axis_index("proto")
    y, zl, c = lax.div(dp, 8), lax.rem(lax.div(dp, 2), 4), lax.rem(dp, 2)
    zh, x = lax.div(pr, 4), lax.rem(pr, 4)
    z = zh * NZL + zl

    def dev(y=y, z=z, c=c, x=x):
        return ((y * NZL + lax.rem(z, NZL)) * NC + c, lax.div(z, NZL) * NX + x)

    xc_ids = [dev(x=lax.rem(x + dx, NX), c=lax.rem(c + dc, NC)) for dx, dc in XC]
    z_of = [lax.rem(z + j, NZ) for j in RING8]
    z_ids = [dev(z=k) for k in z_of]
    y_of = [lax.rem(y + j, NY) for j in RING8]
    y_ids = [dev(y=k) for k in y_of]
    x_of = [lax.rem(x + j, NX) for j in RING4]
    x_ids = [dev(x=k) for k in x_of]
    sib = dev(c=1 - c)
    plane_ids = [dev(x=lax.rem(x + dx, NX), z=lax.rem(z + dz, NZ)) for dx, dz in PLANE]
    step2 = 2 + 4 * c
    near = [lax.rem(z + step, NZ) for step in (step2, 1, 7)]
    near_ids = [dev(z=k) for k in near]
    here = z * NX + x
    cross_ids = [xc_ids[i] for i in range(7) if XC[i][0] and XC[i][1]]

    def remote(src, dst, ssem, rsem, to):
        return pltpu.make_async_remote_copy(
            src_ref=src, dst_ref=dst, send_sem=ssem, recv_sem=rsem, device_id=to, device_id_type=MESH
        )

    def got(ref, sem):
        remote(ref, ref, sem, sem, sib).wait_recv()

    def sent(ref, sem):
        remote(ref, ref, sem, sem, sib).wait_send()

    barrier = pltpu.get_barrier_semaphore()
    load_tok = pltpu.make_async_copy(tok_ref, tok, load_sem.at[0])
    load_key = pltpu.make_async_copy(proto_ref, kraw, load_sem.at[1])
    load_tok.start()
    load_key.start()
    for to in plane_ids + y_ids + cross_ids + [sib]:
        pl.semaphore_signal(barrier, inc=1, device_id=to, device_id_type=MESH)

    off = off_ref[...].astype(F32)
    off_row = jnp.concatenate([off[0:1], off[1:2]], axis=1)
    lane = lax.broadcasted_iota(jnp.int32, (128, 128), 1)
    first = jnp.broadcast_to(off_row, (128, 128)).T.astype(jnp.int32)
    row = lax.broadcasted_iota(jnp.int32, (128, 128), 0)
    first = first + (row & 63) * SEQ
    for part in range(16):
        col = part * 128
        inside = (lane + col >= first) & (lane + col < first + CROP)
        mask[:, pl.ds(col, 128)] = jnp.where(inside, 1.0, 0.0).astype(BF16)
    load_tok.wait()
    total = mm(mask[...], tok[...])
    rows = total / CROP
    pooled[...] = rows
    query = (rows * unit_scale(rows) / math.sqrt(FEAT)).astype(BF16)
    qg[c, zl, pl.ds(0, 128)] = query.astype(F32)
    spec = spec_ref[...].astype(F32)
    both = jnp.concatenate([spec, spec], axis=1)
    half = lax.broadcasted_iota(jnp.int32, (8, 128), 1) // 64
    qg[c, zl, pl.ds(128, 8)] = jnp.where(half == c, jnp.broadcast_to(both, (8, 128)), 0.0)

    load_key.wait()

    def whole(i, sums):
        at = pl.ds(pl.multiple_of(i * 4096, 4096), 4096)
        raw = kraw[at].astype(F32)
        unit = (raw * (unit_scale(raw) * (1.0 / math.sqrt(FEAT)))).astype(BF16)
        kunit[at] = unit
        e = jnp.exp(mm(unit, query, NT) * 10.0)
        k = (e * e).astype(BF16).astype(F32)
        fold = lambda a: jnp.sum(a.reshape(512, 8, 128), axis=0)
        return sums[0] + fold(k), sums[1] + fold(e)

    zero = jnp.zeros((8, 128), F32)
    ks, es = lax.fori_loop(0, 2, whole, (zero, zero))
    r_two[c, :, pl.ds(0, 128)] = jnp.sum(ks, axis=0, keepdims=True)
    r_two[c, :, pl.ds(128, 128)] = jnp.sum(es, axis=0, keepdims=True)

    pl.semaphore_wait(barrier, 11 + NP)
    remote(r_two.at[c], r_two.at[c], r_ssem.at[0], r_rsem.at[0], sib).start()

    mine = qg.at[c, zl]
    for i, to in enumerate(near_ids):
        remote(mine, mine, g_ssem, g_rsem.at[i], to).start()
    remote(mine, mine, gs_ssem, gs_rsem.at[0], sib).start()

    got(r_two.at[1 - c], r_rsem.at[0])
    r_pl[here] = r_two[...]
    for to in plane_ids:
        remote(r_pl.at[here], r_pl.at[here], r_ssem.at[1], r_rsem.at[1], to).start()

    for i in range(8):
        block = kunit[pl.ds(pl.multiple_of((i * 8 + zl * NC + c) * 128, 128), 128)]
        keys[pl.ds(i * 128, 128)] = block
        turned = block.astype(F32).T.astype(BF16)
        keys_t[:, pl.ds(i * 128, 128)] = turned
        keys_t[:, pl.ds(1024 + i * 128, 128)] = turned

    def scores(zp):
        zp128 = pl.multiple_of(zp * 128, 128)
        pair = []
        for v in range(2):
            q = jnp.concatenate([qg[0, zp, pl.ds(v * 64, 64)], qg[1, zp, pl.ds(v * 64, 64)]], axis=0).astype(BF16)
            q16[v, pl.ds(zp128, 128)] = q
            pair.append(q)
        rhs = jnp.concatenate(pair, axis=0)

        out = mm(keys[...], rhs, NT)
        e = jnp.exp(out * 10.0)
        k = (e * e).astype(BF16)
        for v in range(2):
            at = (v, slice(None), pl.ds(zp128, 128))
            s_buf[at] = out[:, v * 128 : v * 128 + 128]
            e_buf[at] = e[:, v * 128 : v * 128 + 128]
            k_buf[at] = k[:, v * 128 : v * 128 + 128]

    got(qg.at[1 - c, zl], gs_rsem.at[0])
    scores(zl)

    steps = ((1, 3), (2, 1), (0, 2))
    for i, step in steps:
        piece = qg.at[c, lax.rem(zl + step, NZL)]
        got(piece, g_rsem.at[i])
        remote(piece, piece, gs_ssem, gs_rsem.at[i + 1], sib).start()
    for i, step in steps:
        zp = lax.rem(zl + step, NZL)
        got(qg.at[1 - c, zp], gs_rsem.at[i + 1])
        scores(zp)

    got(r_pl.at[pl.ds(0, NP)], r_rsem.at[1])
    pairs = []
    for j in range(NZL):
        part = None
        for i in range(NZ * NX):
            if (i // NX) % NZL == j:
                part = r_pl[i] if part is None else part + r_pl[i]
        pairs.append(part)

    def assemble(base):
        tiles = []
        for v in range(2):
            at = base + v * 64
            for j in range(NZL):
                tiles += [pairs[j][0][:, at : at + 64], pairs[j][1][:, at : at + 64]]
        return jnp.concatenate(tiles, axis=1)

    window_scale = PROTOS / assemble(0)
    totals = assemble(128)

    spec_row = jnp.concatenate([qg[0, i, pl.ds(128, 1)] + qg[1, i, pl.ds(128, 1)] for i in range(4)], axis=1)
    group = lax.broadcasted_iota(jnp.int32, (NGROUP, 512), 0)
    onehot = jnp.where(group == jnp.broadcast_to(spec_row, (NGROUP, 512)).astype(jnp.int32), 1.0, 0.0)

    def plane_sum(own, slots, ssem, rsem, between):
        slots[here] = own
        for to in plane_ids:
            remote(slots.at[here], slots.at[here], ssem, rsem, to).start()
        between()

        def result():
            got(slots.at[pl.ds(0, NP)], rsem)
            part = slots[0]
            for i in range(1, NP + 1):
                part = part + slots[i]
            return part

        return result

    def nothing():
        pass

    def a_sum(it, between_1=nothing, between_2=nothing):
        remote(a_src.at[it], a_c.at[it], a_ssem.at[it, 0], a_rsem.at[it, 0], sib).start()
        between_1()
        got(a_c.at[it], a_rsem.at[it, 0])
        part = a_src[it] + a_c[it]
        return plane_sum(part, a_pl.at[it], a_ssem.at[it, 1], a_rsem.at[it, 1], between_2)()

    def b_sum(it, between=None):
        for i, to in enumerate(y_ids):
            remote(b_src.at[it], b_y.at[it, i], b_ssem.at[it], b_rsem.at[it], to).start()
        if between is not None:
            between()
        got(b_y.at[it], b_rsem.at[it])
        part = b_src[it]
        for i in range(7):
            part = part + b_y[it, i]
        return part

    def send_counts():
        cnt_src[...] = jnp.broadcast_to(jnp.sum(onehot, axis=1, keepdims=True), (NGROUP, 128))
        for i, to in enumerate(y_ids):
            remote(cnt_src, cnt_y.at[i], cnt_ssem, cnt_rsem, to).start()

    def halves(value, k0, width):
        hi = value.astype(BF16)
        two[pl.ds(k0, width)] = hi
        two[pl.ds(1024 + k0, width)] = (value - hi.astype(F32)).astype(BF16)

    def split_e(v):
        def block(kb, carry):
            k0 = pl.multiple_of(kb * 32, 32)
            halves(e_buf[v, pl.ds(k0, 32)], k0, 32)
            return carry

        lax.fori_loop(0, 32, block, 0)

    def split_t(v):
        for i in range(8):
            p = p_row[:, pl.ds(pl.multiple_of(v * 1024 + i * 128, 128), 128)]
            col = jnp.broadcast_to(p, (128, 128)).T
            t = k_buf[v, pl.ds(i * 128, 128)].astype(F32) * jnp.concatenate([col] * 4, axis=1)
            t_buf[v, pl.ds(i * 128, 128)] = t
            halves(t, i * 128, 128)

    def q_theirs(step):
        theirs = 1 - c if step == 0 else c
        (split_e, split_t)[step](theirs)
        c_src[step] = mm(keys_t[...], two[...])
        remote(c_src.at[step], c_rcv.at[step], f_ssem.at[step, 0], f_rsem.at[step, 0], sib).start()

    def q_own(step):
        (split_e, split_t)[step](c if step == 0 else 1 - c)
        x_src[step] = mm(keys_t[...], two[...])

    def q_x(step):
        got(c_rcv.at[step], f_rsem.at[step, 0])
        x_src[step] = x_src[step] + c_rcv[step]
        for h in range(2):
            for i, xx in enumerate(x_of):
                piece = x_src.at[step, pl.ds(pl.multiple_of(xx * 32 + h * 16, 16), 16)]
                remote(piece, x_rcv.at[step, h, i], f_ssem.at[step, 1 + h], f_rsem.at[step, 1 + h], x_ids[i]).start()

    def q_z(step, h):
        got(x_rcv.at[step, h], f_rsem.at[step, 1 + h])
        part = x_src[step, pl.ds(pl.multiple_of(x * 32 + h * 16, 16), 16)]
        for i in range(3):
            part = part + x_rcv[step, h, i]
        for i in range(4):
            w_src[step, h, i] = part[:, i * 128 : i * 128 + 128]
        for i, to in enumerate(z_ids):
            piece = w_src.at[step, h, lax.rem(z_of[i], NZL)]
            remote(piece, w_rcv.at[step, h, i], f_ssem.at[step, 3 + h], f_rsem.at[step, 3 + h], to).start()

    def q_end(step, h):
        got(w_rcv.at[step, h], f_rsem.at[step, 3 + h])
        part = w_src[step, h, zl]
        for i in range(7):
            part = part + w_rcv[step, h, i]
        return part

    def columns(it, scale):
        for v in range(2):
            parts = split3(scale[:, v * 512 : v * 512 + 512])
            out = mm(parts, k_buf[v], NT) if it == 0 else mm(parts, kt_buf[v])
            b_src[it, :, pl.ds(v * 1024, 1024)] = jnp.sum(out, axis=0, keepdims=True)

    def row_sums(it, scale):
        for v in range(2):
            out = mm(split3(scale[:, v * 1024 : v * 1024 + 1024]), k_buf[v])
            a_src[it, :, pl.ds(v * 512, 512)] = jnp.sum(out, axis=0, keepdims=True)

    def both_z():
        q_z(0, 0)
        q_z(0, 1)

    def beside_a0():
        send_counts()
        q_theirs(0)
        q_own(0)

    def turn():
        for v in range(2):
            kt_buf[v] = k_buf[v].T

    columns(0, window_scale)
    proto_scale = 1.0 / (PROTOS * b_sum(0, turn))
    row_sums(0, proto_scale)
    window_scale = 1.0 / a_sum(0, nothing, beside_a0)
    columns(1, window_scale)
    proto_scale = 1.0 / (PROTOS * b_sum(1, lambda: q_x(0)))
    row_sums(1, proto_scale)
    window_scale = 1.0 / a_sum(1)
    columns(2, window_scale)
    proto_scale = 1.0 / (PROTOS * b_sum(2, both_z))
    row_sums(2, proto_scale)
    p_row[...] = proto_scale

    def cross():
        for v in range(2):

            def block(kb, acc):
                k0 = pl.multiple_of(kb * 32, 32)
                prod = t_buf[1 - v, pl.ds(k0, 32)] * s_buf[v, pl.ds(k0, 32)]
                return acc + jnp.sum(prod.reshape(4, 8, 512), axis=0)

            acc = lax.fori_loop(0, 32, block, jnp.zeros((8, 512), F32))
            x_own[:, pl.ds(v * 512, 512)] = jnp.sum(acc, axis=0, keepdims=True)

    def beside_a2():
        q_own(1)
        q_x(1)
        cross()
        remote(x_own, x_c, l_ssem.at[0], l_rsem.at[0], sib).start()
        got(x_c, l_rsem.at[0])
        cross_sum.append(plane_sum(x_own[...] + x_c[...], x_pl, l_ssem.at[1], l_rsem.at[1], nothing))
        got(cnt_y, cnt_rsem)
        counts = cnt_src[...]
        for i in range(7):
            counts = counts + cnt_y[i]
        seen = jnp.sum(onehot * jnp.concatenate([counts] * 4, axis=1), axis=0, keepdims=True)
        weight = WINDOWS / (NGROUP * seen)
        tot_v = [totals[:, 0:512], totals[:, 512:1024]]
        known.extend((weight, tot_v, [5.0 * weight / tot_v[v] for v in range(2)]))

    cross_sum, known = [], []
    last = 1.0 / a_sum(2, lambda: q_theirs(1), beside_a2)

    weight, tot_v, a_v = known
    last_v = [last[:, 0:512], last[:, 512:1024]]
    b_v = [5.0 * weight * last_v[1 - v] for v in range(2)]
    for v in range(2):
        ab_rows[0, v] = a_v[v]
        ab_rows[1, v] = b_v[v]

    def add_slots(ref):
        out = ref[0]
        for i in range(1, 8):
            out = out + ref[i]
        return out

    def key_part(slot, yy):
        k0 = pl.multiple_of(yy * 128, 128)
        part = jnp.zeros((128, FEAT), F32)
        for v in range(2):
            at = (pl.ds(k0, 128), slice(None))
            g = (e_buf[(v,) + at] * a_v[v] - t_buf[(1 - v,) + at] * b_v[v]).astype(BF16)
            part = part + mm(g, q16[v])
        kg_src[slot] = part

    ahead = lambda j: lax.rem(y + j, NY)
    up1, up2, down1, down2 = (dev(y=ahead(j)) for j in (1, 2, 7, 6))
    key_part(4, ahead(4))
    remote(kg_src.at[4, pl.ds(0, 64)], kg_half.at[0], kg_ssem.at[0], kg_rsem.at[0], up2).start()
    remote(kg_src.at[4, pl.ds(64, 64)], kg_half.at[1], kg_ssem.at[1], kg_rsem.at[1], down2).start()
    key_part(3, ahead(3))
    remote(kg_src.at[3], kg_fwd.at[0], kg_ssem.at[2], kg_rsem.at[2], up1).start()
    key_part(5, ahead(5))
    remote(kg_src.at[5], kg_fwd.at[1], kg_ssem.at[3], kg_rsem.at[3], down1).start()
    key_part(1, ahead(1))
    remote(kg_src.at[1], kg_y.at[0], kg_ssem.at[4], kg_rsem.at[4], up1).start()
    key_part(7, ahead(7))
    remote(kg_src.at[7], kg_y.at[1], kg_ssem.at[5], kg_rsem.at[5], down1).start()
    q_z(1, 0)
    key_part(2, ahead(2))
    key_part(6, ahead(6))
    key_part(0, y)
    q_z(1, 1)

    shared = cross_sum[0]()
    terms = jnp.zeros((1, 512), F32)
    for v in range(2):
        x_row = shared[:, v * 512 : v * 512 + 512]
        terms = terms + 0.5 * weight * (jnp.log(tot_v[v]) - 10.0 * last_v[1 - v] * x_row)
    l_y[y] = terms[:, 0:128] + terms[:, 128:256] + terms[:, 256:384] + terms[:, 384:512]
    for to in y_ids:
        remote(l_y.at[y], l_y.at[y], l_ssem.at[2], l_rsem.at[2], to).start()

    got(kg_fwd.at[0], kg_rsem.at[2])
    got(kg_half.at[0], kg_rsem.at[0])
    kg_src[2, pl.ds(0, 64)] = kg_src[2, pl.ds(0, 64)] + kg_fwd[0, pl.ds(0, 64)] + kg_half[0]
    kg_src[2, pl.ds(64, 64)] = kg_src[2, pl.ds(64, 64)] + kg_fwd[0, pl.ds(64, 64)]
    remote(kg_src.at[2], kg_y.at[2], kg_ssem.at[6], kg_rsem.at[6], up2).start()
    got(kg_fwd.at[1], kg_rsem.at[3])
    got(kg_half.at[1], kg_rsem.at[1])
    kg_src[6, pl.ds(0, 64)] = kg_src[6, pl.ds(0, 64)] + kg_fwd[1, pl.ds(0, 64)]
    kg_src[6, pl.ds(64, 64)] = kg_src[6, pl.ds(64, 64)] + kg_fwd[1, pl.ds(64, 64)] + kg_half[1]
    remote(kg_src.at[6], kg_y.at[3], kg_ssem.at[7], kg_rsem.at[7], down2).start()

    at = pl.ds(pl.multiple_of(zl * 128, 128), 128)
    for h in range(2):
        part = ab_rows[0, c, :, at] * q_end(0, h) - ab_rows[1, c, :, at] * q_end(1, h)
        feats = pl.ds(pl.multiple_of(x * 32 + h * 16, 16), 16)
        mine = fin.at[c, feats]
        fin[c, feats] = part
        for to in xc_ids:
            remote(mine, mine, fin_ssem.at[h], fin_rsem.at[h], to).start()

    part = kg_src[0]
    for i, k in ((0, 4), (1, 5), (2, 6), (3, 7)):
        got(kg_y.at[i], kg_rsem.at[k])
        part = part + kg_y[i]
    own = pl.multiple_of((y * 8 + zl * NC + c) * 128, 128)
    pgrad_ref[...] = unit_back(kraw[pl.ds(own, 128)].astype(F32), part)

    for h in range(2):
        got(w_rcv.at[0, h], fin_rsem.at[h])
    for v in range(2):
        qt[v] = fin[v].T
    for v in range(2):
        grad = qt[v, pl.ds(pl.multiple_of(c * 64, 64), 64)]
        view_ref[v] = unit_back(pooled[pl.ds(v * 64, 64)], grad)

    got(l_y.at[pl.ds(0, 7)], l_rsem.at[2])
    loss_ref[...] = jnp.sum(add_slots(l_y), axis=1, keepdims=True) * (1.0 / WINDOWS)

    sent(qg.at[0, pl.ds(0, 3)], g_ssem)
    sent(qg.at[0], gs_ssem)
    for it in range(3):
        sent(a_c.at[it], a_ssem.at[it, 0])
        sent(a_pl.at[it, pl.ds(0, NP)], a_ssem.at[it, 1])
    for it in range(3):
        sent(b_y.at[it], b_ssem.at[it])
    sent(r_two.at[0], r_ssem.at[0])
    sent(r_pl.at[pl.ds(0, NP)], r_ssem.at[1])
    sent(cnt_y, cnt_ssem)
    for i in range(2):
        sent(kg_half.at[i], kg_ssem.at[i])
        sent(kg_fwd.at[i], kg_ssem.at[2 + i])
        sent(kg_y.at[i], kg_ssem.at[4 + i])
        sent(kg_y.at[2 + i], kg_ssem.at[6 + i])
        sent(c_rcv.at[i], f_ssem.at[i, 0])
        for h in range(2):
            sent(x_rcv.at[i, h], f_ssem.at[i, 1 + h])
            sent(w_rcv.at[i, h], f_ssem.at[i, 3 + h])
        sent(w_rcv.at[0, i], fin_ssem.at[i])
    sent(x_c, l_ssem.at[0])
    sent(x_pl.at[pl.ds(0, NP)], l_ssem.at[1])
    sent(l_y.at[pl.ds(0, 7)], l_ssem.at[2])


def hand_on(view_in, pgrad_in, loss_in, view_ref, pgrad_ref, loss_ref):
    view_ref[...] = view_in[...]
    pgrad_ref[...] = pgrad_in[...]
    loss_ref[...] = loss_in[...]


def on_device(tokens, offsets, species, prototypes):
    vmem = pltpu.VMEM
    dma = pltpu.SemaphoreType.DMA
    anywhere = pl.BlockSpec(memory_space=pl.ANY)
    inside = pl.BlockSpec(memory_space=pltpu.VMEM)
    scratch = [
        vmem((64 * SEQ, FEAT), BF16),
        vmem((128, 64 * SEQ), BF16),
        vmem((8192, FEAT), BF16),
        vmem((8192, FEAT), BF16),
        vmem((1024, FEAT), BF16),
        vmem((FEAT, 2048), BF16),
        vmem((128, FEAT), F32),
        vmem((2, 4, 136, FEAT), F32),
        vmem((2, 512, FEAT), BF16),
        vmem((2, 1024, 512), F32),
        vmem((2, 1024, 512), F32),
        vmem((2, 1024, 512), BF16),
        vmem((2, 512, 1024), BF16),
        vmem((2, 1024, 512), F32),
        vmem((2048, 512), BF16),
        vmem((3, 1, 1024), F32),
        vmem((3, 1, 1024), F32),
        vmem((3, NP + 1, 1, 1024), F32),
        vmem((3, 1, 2048), F32),
        vmem((3, 7, 1, 2048), F32),
        vmem((2, 1, 256), F32),
        vmem((NP + 1, 2, 1, 256), F32),
        vmem((NGROUP, 128), F32),
        vmem((7, NGROUP, 128), F32),
        vmem((8, 128, FEAT), F32),
        vmem((2, 64, FEAT), F32),
        vmem((2, 128, FEAT), F32),
        vmem((4, 128, FEAT), F32),
        vmem((2, FEAT, 512), F32),
        vmem((2, FEAT, 512), F32),
        vmem((2, FEAT, 512), F32),
        vmem((2, 2, 3, 16, 512), F32),
        vmem((2, 2, 4, 16, 128), F32),
        vmem((2, 2, 7, 16, 128), F32),
        vmem((2, FEAT, 128), F32),
        vmem((8, 1, 128), F32),
        vmem((1, 1024), F32),
        vmem((1, 1024), F32),
        vmem((NP + 1, 1, 1024), F32),
        vmem((1, 2048), F32),
        vmem((2, 2, 1, 512), F32),
        vmem((2, 128, FEAT), F32),
        dma((2,)),
        dma, dma((3,)), dma, dma((4,)),
        dma((3, 2)), dma((3, 2)), dma((3,)), dma((3,)), dma((2,)), dma((2,)), dma, dma,
        dma((8,)), dma((8,)), dma((2, 5)), dma((2, 5)), dma((2,)), dma((2,)), dma((3,)), dma((3,)),
    ]
    view_grads, proto_grads, loss = pl.pallas_call(
        kernel,
        out_shape=(vmem((2, 64, FEAT), F32), vmem((128, FEAT), F32), vmem((1, 1), F32)),
        in_specs=[anywhere, inside, inside, anywhere],
        out_specs=(inside, inside, inside),
        scratch_shapes=scratch,
        compiler_params=pltpu.CompilerParams(
            collective_id=0, has_side_effects=True, vmem_limit_bytes=60 * 2**20
        ),
        name="swav_step",
    )(
        tokens.reshape(64 * SEQ, FEAT),
        offsets,
        species.reshape(1, 64),
        prototypes,
    )
    view_grads, proto_grads, loss = pl.pallas_call(
        hand_on,
        out_shape=(
            jax.ShapeDtypeStruct((2, 64, FEAT), F32),
            jax.ShapeDtypeStruct((128, FEAT), F32),
            jax.ShapeDtypeStruct((1, 1), F32),
        ),
        in_specs=[inside] * 3,
        out_specs=(inside, inside, inside),
        compiler_params=pltpu.CompilerParams(vmem_limit_bytes=16 * 2**20),
        name="results",
    )(*(pltpu.with_memory_space_constraint(a, pltpu.VMEM) for a in (view_grads, proto_grads, loss)))
    return view_grads, proto_grads, loss.reshape(())


def solution(mesh):
    return jax.shard_map(
        on_device,
        mesh=mesh,
        in_specs=(P("dp", None, None), P(None, "dp"), P("dp"), P("proto", None)),
        out_specs=(P(None, "dp", None), P(("proto", "dp"), None), P()),
        check_vma=False,
    )
```

```python
import math

import jax
import jax.numpy as jnp
from jax import lax
from jax.experimental import pallas as pl
from jax.experimental.pallas import tpu as pltpu
from jax.sharding import PartitionSpec as P

MESH = pl.DeviceIdType.MESH
F32 = jnp.float32
BF16 = jnp.bfloat16
NGROUP = 16
CROP = 24
SEQ = 32
FEAT = 128
WINDOWS = 4096
PROTOS = 65536
EPS = 1e-6
NY, NZL, NC, NZH, NX = 8, 4, 2, 2, 4
NZ = NZH * NZL
RING8 = (4, 3, 5, 2, 6, 1, 7)
XC = ((2, 0), (2, 1), (1, 0), (3, 0), (1, 1), (3, 1), (0, 1))
RING4 = (2, 1, 3)
PLANE = tuple(
    sorted(
        ((dx, dz) for dx in range(NX) for dz in range(NZ) if dx or dz),
        key=lambda o: -(min(o[0], NX - o[0]) + min(o[1], NZ - o[1])),
    )
)
NP = len(PLANE)
NT = (((1,), (1,)), ((), ()))
NN = (((1,), (0,)), ((), ()))


def mm(a, b, dims=NN):
    return lax.dot_general(a, b, dims, preferred_element_type=F32)


def split3(row, count=16):
    hi = row.astype(BF16).astype(F32)
    rest = row - hi
    mid = rest.astype(BF16).astype(F32)
    lo = rest - mid
    width = row.shape[1]
    at = lax.broadcasted_iota(jnp.int32, (count, width), 0)
    full = lambda r: jnp.broadcast_to(r, (count, width))
    out = jnp.where(at == 0, full(hi), jnp.where(at == 1, full(mid), jnp.where(at == 2, full(lo), 0.0)))
    return out.astype(BF16)


def unit_scale(rows):
    return lax.rsqrt(jnp.mean(rows * rows, axis=-1, keepdims=True) + EPS)


def unit_back(rows, grad):
    scale = unit_scale(rows)
    along = jnp.mean(rows * grad, axis=-1, keepdims=True)
    return (grad - rows * (along * scale * scale)) * (scale / math.sqrt(FEAT))


def kernel(
    tok_ref, off_ref, spec_ref, proto_ref,
    view_ref, pgrad_ref, loss_ref,
    tok, mask, kraw, kunit, keys, keys_t, pooled, qg, q16, s_buf, e_buf, k_buf, kt_buf, t_buf, two,
    a_src, a_c, a_pl, b_src, b_y, r_two, r_pl, cnt_src, cnt_y,
    kg_src, kg_half, kg_fwd, kg_y, c_src, c_rcv, x_src, x_rcv, w_src, w_rcv, fin, l_y,
    x_own, x_c, x_pl, p_row, ab_rows, qt,
    load_sem, g_ssem, g_rsem, gs_ssem, gs_rsem,
    a_ssem, a_rsem, b_ssem, b_rsem, r_ssem, r_rsem, cnt_ssem, cnt_rsem,
    kg_ssem, kg_rsem, f_ssem, f_rsem, fin_ssem, fin_rsem, l_ssem, l_rsem,
):
    dp = lax.axis_index("dp")
    pr = lax.axis_index("proto")
    y, zl, c = lax.div(dp, 8), lax.rem(lax.div(dp, 2), 4), lax.rem(dp, 2)
    zh, x = lax.div(pr, 4), lax.rem(pr, 4)
    z = zh * NZL + zl

    def dev(y=y, z=z, c=c, x=x):
        return ((y * NZL + lax.rem(z, NZL)) * NC + c, lax.div(z, NZL) * NX + x)

    xc_ids = [dev(x=lax.rem(x + dx, NX), c=lax.rem(c + dc, NC)) for dx, dc in XC]
    z_of = [lax.rem(z + j, NZ) for j in RING8]
    z_ids = [dev(z=k) for k in z_of]
    y_of = [lax.rem(y + j, NY) for j in RING8]
    y_ids = [dev(y=k) for k in y_of]
    x_of = [lax.rem(x + j, NX) for j in RING4]
    x_ids = [dev(x=k) for k in x_of]
    sib = dev(c=1 - c)
    plane_ids = [dev(x=lax.rem(x + dx, NX), z=lax.rem(z + dz, NZ)) for dx, dz in PLANE]
    step2 = 2 + 4 * c
    near = [lax.rem(z + step, NZ) for step in (step2, 1, 7)]
    near_ids = [dev(z=k) for k in near]
    here = z * NX + x
    cross_ids = [xc_ids[i] for i in range(7) if XC[i][0] and XC[i][1]]

    def remote(src, dst, ssem, rsem, to):
        return pltpu.make_async_remote_copy(
            src_ref=src, dst_ref=dst, send_sem=ssem, recv_sem=rsem, device_id=to, device_id_type=MESH
        )

    def got(ref, sem):
        remote(ref, ref, sem, sem, sib).wait_recv()

    def sent(ref, sem):
        remote(ref, ref, sem, sem, sib).wait_send()

    barrier = pltpu.get_barrier_semaphore()
    load_tok = pltpu.make_async_copy(tok_ref, tok, load_sem.at[0])
    load_key = pltpu.make_async_copy(proto_ref, kraw, load_sem.at[1])
    load_tok.start()
    load_key.start()
    for to in plane_ids + y_ids + cross_ids + [sib]:
        pl.semaphore_signal(barrier, inc=1, device_id=to, device_id_type=MESH)

    off = off_ref[...].astype(F32)
    off_row = jnp.concatenate([off[0:1], off[1:2]], axis=1)
    lane = lax.broadcasted_iota(jnp.int32, (128, 128), 1)
    first = jnp.broadcast_to(off_row, (128, 128)).T.astype(jnp.int32)
    row = lax.broadcasted_iota(jnp.int32, (128, 128), 0)
    first = first + (row & 63) * SEQ
    for part in range(16):
        col = part * 128
        inside = (lane + col >= first) & (lane + col < first + CROP)
        mask[:, pl.ds(col, 128)] = jnp.where(inside, 1.0, 0.0).astype(BF16)
    load_tok.wait()
    total = mm(mask[...], tok[...])
    rows = total / CROP
    pooled[...] = rows
    query = (rows * unit_scale(rows) / math.sqrt(FEAT)).astype(BF16)
    qg[c, zl, pl.ds(0, 128)] = query.astype(F32)
    spec = spec_ref[...].astype(F32)
    both = jnp.concatenate([spec, spec], axis=1)
    half = lax.broadcasted_iota(jnp.int32, (8, 128), 1) // 64
    qg[c, zl, pl.ds(128, 8)] = jnp.where(half == c, jnp.broadcast_to(both, (8, 128)), 0.0)

    load_key.wait()

    def whole(i, sums):
        at = pl.ds(pl.multiple_of(i * 4096, 4096), 4096)
        raw = kraw[at].astype(F32)
        unit = (raw * (unit_scale(raw) * (1.0 / math.sqrt(FEAT)))).astype(BF16)
        kunit[at] = unit
        e = jnp.exp(mm(unit, query, NT) * 10.0)
        k = (e * e).astype(BF16).astype(F32)
        fold = lambda a: jnp.sum(a.reshape(512, 8, 128), axis=0)
        return sums[0] + fold(k), sums[1] + fold(e)

    zero = jnp.zeros((8, 128), F32)
    ks, es = lax.fori_loop(0, 2, whole, (zero, zero))
    r_two[c, :, pl.ds(0, 128)] = jnp.sum(ks, axis=0, keepdims=True)
    r_two[c, :, pl.ds(128, 128)] = jnp.sum(es, axis=0, keepdims=True)

    pl.semaphore_wait(barrier, 11 + NP)
    remote(r_two.at[c], r_two.at[c], r_ssem.at[0], r_rsem.at[0], sib).start()

    mine = qg.at[c, zl]
    for i, to in enumerate(near_ids):
        remote(mine, mine, g_ssem, g_rsem.at[i], to).start()
    remote(mine, mine, gs_ssem, gs_rsem.at[0], sib).start()

    got(r_two.at[1 - c], r_rsem.at[0])
    r_pl[here] = r_two[...]
    for to in plane_ids:
        remote(r_pl.at[here], r_pl.at[here], r_ssem.at[1], r_rsem.at[1], to).start()

    for i in range(8):
        block = kunit[pl.ds(pl.multiple_of((i * 8 + zl * NC + c) * 128, 128), 128)]
        keys[pl.ds(i * 128, 128)] = block

    def scores(zp):
        zp128 = pl.multiple_of(zp * 128, 128)
        pair = []
        for v in range(2):
            q = jnp.concatenate([qg[0, zp, pl.ds(v * 64, 64)], qg[1, zp, pl.ds(v * 64, 64)]], axis=0).astype(BF16)
            q16[v, pl.ds(zp128, 128)] = q
            pair.append(q)
        rhs = jnp.concatenate(pair, axis=0)

        out = mm(keys[...], rhs, NT)
        e = jnp.exp(out * 10.0)
        k = (e * e).astype(BF16)
        for v in range(2):
            at = (v, slice(None), pl.ds(zp128, 128))
            s_buf[at] = out[:, v * 128 : v * 128 + 128]
            e_buf[at] = e[:, v * 128 : v * 128 + 128]
            k_buf[at] = k[:, v * 128 : v * 128 + 128]

    got(qg.at[1 - c, zl], gs_rsem.at[0])
    scores(zl)

    steps = ((1, 3), (2, 1), (0, 2))
    for i, step in steps:
        piece = qg.at[c, lax.rem(zl + step, NZL)]
        got(piece, g_rsem.at[i])
        remote(piece, piece, gs_ssem, gs_rsem.at[i + 1], sib).start()
    for i, step in steps:
        zp = lax.rem(zl + step, NZL)
        got(qg.at[1 - c, zp], gs_rsem.at[i + 1])
        scores(zp)

    got(r_pl.at[pl.ds(0, NP)], r_rsem.at[1])
    pairs = []
    for j in range(NZL):
        part = None
        for i in range(NZ * NX):
            if (i // NX) % NZL == j:
                part = r_pl[i] if part is None else part + r_pl[i]
        pairs.append(part)

    def assemble(base):
        tiles = []
        for v in range(2):
            at = base + v * 64
            for j in range(NZL):
                tiles += [pairs[j][0][:, at : at + 64], pairs[j][1][:, at : at + 64]]
        return jnp.concatenate(tiles, axis=1)

    window_scale = PROTOS / assemble(0)
    totals = assemble(128)

    spec_row = jnp.concatenate([qg[0, i, pl.ds(128, 1)] + qg[1, i, pl.ds(128, 1)] for i in range(4)], axis=1)
    group = lax.broadcasted_iota(jnp.int32, (NGROUP, 512), 0)
    onehot = jnp.where(group == jnp.broadcast_to(spec_row, (NGROUP, 512)).astype(jnp.int32), 1.0, 0.0)

    def plane_sum(own, slots, ssem, rsem, between):
        slots[here] = own
        for to in plane_ids:
            remote(slots.at[here], slots.at[here], ssem, rsem, to).start()
        between()

        def result():
            got(slots.at[pl.ds(0, NP)], rsem)
            part = slots[0]
            for i in range(1, NP + 1):
                part = part + slots[i]
            return part

        return result

    def nothing():
        pass

    def a_sum(it, between_1=nothing, between_2=nothing):
        remote(a_src.at[it], a_c.at[it], a_ssem.at[it, 0], a_rsem.at[it, 0], sib).start()
        between_1()
        got(a_c.at[it], a_rsem.at[it, 0])
        part = a_src[it] + a_c[it]
        return plane_sum(part, a_pl.at[it], a_ssem.at[it, 1], a_rsem.at[it, 1], between_2)()

    def b_sum(it, between=None):
        for i, to in enumerate(y_ids):
            remote(b_src.at[it], b_y.at[it, i], b_ssem.at[it], b_rsem.at[it], to).start()
        if between is not None:
            between()
        got(b_y.at[it], b_rsem.at[it])
        part = b_src[it]
        for i in range(7):
            part = part + b_y[it, i]
        return part

    def send_counts():
        cnt_src[...] = jnp.broadcast_to(jnp.sum(onehot, axis=1, keepdims=True), (NGROUP, 128))
        for i, to in enumerate(y_ids):
            remote(cnt_src, cnt_y.at[i], cnt_ssem, cnt_rsem, to).start()

    def halves(value, k0, width):
        hi = value.astype(BF16)
        two[pl.ds(k0, width)] = hi
        two[pl.ds(1024 + k0, width)] = (value - hi.astype(F32)).astype(BF16)

    def split_e(v):
        def block(kb, carry):
            k0 = pl.multiple_of(kb * 32, 32)
            halves(e_buf[v, pl.ds(k0, 32)], k0, 32)
            return carry

        lax.fori_loop(0, 32, block, 0)

    def split_t(v):
        for i in range(8):
            p = p_row[:, pl.ds(pl.multiple_of(v * 1024 + i * 128, 128), 128)]
            col = jnp.broadcast_to(p, (128, 128)).T
            t = k_buf[v, pl.ds(i * 128, 128)].astype(F32) * jnp.concatenate([col] * 4, axis=1)
            t_buf[v, pl.ds(i * 128, 128)] = t
            halves(t, i * 128, 128)

    def q_theirs(step):
        theirs = 1 - c if step == 0 else c
        (split_e, split_t)[step](theirs)
        c_src[step] = mm(keys_t[...], two[...])
        remote(c_src.at[step], c_rcv.at[step], f_ssem.at[step, 0], f_rsem.at[step, 0], sib).start()

    def q_own(step):
        (split_e, split_t)[step](c if step == 0 else 1 - c)
        x_src[step] = mm(keys_t[...], two[...])

    def q_x(step):
        got(c_rcv.at[step], f_rsem.at[step, 0])
        x_src[step] = x_src[step] + c_rcv[step]
        for h in range(2):
            for i, xx in enumerate(x_of):
                piece = x_src.at[step, pl.ds(pl.multiple_of(xx * 32 + h * 16, 16), 16)]
                remote(piece, x_rcv.at[step, h, i], f_ssem.at[step, 1 + h], f_rsem.at[step, 1 + h], x_ids[i]).start()

    def q_z(step, h):
        got(x_rcv.at[step, h], f_rsem.at[step, 1 + h])
        part = x_src[step, pl.ds(pl.multiple_of(x * 32 + h * 16, 16), 16)]
        for i in range(3):
            part = part + x_rcv[step, h, i]
        for i in range(4):
            w_src[step, h, i] = part[:, i * 128 : i * 128 + 128]
        for i, to in enumerate(z_ids):
            piece = w_src.at[step, h, lax.rem(z_of[i], NZL)]
            remote(piece, w_rcv.at[step, h, i], f_ssem.at[step, 3 + h], f_rsem.at[step, 3 + h], to).start()

    def q_end(step, h):
        got(w_rcv.at[step, h], f_rsem.at[step, 3 + h])
        part = w_src[step, h, zl]
        for i in range(7):
            part = part + w_rcv[step, h, i]
        return part

    def columns(it, scale):
        for v in range(2):
            parts = split3(scale[:, v * 512 : v * 512 + 512])
            out = mm(parts, k_buf[v], NT) if it == 0 else mm(parts, kt_buf[v])
            b_src[it, :, pl.ds(v * 1024, 1024)] = jnp.sum(out, axis=0, keepdims=True)

    def row_sums(it, scale):
        for v in range(2):
            out = mm(split3(scale[:, v * 1024 : v * 1024 + 1024]), k_buf[v])
            a_src[it, :, pl.ds(v * 512, 512)] = jnp.sum(out, axis=0, keepdims=True)

    def both_z():
        q_z(0, 0)
        q_z(0, 1)

    def beside_a0():
        send_counts()
        for i in range(8):
            turned = keys[pl.ds(i * 128, 128)].astype(F32).T.astype(BF16)
            keys_t[:, pl.ds(i * 128, 128)] = turned
            keys_t[:, pl.ds(1024 + i * 128, 128)] = turned
        q_theirs(0)
        q_own(0)

    def turn():
        for v in range(2):
            kt_buf[v] = k_buf[v].T

    columns(0, window_scale)
    proto_scale = 1.0 / (PROTOS * b_sum(0, turn))
    row_sums(0, proto_scale)
    window_scale = 1.0 / a_sum(0, nothing, beside_a0)
    columns(1, window_scale)
    proto_scale = 1.0 / (PROTOS * b_sum(1, lambda: q_x(0)))
    row_sums(1, proto_scale)
    window_scale = 1.0 / a_sum(1)
    columns(2, window_scale)
    proto_scale = 1.0 / (PROTOS * b_sum(2, both_z))
    row_sums(2, proto_scale)
    p_row[...] = proto_scale

    def cross():
        for v in range(2):

            def block(kb, acc):
                k0 = pl.multiple_of(kb * 32, 32)
                prod = t_buf[1 - v, pl.ds(k0, 32)] * s_buf[v, pl.ds(k0, 32)]
                return acc + jnp.sum(prod.reshape(4, 8, 512), axis=0)

            acc = lax.fori_loop(0, 32, block, jnp.zeros((8, 512), F32))
            x_own[:, pl.ds(v * 512, 512)] = jnp.sum(acc, axis=0, keepdims=True)

    def beside_a2():
        q_own(1)
        q_x(1)
        cross()
        remote(x_own, x_c, l_ssem.at[0], l_rsem.at[0], sib).start()
        got(x_c, l_rsem.at[0])
        cross_sum.append(plane_sum(x_own[...] + x_c[...], x_pl, l_ssem.at[1], l_rsem.at[1], nothing))
        got(cnt_y, cnt_rsem)
        counts = cnt_src[...]
        for i in range(7):
            counts = counts + cnt_y[i]
        seen = jnp.sum(onehot * jnp.concatenate([counts] * 4, axis=1), axis=0, keepdims=True)
        weight = WINDOWS / (NGROUP * seen)
        tot_v = [totals[:, 0:512], totals[:, 512:1024]]
        known.extend((weight, tot_v, [5.0 * weight / tot_v[v] for v in range(2)]))

    cross_sum, known = [], []
    last = 1.0 / a_sum(2, lambda: q_theirs(1), beside_a2)

    weight, tot_v, a_v = known
    last_v = [last[:, 0:512], last[:, 512:1024]]
    b_v = [5.0 * weight * last_v[1 - v] for v in range(2)]
    for v in range(2):
        ab_rows[0, v] = a_v[v]
        ab_rows[1, v] = b_v[v]

    def add_slots(ref):
        out = ref[0]
        for i in range(1, 8):
            out = out + ref[i]
        return out

    def key_part(slot, yy):
        k0 = pl.multiple_of(yy * 128, 128)
        part = jnp.zeros((128, FEAT), F32)
        for v in range(2):
            at = (pl.ds(k0, 128), slice(None))
            g = (e_buf[(v,) + at] * a_v[v] - t_buf[(1 - v,) + at] * b_v[v]).astype(BF16)
            part = part + mm(g, q16[v])
        kg_src[slot] = part

    ahead = lambda j: lax.rem(y + j, NY)
    up1, up2, down1, down2 = (dev(y=ahead(j)) for j in (1, 2, 7, 6))
    key_part(4, ahead(4))
    remote(kg_src.at[4, pl.ds(0, 64)], kg_half.at[0], kg_ssem.at[0], kg_rsem.at[0], up2).start()
    remote(kg_src.at[4, pl.ds(64, 64)], kg_half.at[1], kg_ssem.at[1], kg_rsem.at[1], down2).start()
    key_part(3, ahead(3))
    remote(kg_src.at[3], kg_fwd.at[0], kg_ssem.at[2], kg_rsem.at[2], up1).start()
    key_part(5, ahead(5))
    remote(kg_src.at[5], kg_fwd.at[1], kg_ssem.at[3], kg_rsem.at[3], down1).start()
    key_part(1, ahead(1))
    remote(kg_src.at[1], kg_y.at[0], kg_ssem.at[4], kg_rsem.at[4], up1).start()
    key_part(7, ahead(7))
    remote(kg_src.at[7], kg_y.at[1], kg_ssem.at[5], kg_rsem.at[5], down1).start()
    q_z(1, 0)
    key_part(2, ahead(2))
    key_part(6, ahead(6))
    key_part(0, y)
    q_z(1, 1)

    shared = cross_sum[0]()
    terms = jnp.zeros((1, 512), F32)
    for v in range(2):
        x_row = shared[:, v * 512 : v * 512 + 512]
        terms = terms + 0.5 * weight * (jnp.log(tot_v[v]) - 10.0 * last_v[1 - v] * x_row)
    l_y[y] = terms[:, 0:128] + terms[:, 128:256] + terms[:, 256:384] + terms[:, 384:512]
    for to in y_ids:
        remote(l_y.at[y], l_y.at[y], l_ssem.at[2], l_rsem.at[2], to).start()

    got(kg_fwd.at[0], kg_rsem.at[2])
    got(kg_half.at[0], kg_rsem.at[0])
    kg_src[2, pl.ds(0, 64)] = kg_src[2, pl.ds(0, 64)] + kg_fwd[0, pl.ds(0, 64)] + kg_half[0]
    kg_src[2, pl.ds(64, 64)] = kg_src[2, pl.ds(64, 64)] + kg_fwd[0, pl.ds(64, 64)]
    remote(kg_src.at[2], kg_y.at[2], kg_ssem.at[6], kg_rsem.at[6], up2).start()
    got(kg_fwd.at[1], kg_rsem.at[3])
    got(kg_half.at[1], kg_rsem.at[1])
    kg_src[6, pl.ds(0, 64)] = kg_src[6, pl.ds(0, 64)] + kg_fwd[1, pl.ds(0, 64)]
    kg_src[6, pl.ds(64, 64)] = kg_src[6, pl.ds(64, 64)] + kg_fwd[1, pl.ds(64, 64)] + kg_half[1]
    remote(kg_src.at[6], kg_y.at[3], kg_ssem.at[7], kg_rsem.at[7], down2).start()

    at = pl.ds(pl.multiple_of(zl * 128, 128), 128)
    for h in range(2):
        part = ab_rows[0, c, :, at] * q_end(0, h) - ab_rows[1, c, :, at] * q_end(1, h)
        feats = pl.ds(pl.multiple_of(x * 32 + h * 16, 16), 16)
        mine = fin.at[c, feats]
        fin[c, feats] = part
        for to in xc_ids:
            remote(mine, mine, fin_ssem.at[h], fin_rsem.at[h], to).start()

    part = kg_src[0]
    for i, k in ((0, 4), (1, 5), (2, 6), (3, 7)):
        got(kg_y.at[i], kg_rsem.at[k])
        part = part + kg_y[i]
    own = pl.multiple_of((y * 8 + zl * NC + c) * 128, 128)
    pgrad_ref[...] = unit_back(kraw[pl.ds(own, 128)].astype(F32), part)

    for h in range(2):
        got(w_rcv.at[0, h], fin_rsem.at[h])
    for v in range(2):
        qt[v] = fin[v].T
    for v in range(2):
        grad = qt[v, pl.ds(pl.multiple_of(c * 64, 64), 64)]
        view_ref[v] = unit_back(pooled[pl.ds(v * 64, 64)], grad)

    got(l_y.at[pl.ds(0, 7)], l_rsem.at[2])
    loss_ref[...] = jnp.sum(add_slots(l_y), axis=1, keepdims=True) * (1.0 / WINDOWS)

    sent(qg.at[0, pl.ds(0, 3)], g_ssem)
    sent(qg.at[0], gs_ssem)
    for it in range(3):
        sent(a_c.at[it], a_ssem.at[it, 0])
        sent(a_pl.at[it, pl.ds(0, NP)], a_ssem.at[it, 1])
    for it in range(3):
        sent(b_y.at[it], b_ssem.at[it])
    sent(r_two.at[0], r_ssem.at[0])
    sent(r_pl.at[pl.ds(0, NP)], r_ssem.at[1])
    sent(cnt_y, cnt_ssem)
    for i in range(2):
        sent(kg_half.at[i], kg_ssem.at[i])
        sent(kg_fwd.at[i], kg_ssem.at[2 + i])
        sent(kg_y.at[i], kg_ssem.at[4 + i])
        sent(kg_y.at[2 + i], kg_ssem.at[6 + i])
        sent(c_rcv.at[i], f_ssem.at[i, 0])
        for h in range(2):
            sent(x_rcv.at[i, h], f_ssem.at[i, 1 + h])
            sent(w_rcv.at[i, h], f_ssem.at[i, 3 + h])
        sent(w_rcv.at[0, i], fin_ssem.at[i])
    sent(x_c, l_ssem.at[0])
    sent(x_pl.at[pl.ds(0, NP)], l_ssem.at[1])
    sent(l_y.at[pl.ds(0, 7)], l_ssem.at[2])


def hand_on(view_in, pgrad_in, loss_in, view_ref, pgrad_ref, loss_ref):
    view_ref[...] = view_in[...]
    pgrad_ref[...] = pgrad_in[...]
    loss_ref[...] = loss_in[...]


def on_device(tokens, offsets, species, prototypes):
    vmem = pltpu.VMEM
    dma = pltpu.SemaphoreType.DMA
    anywhere = pl.BlockSpec(memory_space=pl.ANY)
    inside = pl.BlockSpec(memory_space=pltpu.VMEM)
    scratch = [
        vmem((64 * SEQ, FEAT), BF16),
        vmem((128, 64 * SEQ), BF16),
        vmem((8192, FEAT), BF16),
        vmem((8192, FEAT), BF16),
        vmem((1024, FEAT), BF16),
        vmem((FEAT, 2048), BF16),
        vmem((128, FEAT), F32),
        vmem((2, 4, 136, FEAT), F32),
        vmem((2, 512, FEAT), BF16),
        vmem((2, 1024, 512), F32),
        vmem((2, 1024, 512), F32),
        vmem((2, 1024, 512), BF16),
        vmem((2, 512, 1024), BF16),
        vmem((2, 1024, 512), F32),
        vmem((2048, 512), BF16),
        vmem((3, 1, 1024), F32),
        vmem((3, 1, 1024), F32),
        vmem((3, NP + 1, 1, 1024), F32),
        vmem((3, 1, 2048), F32),
        vmem((3, 7, 1, 2048), F32),
        vmem((2, 1, 256), F32),
        vmem((NP + 1, 2, 1, 256), F32),
        vmem((NGROUP, 128), F32),
        vmem((7, NGROUP, 128), F32),
        vmem((8, 128, FEAT), F32),
        vmem((2, 64, FEAT), F32),
        vmem((2, 128, FEAT), F32),
        vmem((4, 128, FEAT), F32),
        vmem((2, FEAT, 512), F32),
        vmem((2, FEAT, 512), F32),
        vmem((2, FEAT, 512), F32),
        vmem((2, 2, 3, 16, 512), F32),
        vmem((2, 2, 4, 16, 128), F32),
        vmem((2, 2, 7, 16, 128), F32),
        vmem((2, FEAT, 128), F32),
        vmem((8, 1, 128), F32),
        vmem((1, 1024), F32),
        vmem((1, 1024), F32),
        vmem((NP + 1, 1, 1024), F32),
        vmem((1, 2048), F32),
        vmem((2, 2, 1, 512), F32),
        vmem((2, 128, FEAT), F32),
        dma((2,)),
        dma, dma((3,)), dma, dma((4,)),
        dma((3, 2)), dma((3, 2)), dma((3,)), dma((3,)), dma((2,)), dma((2,)), dma, dma,
        dma((8,)), dma((8,)), dma((2, 5)), dma((2, 5)), dma((2,)), dma((2,)), dma((3,)), dma((3,)),
    ]
    view_grads, proto_grads, loss = pl.pallas_call(
        kernel,
        out_shape=(vmem((2, 64, FEAT), F32), vmem((128, FEAT), F32), vmem((1, 1), F32)),
        in_specs=[anywhere, inside, inside, anywhere],
        out_specs=(inside, inside, inside),
        scratch_shapes=scratch,
        compiler_params=pltpu.CompilerParams(
            collective_id=0, has_side_effects=True, vmem_limit_bytes=60 * 2**20
        ),
        name="swav_step",
    )(
        tokens.reshape(64 * SEQ, FEAT),
        offsets,
        species.reshape(1, 64),
        prototypes,
    )
    view_grads, proto_grads, loss = pl.pallas_call(
        hand_on,
        out_shape=(
            jax.ShapeDtypeStruct((2, 64, FEAT), F32),
            jax.ShapeDtypeStruct((128, FEAT), F32),
            jax.ShapeDtypeStruct((1, 1), F32),
        ),
        in_specs=[inside] * 3,
        out_specs=(inside, inside, inside),
        compiler_params=pltpu.CompilerParams(vmem_limit_bytes=16 * 2**20),
        name="results",
    )(*(pltpu.with_memory_space_constraint(a, pltpu.VMEM) for a in (view_grads, proto_grads, loss)))
    return view_grads, proto_grads, loss.reshape(())


def solution(mesh):
    return jax.shard_map(
        on_device,
        mesh=mesh,
        in_specs=(P("dp", None, None), P(None, "dp"), P("dp"), P("proto", None)),
        out_specs=(P(None, "dp", None), P(("proto", "dp"), None), P()),
        check_vma=False,
    )
```
